32 devices in a mesh: wide: 4 (over y, core), narrow: 8 (over z, x).
Axes of the slice: x: 2, y: 2, z: 4, core: 2. Of those that a mesh axis runs over, the one named last changes fastest.
Arguments:
- variables: bfloat16 [8, 2048, 768], P(None, 'wide'), may hold values from -6 to 6
- valid_slots: int32 [8, 48], replicated, may hold values from 0 to 1, as said below
- out_grad: bfloat16 [8, 2048, 1024], P(None, 'wide'), may hold values from -6 to 6
- patch_embed: bfloat16 [768, 1024], replicated, may hold values from -1.5 to 1.5
- variable_embed: bfloat16 [48, 1024], replicated, may hold values from -6 to 6
- pool_query: float32 [1024], P('narrow'), may hold values from -6 to 6
- pool_key: bfloat16 [1024, 1024], P(None, 'narrow'), may hold values from -0.1875 to 0.1875
- pool_value: bfloat16 [1024, 1024], P(None, 'narrow'), may hold values from -0.1875 to 0.1875
- value_shift: float32 [1024], P('narrow'), may hold values from -1.5 to 1.5
- pool_output: bfloat16 [1024, 1024], P('narrow'), may hold values from -0.1875 to 0.1875
- pool_bias: float32 [1024], replicated, may hold values from -1.5 to 1.5
- first_gain: float32 [1024], replicated, may hold values from 0.3 to 2
- first_shift: float32 [1024], replicated, may hold values from -2 to 2
- self_weights: bfloat16 [1024, 3, 1024], P(None, None, 'narrow'), may hold values from -0.1875 to 0.1875
- query_bias: float32 [1024], P('narrow'), may hold values from -3 to 3
- value_bias: float32 [1024], P('narrow'), may hold values from -0.3 to 0.3
- self_output: bfloat16 [1024, 1024], P('narrow'), may hold values from -0.1875 to 0.1875
- output_bias: float32 [1024], replicated, may hold values from -1.5 to 1.5
- second_gain: float32 [1024], replicated, may hold values from 0.3 to 2
- second_shift: float32 [1024], replicated, may hold values from -2 to 2
- feed_up: bfloat16 [1024, 4096], P(None, 'narrow'), may hold values from -0.1875 to 0.1875
- up_bias: float32 [4096], P('narrow'), may hold values from -3 to 3
- feed_down: bfloat16 [4096, 1024], P('narrow'), may hold values from -0.09375 to 0.09375
- down_bias: float32 [1024], replicated, may hold values from -3 to 3
Outputs:
- block_out: bfloat16 [8, 2048, 1024], P(None, 'wide')
- grad_variables: float32 [8, 2048, 768], P(None, 'wide')
- grad_patch_embed: float32 [768, 1024], replicated
- grad_variable_embed: float32 [48, 1024], replicated
- grad_pool_query: float32 [1024], P('narrow')
- grad_pool_key: float32 [1024, 1024], P(None, 'narrow')
- grad_pool_value: float32 [1024, 1024], P(None, 'narrow')
- grad_value_shift: float32 [1024], P('narrow')
- grad_pool_output: float32 [1024, 1024], P('narrow')
- grad_pool_bias: float32 [1024], replicated
- grad_first_gain: float32 [1024], replicated
- grad_first_shift: float32 [1024], replicated
- grad_self_weights: float32 [1024, 3, 1024], P(None, None, 'narrow')
- grad_query_bias: float32 [1024], P('narrow')
- grad_value_bias: float32 [1024], P('narrow')
- grad_self_output: float32 [1024, 1024], P('narrow')
- grad_output_bias: float32 [1024], replicated
- grad_second_gain: float32 [1024], replicated
- grad_second_shift: float32 [1024], replicated
- grad_feed_up: float32 [1024, 4096], P(None, 'narrow')
- grad_up_bias: float32 [4096], P('narrow')
- grad_feed_down: float32 [4096, 1024], P('narrow')
- grad_down_bias: float32 [1024], replicated
The draws below stay inside these ranges and needn't reach their ends.
Inputs may be any that keep to these rules, and one draw needn't show every extreme that they name: `valid_slots`: every row holds exactly 30 ones.
All inputs are finite; a program needn't handle non-finite values.
Results may differ from the reference program's by a relative error of at most 0.025.
Values may be sent and summed in bfloat16 or wider, within the bound.
No kernel may reach another device: no remote copies, remote signals or barrier semaphores. Data moves between devices by JAX's collectives and lax.ppermute only.
A program may use at most 576 MiB of HBM per device.

```python
import math
import jax
import jax.numpy as jnp
from jax import lax

D = 1024
HEADS = 16
HEAD_DIM = 64
FF = 4096
VARS = 48
PIX = 16
VALID = 30
SEQ_LEN = 2048
SAMPLES = 8


def draw_valid_slots(key, part):
    key = jax.random.fold_in(key, 7)
    sample_keys = jax.random.split(key, SAMPLES)
    orders = jax.vmap(lambda sample_key: jax.random.permutation(sample_key, VARS))(sample_keys)
    return (orders < VALID).astype(jnp.int32)


def levels(rng, dims, shards, low, high):
    gain, own = 1.0, jax.random.fold_in(rng, 6)
    for position, blocks in shards:
        steps = jnp.exp(jax.random.uniform(jax.random.fold_in(own, position), (blocks,), jnp.float32, low / len(shards), high / len(shards)))
        gain = gain * jnp.repeat(steps, dims[position] // blocks).reshape([-1 if axis == position else 1 for axis in range(len(dims))])
    return gain


def centred(own_key, dims, spread, most, pieces=(), kind=jnp.bfloat16):
    drawn = spread * jax.random.normal(own_key, dims, jnp.float32)
    if pieces:
        drawn = drawn * levels(own_key, dims, pieces, -0.22, 0.18)
    return jnp.clip(drawn, -most, most).astype(kind)


def setup_inputs(seed: int = 0) -> dict:
    key_list = jax.random.split(jax.random.key(seed), 25)
    variables = centred(key_list[0], (SAMPLES, SEQ_LEN, VARS * PIX), 1.0, 6.0, ((1, 4),))
    valid_slots = draw_valid_slots(jax.random.fold_in(key_list[24], 71), 0)
    out_grad = centred(key_list[2], (SAMPLES, SEQ_LEN, D), 1.0, 6.0, ((1, 4),))
    patch_embed = centred(key_list[3], (VARS * PIX, D), PIX ** -0.5, 1.5)
    variable_embed = centred(key_list[4], (VARS, D), 1.0, 6.0)
    pool_query = centred(key_list[5], (D,), 1.0, 6.0, ((0, 8),), jnp.float32)
    pool_key = centred(key_list[6], (D, D), D ** -0.5, 0.1875, ((1, 8),))
    pool_value = centred(key_list[7], (D, D), D ** -0.5, 0.1875, ((1, 8),))
    value_shift = centred(key_list[8], (D,), 0.25, 1.5, ((0, 8),), jnp.float32)
    pool_output = centred(key_list[9], (D, D), D ** -0.5, 0.1875, ((0, 8),))
    pool_bias = centred(key_list[10], (D,), 0.25, 1.5, (), jnp.float32)
    first_gain = jnp.clip(jnp.exp(jax.random.uniform(key_list[11], (D,), jnp.float32, math.log(0.3), math.log(2.0))), 0.3, 2.0)
    first_shift = centred(key_list[12], (D,), 0.3, 2.0, (), jnp.float32)
    self_weights = centred(key_list[13], (D, 3, D), D ** -0.5, 0.1875, ((2, 8),))
    query_bias = centred(key_list[14], (D,), 0.5, 3.0, ((0, 8),), jnp.float32)
    value_bias = centred(key_list[15], (D,), 0.05, 0.3, ((0, 8),), jnp.float32)
    self_output = centred(key_list[16], (D, D), D ** -0.5, 0.1875, ((0, 8),))
    output_bias = centred(key_list[17], (D,), 0.25, 1.5, (), jnp.float32)
    second_gain = jnp.clip(jnp.exp(jax.random.uniform(key_list[18], (D,), jnp.float32, math.log(0.3), math.log(2.0))), 0.3, 2.0)
    second_shift = centred(key_list[19], (D,), 0.3, 2.0, (), jnp.float32)
    feed_up = centred(key_list[20], (D, FF), D ** -0.5, 0.1875, ((1, 8),))
    up_bias = centred(key_list[21], (FF,), 0.5, 3.0, ((0, 8),), jnp.float32)
    feed_down = centred(key_list[22], (FF, D), FF ** -0.5, 0.09375, ((0, 8),))
    down_bias = centred(key_list[23], (D,), 0.5, 3.0, (), jnp.float32)
    return dict(variables=variables, valid_slots=valid_slots, out_grad=out_grad, patch_embed=patch_embed, variable_embed=variable_embed, pool_query=pool_query, pool_key=pool_key, pool_value=pool_value, value_shift=value_shift, pool_output=pool_output, pool_bias=pool_bias, first_gain=first_gain, first_shift=first_shift, self_weights=self_weights, query_bias=query_bias, value_bias=value_bias, self_output=self_output, output_bias=output_bias, second_gain=second_gain, second_shift=second_shift, feed_up=feed_up, up_bias=up_bias, feed_down=feed_down, down_bias=down_bias)


@jax.custom_vjp
def low(v):
    return lax.optimization_barrier(v.astype(jnp.bfloat16)).astype(jnp.float32)

@jax.custom_vjp
def low_back(v):
    return v

def low_keep(v):
    return (low(v), None)

def low_pass(kept, grad):
    return (grad,)

def back_keep(v):
    return (v, None)

def back_low(kept, grad):
    return (low(grad),)
low.defvjp(low_keep, low_pass)
low_back.defvjp(back_keep, back_low)

def layer_norm(stream, norm_gain, norm_shift):
    centered = stream - lax.optimization_barrier(jnp.mean(stream, -1, keepdims=True))
    variance = lax.optimization_barrier(jnp.mean(centered * centered, -1, keepdims=True))
    return centered * lax.rsqrt(variance + 1e-05) * norm_gain + norm_shift

def sample_forward(sample, slot_valid, patch_embed, variable_embed, pool_query, pool_key, pool_value, value_shift, pool_output, pool_bias, first_gain, first_shift, self_weights, query_bias, value_bias, self_output, output_bias, second_gain, second_shift, feed_up, up_bias, feed_down, down_bias):
    highest = lax.Precision.HIGHEST
    score_scale = HEAD_DIM ** (-0.5)
    length = sample.shape[0]
    embed_table = jnp.concatenate([patch_embed, variable_embed], 0)
    folded = jnp.einsum('dhe,he->hd', pool_key.reshape(D, HEADS, HEAD_DIM), pool_query.reshape(HEADS, HEAD_DIM), precision=highest)
    slot_proj = jnp.einsum('rd,hd->rh', embed_table, folded, precision=highest) * score_scale
    patch_terms = slot_proj[:VARS * PIX].reshape(VARS, PIX, HEADS)
    slot_terms = slot_proj[VARS * PIX:]
    pixels = sample.reshape(length, VARS, PIX)
    scores = jnp.einsum('tvc,vch->thv', pixels, patch_terms, precision=highest) + slot_terms.T[None]
    scores = jnp.where(slot_valid[None, None, :] > 0, scores, -1e+30)
    weights = jnp.exp(scores - lax.optimization_barrier(jnp.max(scores, -1, keepdims=True)))
    weights = weights / lax.optimization_barrier(jnp.sum(weights, -1, keepdims=True))
    mixed = jnp.concatenate([(weights[..., None] * pixels[:, None]).reshape(length, HEADS, VARS * PIX), weights], -1)
    mixed = low(mixed)
    embedded = low(low_back(jnp.einsum('thr,rd->thd', mixed, embed_table, precision=highest)))
    pooled = jnp.einsum('thd,dhe->the', embedded, pool_value.reshape(D, HEADS, HEAD_DIM), precision=highest)
    pooled = pooled + value_shift.reshape(HEADS, HEAD_DIM)
    pooled = low(low_back(pooled.reshape(length, D)))
    stream_zero = low_back(jnp.dot(pooled, pool_output, precision=highest) + pool_bias)
    normed_one = low(layer_norm(stream_zero, first_gain, first_shift))
    triple = jnp.dot(normed_one, self_weights.reshape(D, 3 * D), precision=highest).reshape(length, 3, D)
    queries = low(low_back(triple[:, 0] + query_bias)).reshape(length, HEADS, HEAD_DIM)
    keys = low(low_back(triple[:, 1])).reshape(length, HEADS, HEAD_DIM)
    values = low(low_back(triple[:, 2] + value_bias)).reshape(length, HEADS, HEAD_DIM)
    logits = low_back(score_scale * jnp.einsum('qhe,khe->hqk', queries, keys, precision=highest))
    row_peak = lax.optimization_barrier(jnp.max(logits, -1, keepdims=True))
    log_total = row_peak + jnp.log(lax.optimization_barrier(jnp.sum(jnp.exp(logits - row_peak), -1, keepdims=True)))
    probs = low(jnp.exp(logits - log_total))
    attended = jnp.einsum('hqk,khe->qhe', probs, values, precision=highest).reshape(length, D)
    attended = low(low_back(attended))
    stream_one = stream_zero + low_back(jnp.dot(attended, self_output, precision=highest) + output_bias)
    normed_two = low(layer_norm(stream_one, second_gain, second_shift))
    hidden_pre = low_back(jnp.dot(normed_two, feed_up, precision=highest) + up_bias)
    active = low(jax.nn.gelu(hidden_pre, approximate=False))
    return stream_one + low_back(jnp.dot(active, feed_down, precision=highest) + down_bias)

def reference(variables, valid_slots, out_grad, patch_embed, variable_embed, pool_query, pool_key, pool_value, value_shift, pool_output, pool_bias, first_gain, first_shift, self_weights, query_bias, value_bias, self_output, output_bias, second_gain, second_shift, feed_up, up_bias, feed_down, down_bias):
    params = tuple((item.astype(jnp.float32) for item in (patch_embed, variable_embed, pool_query, pool_key, pool_value, value_shift, pool_output, pool_bias, first_gain, first_shift, self_weights, query_bias, value_bias, self_output, output_bias, second_gain, second_shift, feed_up, up_bias, feed_down, down_bias)))
    pixels_in = variables.astype(jnp.float32)

    def forward(pixels_all, *weights_all):

        def per_sample(sample_pair):
            return sample_forward(sample_pair[0], sample_pair[1], *weights_all)
        return lax.map(jax.checkpoint(per_sample), (pixels_all, valid_slots))
    result, pullback = jax.vjp(forward, pixels_in, *params)
    grads = pullback(out_grad.astype(jnp.float32))
    return (result.astype(jnp.bfloat16), grads[0], grads[1], grads[2], grads[3], grads[4], grads[5], grads[6], grads[7], grads[8], grads[9], grads[10], grads[11], grads[12], grads[13], grads[14], grads[15], grads[16], grads[17], grads[18], grads[19], grads[20], grads[21])
```

```python
import jax
import jax.numpy as jnp
from jax import lax
from jax.experimental import pallas as pl
from jax.experimental.pallas import tpu as pltpu
from jax.sharding import PartitionSpec as P

HEAD_DIM = 64
VARS = 48
PIX = 16
SCALE = HEAD_DIM ** (-0.5)
VMEM_BYTES = 56 * 1024 * 1024

highest = lax.Precision.HIGHEST
AXES = ("wide", "narrow")
F32 = jnp.float32
BF16 = jnp.bfloat16


def low(tensor):
    return tensor.astype(BF16)


def dot(left, right, dims=((1,), (0,)), precision=None):
    return lax.dot_general(
        left, right, (dims, ((), ())), precision=precision, preferred_element_type=F32
    )


NT = ((1,), (1,))
TN = ((0,), (0,))


def params(bytes_limit=VMEM_BYTES):
    return pltpu.CompilerParams(vmem_limit_bytes=bytes_limit)


def struct(shape, dtype):
    return jax.ShapeDtypeStruct(shape, dtype)


def tie(tensor, *others):
    return lax.optimization_barrier((tensor,) + others)[0]


def fixed(shape, *start):
    start = start or (0,) * len(shape)
    return pl.BlockSpec(shape, lambda *_: start)


def per_block(shape, offset=0, *rest):
    rest = rest or (0,) * len(shape)
    return pl.BlockSpec((1,) + shape, lambda n: (n + offset,) + rest)


def cost(flops, bytes_accessed):
    return pl.CostEstimate(flops=flops, bytes_accessed=bytes_accessed, transcendentals=0)


class Ring:
    def __init__(self, wide_size, narrow_size):
        self.wide, self.narrow = wide_size, narrow_size
        self.order = list(range(0, narrow_size, 2)) + list(range(1, narrow_size, 2))[::-1]
        place = {device: index for index, device in enumerate(self.order)}
        self.w = lax.axis_index("wide")
        self.n = lax.axis_index("narrow")
        self.core = self.w % 2
        self.pos = jnp.where(self.n % 2 == 0, self.n // 2, narrow_size - 1 - self.n // 2)

        def step(device, hops):
            return self.order[(place[device] + hops) % narrow_size]

        every = [(w, n) for w in range(wide_size) for n in range(narrow_size)]
        flat = lambda w, n: w * narrow_size + n
        bits = lambda size: [1 << i for i in range(size.bit_length() - 1)]
        self.forward = [(flat(w, n), flat(w, step(n, 1))) for w, n in every]
        self.backward = [(flat(w, n), flat(w, step(n, -1))) for w, n in every]
        self.by_core = [(flat(w, n), flat(w, step(n, 1 - 2 * (w % 2)))) for w, n in every]
        self.by_core_back = [(dst, src) for src, dst in self.by_core]
        self.wide_swap = {
            bit: [(flat(w, n), flat(w ^ bit, n)) for w, n in every] for bit in bits(wide_size)
        }
        self.narrow_swap = {
            bit: [(flat(w, n), flat(w, n ^ bit)) for w, n in every] for bit in bits(narrow_size)
        }

    def move(self, tensor, pairs):
        return lax.ppermute(tensor, AXES, pairs)

    def swap(self, tensor, bit=1):
        return self.move(tensor, self.wide_swap[bit])

    def at(self, hops):
        index = (self.pos + hops + self.narrow) % self.narrow
        return jnp.where(2 * index < self.narrow, 2 * index, 2 * (self.narrow - 1 - index) + 1)

    def first(self, hops):
        return self.at(jnp.where(self.core == 0, -hops, hops))

    def second(self, hops):
        return self.at(jnp.where(self.core == 0, hops, -hops))

    def add_everywhere(self, tensor):
        for pairs in list(self.wide_swap.values()) + list(self.narrow_swap.values()):
            tensor = tensor + self.move(tensor, pairs)
        return tensor

    def gather_wide(self, block):
        pieces = {0: block}
        for bit in self.wide_swap:
            for shift in list(pieces):
                pieces[shift | bit] = self.swap(pieces[shift], bit)
        return [pieces[shift] for shift in range(self.wide)]

    def finish_shared(self, partial):
        half = partial.shape[0] // 2
        mine = lax.dynamic_slice_in_dim(partial, self.core * half, half, 0)
        theirs = lax.dynamic_slice_in_dim(partial, (1 - self.core) * half, half, 0)
        total = mine.astype(F32) + self.swap(theirs).astype(F32)
        for bit in self.wide_swap:
            if bit > 1:
                total = total + self.swap(low(total), bit).astype(F32)
        total = low(total)
        other = self.swap(total)
        first = jnp.where(self.core == 0, total, other).astype(F32)
        second = jnp.where(self.core == 0, other, total).astype(F32)
        return first, second


def blank(shape, dtype):
    return pl.pallas_call(
        lambda o_ref: None,
        out_shape=struct(shape, dtype),
        out_specs=pl.BlockSpec(memory_space=pl.ANY),
        compiler_params=params(),
        name="blank",
    )()


def put(out, piece, index):
    return lax.dynamic_update_index_in_dim(out, piece, index, 0)


class GatherShared:
    def __init__(self, ring, block):
        self.ring, self.current, self.hops = ring, block, 0
        self.out = put(blank((ring.narrow,) + block.shape, block.dtype), block, ring.n)

    def step(self):
        ring, self.hops = self.ring, self.hops + 1
        self.current = ring.move(self.current, ring.by_core)
        self.out = put(self.out, self.current, ring.first(self.hops))
        if 2 * self.hops < ring.narrow:
            other = ring.swap(self.current)
            self.out = put(self.out, other, ring.second(self.hops))
        return self.current

    def finish(self):
        while 2 * self.hops < self.ring.narrow:
            self.step()
        return self.out


class GatherOwn:
    def __init__(self, ring, block, dtype):
        self.ring, self.hops, self.dtype = ring, 0, dtype
        self.ahead = self.behind = block
        self.out = blank((ring.narrow,) + block.shape, dtype)
        self.out = put(self.out, block.astype(dtype), ring.n)

    def step(self):
        ring, self.hops = self.ring, self.hops + 1
        self.ahead = ring.move(self.ahead, ring.forward)
        self.out = put(self.out, self.ahead.astype(self.dtype), ring.at(-self.hops))
        if 2 * self.hops < ring.narrow:
            self.behind = ring.move(self.behind, ring.backward)
            self.out = put(self.out, self.behind.astype(self.dtype), ring.at(self.hops))
        return self.ahead, self.behind

    def finish(self):
        while 2 * self.hops < self.ring.narrow:
            self.step()
        return self.out


class ScatterShared:
    def __init__(self, ring, blocks):
        self.ring, self.blocks, self.hops = ring, blocks, ring.narrow // 2
        self.current = self.pick(ring.first(self.hops))
        self.others = [self.ring.swap(self.pick(ring.second(h))) for h in range(1, self.hops)]

    def pick(self, index):
        return lax.dynamic_index_in_dim(self.blocks, index, 0, keepdims=False)

    def step(self):
        ring, self.hops = self.ring, self.hops - 1
        moved = ring.move(self.current, ring.by_core_back).astype(F32)
        if self.hops:
            own = self.pick(ring.first(self.hops)).astype(F32)
            self.current = low(moved + own + self.others[self.hops - 1].astype(F32))
        else:
            self.current = low(moved + self.pick(ring.n).astype(F32))
        return self.current

    def finish(self):
        while self.hops:
            self.step()
        return self.current


def split_three(tensor):
    top = low(tensor)
    rest = tensor - top.astype(F32)
    middle = low(rest)
    return top, middle, low(rest - middle.astype(F32))


def join(rows, start, count, step):
    picked = [rows[start + i * step : start + i * step + count].astype(F32) for i in range(3)]
    return picked[0] + (picked[1] + picked[2])


def prepare_kernel(
    heads, key_ref, query_ref, table_ref, value_ref, output_ref, triple_ref, bias_ref, o_ref, p_ref
):
    cols = key_ref.shape[1]
    keys, table = key_ref[...], table_ref[...]
    lane = lax.broadcasted_iota(jnp.int32, (8, cols), 1)
    row = lax.broadcasted_iota(jnp.int32, (8, cols), 0)
    masked = jnp.where(lane // HEAD_DIM == row, query_ref[...], 0.0)
    folded = sum(dot(part, keys, NT) for part in split_three(masked)[::-1])
    folded_parts = split_three(folded)
    terms = sum(dot(part, table, NT) for part in folded_parts[::-1]) * SCALE
    bias = split_three(bias_ref[...])
    rows = [part[:heads].astype(F32) for part in split_three(terms)]
    rows += [part[:heads].astype(F32) for part in folded_parts[:2]]
    rows += [part.astype(F32) for part in bias]
    count = sum(part.shape[0] for part in rows)
    extra = o_ref.shape[0] - cols
    if extra > count:
        rows.append(jnp.zeros((extra - count, o_ref.shape[1]), F32))
    o_ref[:cols] = low(dot(table, value_ref[...]).T)
    o_ref[cols:] = low(jnp.concatenate(rows, 0))
    p_ref[:3] = triple_ref[...]
    p_ref[3] = output_ref[...].astype(F32).T.astype(BF16)


def prepare_call(heads, keys, query, table, values, output, triple, bias):
    depth, cols = keys.shape
    extra = -(-(5 * heads + 3) // 16) * 16
    return pl.pallas_call(
        lambda *refs: prepare_kernel(heads, *refs),
        out_shape=[struct((cols + extra, depth), BF16), struct((4, depth, cols), BF16)],
        compiler_params=params(),
        cost_estimate=cost(4 << 30, 4 << 20),
        name="prepare",
    )(keys, query, table, values, output, triple, bias)


def stage_kernel(up_ref, down_ref, output_ref, value_ref, o_ref):
    flip = lambda ref: ref[...].astype(F32).T.astype(BF16)
    o_ref[...] = jnp.concatenate([up_ref[...], flip(down_ref), flip(output_ref), value_ref[...]], 1)


def stage_call(up, down, output, value):
    lanes = up.shape[1] + down.shape[0] + output.shape[0] + value.shape[1]
    return pl.pallas_call(
        stage_kernel,
        out_shape=struct((up.shape[0], lanes), BF16),
        compiler_params=params(),
        cost_estimate=cost(1 << 28, 4 << 20),
        name="stage",
    )(up, down, output, value)


def arrange_kernel(x_ref, g_ref, x1_ref, xt_ref, gt_ref):
    pixels = x_ref[...]
    x1_ref[...] = jnp.concatenate([pixels, jnp.ones((pixels.shape[0], VARS), BF16)], 1)
    xt_ref[...] = pixels.astype(F32).T.astype(BF16)
    gt_ref[...] = g_ref[...].astype(F32).T.astype(BF16)


def arrange_call(pixels, grads):
    tokens, width = pixels.shape
    return pl.pallas_call(
        arrange_kernel,
        out_shape=[
            struct((tokens, width + VARS), BF16),
            struct((width, tokens), BF16),
            struct((grads.shape[1], tokens), BF16),
        ],
        compiler_params=params(),
        cost_estimate=cost(1 << 28, 4 << 20),
        name="arrange",
    )(pixels, grads)


def slot_mask():
    slot = lax.broadcasted_iota(jnp.int32, (VARS, VARS * PIX + VARS), 0)
    column = lax.broadcasted_iota(jnp.int32, (VARS, VARS * PIX + VARS), 1)
    return slot == jnp.where(column < VARS * PIX, column // PIX, column - VARS * PIX)


def mix(weights, pixels_wide):
    tokens = weights.shape[1]
    spread = weights[:, None, :] * pixels_wide
    return jnp.concatenate([low(spread.reshape(VARS * PIX, tokens)), low(weights)], 0)


def pool_kernel(x_ref, xt_ref, valid_ref, tvt_ref, extra_ref, w_ref, o_ref):
    cols = tvt_ref.shape[1]
    heads = cols // HEAD_DIM
    tokens, width = x_ref.shape
    pixels = x_ref[...]
    pixels_wide = xt_ref[...].astype(F32).reshape(VARS, PIX, tokens)
    valid = valid_ref[...] > 0
    extra = extra_ref[0].astype(F32)
    mask = slot_mask()
    parts = []
    for h in range(heads):
        scores = jnp.zeros((VARS, tokens), F32)
        for part in (2, 1, 0):
            row = extra[part * heads + h : part * heads + h + 1, :width]
            scores = scores + dot(low(jnp.where(mask, row, 0.0)), pixels, NT)
        scores = jnp.where(valid, scores, -1e30)
        weights = jnp.exp(scores - jnp.max(scores, 0, keepdims=True))
        weights = weights / jnp.sum(weights, 0, keepdims=True)
        w_ref[0, h] = weights
        mixed = mix(weights, pixels_wide)
        parts.append(dot(tvt_ref[0, h * HEAD_DIM : (h + 1) * HEAD_DIM, :width], mixed))
    pooled = jnp.concatenate(parts, 0) if heads > 1 else parts[0]
    shift = join(extra, 5 * heads, 1, 1)[:, :cols]
    o_ref[0] = low(pooled.T + shift)


def pool_call(pixels, pixels_t, valid, pack, cols, start, count):
    heads = cols // HEAD_DIM
    tokens, width = pixels.shape
    depth, extra = pack.shape[2], pack.shape[1] - cols
    return pl.pallas_call(
        pool_kernel,
        grid=(count,),
        in_specs=[
            fixed((tokens, width)),
            fixed(pixels_t.shape),
            fixed((VARS, 1)),
            per_block((cols, depth), start),
            per_block((extra, depth), start, cols // extra, 0),
        ],
        out_specs=[per_block((heads, VARS, tokens)), per_block((tokens, cols))],
        out_shape=[
            struct((count, heads, VARS, tokens), F32),
            struct((count, tokens, cols), BF16),
        ],
        compiler_params=params(),
        cost_estimate=cost(count * heads * tokens * 1400000, 4 << 20),
        name="pool",
    )(pixels, pixels_t, valid, pack, pack)


def pool_back_kernel(
    first, last, x_ref, xt_ref, w_ref, tvt_ref, out_ref, extra_ref, p_ref, g_ref, gt_ref, *rest
):
    if not first:
        before_ref, rest = rest[1], rest[2:]
    pack_ref, gx_ref, terms_ref, shift_ref = rest[:4]
    sum_ref = rest[4] if last else gx_ref
    cols = tvt_ref.shape[1]
    heads = cols // HEAD_DIM
    tokens, full = x_ref.shape
    width = VARS * PIX
    pixels = x_ref[...]
    pixels_wide = xt_ref[...].astype(F32).reshape(VARS, PIX, tokens)
    extra = extra_ref[0].astype(F32)
    mask = slot_mask()
    grads = low(dot(g_ref[...], out_ref[0, 0]))
    shift_ref[0] = jnp.sum(grads.astype(F32), 0, keepdims=True)
    lane = lax.broadcasted_iota(jnp.int32, grads.shape, 1)
    table_value = tvt_ref[0, :, :full].astype(F32).T.astype(BF16)
    product = jnp.zeros((full, cols), F32)
    total = jnp.zeros((width, tokens), F32)
    for h in range(heads):
        weights = w_ref[0, h]
        own = jnp.where(lane // HEAD_DIM == h, grads, 0) if heads > 1 else grads
        grad_mixed = dot(table_value, own, NT)
        grad_wide = grad_mixed[:width].reshape(VARS, PIX, tokens)
        grad_weights = jnp.sum(grad_wide * pixels_wide, 1) + grad_mixed[width:]
        inner = jnp.sum(weights * grad_weights, 0, keepdims=True)
        grad_scores = weights * (grad_weights - inner)
        product = product + dot(mix(weights, pixels_wide), own)
        total = total + (weights[:, None, :] * grad_wide).reshape(width, tokens)
        gs_top = low(grad_scores)
        gs_rest = low(grad_scores - gs_top.astype(F32))
        top, middle = [
            low(jnp.where(mask, extra[part * heads + h : part * heads + h + 1, :full], 0.0))[
                :, :width
            ]
            for part in (0, 1)
        ]
        stacked = jnp.concatenate([top, top, middle], 0)
        total = total + dot(stacked, jnp.concatenate([gs_top, gs_rest, gs_top], 0), TN)
        both = dot(jnp.concatenate([gs_top, gs_rest], 0), pixels)
        by_slot = jnp.where(mask, both[:VARS] + both[VARS:], 0.0)
        terms_ref[0, h : h + 1, :] = jnp.sum(by_slot, 0, keepdims=True)
    pack_ref[0, 0] = low(dot(gt_ref[...], p_ref[0]))
    pack_ref[0, 1, :full] = low(product)
    pack_ref[0, 1, full:] = jnp.zeros((pack_ref.shape[2] - full, cols), BF16)
    step = pl.program_id(0)

    @pl.when(step == 0)
    def _():
        if first:
            sum_ref[...] = total
        else:
            sum_ref[...] = before_ref[...] + total

    @pl.when(step > 0)
    def _():
        sum_ref[...] += total

    if last:

        @pl.when(step == pl.num_programs(0) - 1)
        def _():
            gx_ref[...] = low(sum_ref[...].T)


def pool_back_call(
    pixels, pixels_t, weights, pack, mixers, pooled, grads, grads_t, start, before, last
):
    count, heads, _, tokens = weights.shape
    depth = pack.shape[2]
    cols = heads * HEAD_DIM
    extra = pack.shape[1] - cols
    full = pixels.shape[1]
    width = pixels_t.shape[0]
    in_specs = [
        fixed(pixels.shape),
        fixed(pixels_t.shape),
        per_block((heads, VARS, tokens)),
        per_block((cols, depth), start),
        per_block((1, depth, cols), start, 3, 0, 0),
        per_block((extra, depth), start, cols // extra, 0),
        per_block((tokens, cols)),
        fixed(grads.shape),
        fixed(grads_t.shape),
    ]
    operands = [pixels, pixels_t, weights, pack, mixers, pack, pooled, grads, grads_t]
    aliases = {}
    if before:
        in_specs += [pl.BlockSpec(memory_space=pl.ANY), fixed((width, tokens))]
        aliases = {len(operands): 0}
        operands += list(before)
    total = struct((tokens, width), BF16) if last else struct((width, tokens), F32)
    return pl.pallas_call(
        lambda *refs: pool_back_kernel(not before, last, *refs),
        grid=(count,),
        in_specs=in_specs,
        out_specs=[
            per_block((2, depth, cols), start),
            fixed(total.shape),
            per_block((heads, full)),
            per_block((1, cols)),
        ],
        out_shape=[
            struct((pack.shape[0], 2, depth, cols), BF16),
            total,
            struct((count, heads, full), F32),
            struct((count, 1, cols), F32),
        ],
        scratch_shapes=[pltpu.VMEM((width, tokens), F32)] if last else [],
        input_output_aliases=aliases,
        compiler_params=params(),
        cost_estimate=cost(count * heads * tokens * 1700000, 6 << 20),
        name="pool_back",
    )(*operands)


def normalise(stream):
    centered = stream - jnp.mean(stream, -1, keepdims=True)
    scale = lax.rsqrt(jnp.mean(centered * centered, -1, keepdims=True) + 1e-05)
    return centered * scale, scale


def normalise_back(grad, stream, gain):
    hat, scale = normalise(stream)
    through = grad * gain
    inner = through - jnp.mean(through, -1, keepdims=True)
    inner = inner - hat * jnp.mean(through * hat, -1, keepdims=True)
    add = lambda tensor: jnp.sum(tensor, 0, keepdims=True)
    return scale * inner, add(grad * hat), add(grad)


def enter_kernel(p_refs, w_ref, bias_ref, gain_ref, shift_ref, s_ref, x_ref, xt_ref):
    stream = jnp.zeros(s_ref.shape, F32) + bias_ref[...]
    index = 0
    for p_ref in p_refs:
        for i in range(p_ref.shape[0]):
            stream = stream + dot(p_ref[i], w_ref[index, 0], NT)
            index += 1
    s_ref[...] = stream
    hat, _ = normalise(stream)
    rows = hat * gain_ref[...] + shift_ref[...]
    x_ref[...] = low(rows)
    xt_ref[...] = low(rows.T)


def enter_call(pooled, mixers, bias, gain, shift):
    tokens = pooled[0].shape[1]
    blocks, _, depth, cols = mixers.shape
    row = fixed((1, depth))
    count = len(pooled)
    return pl.pallas_call(
        lambda *refs: enter_kernel(refs[:count], *refs[count:]),
        grid=(1,),
        in_specs=[fixed(p.shape) for p in pooled]
        + [fixed((blocks, 1, depth, cols), 0, 3, 0, 0), row, row, row],
        out_specs=[fixed((tokens, depth)), fixed((tokens, depth)), fixed((depth, tokens))],
        out_shape=[
            struct((tokens, depth), F32),
            struct((tokens, depth), BF16),
            struct((depth, tokens), BF16),
        ],
        compiler_params=params(),
        cost_estimate=cost(2 << 30, 8 << 20),
        name="enter",
    )(*pooled, mixers, bias, gain, shift)


def beside(ref):
    return jnp.concatenate([ref[0, i] for i in range(3)], 1)


def project_kernel(x_ref, w_ref, extra_ref, q_ref, kv_ref):
    cols = q_ref.shape[2]
    heads = cols // HEAD_DIM
    bias = join(extra_ref[0], 5 * heads, 1, 1)
    triple = dot(x_ref[...], beside(w_ref))
    q_ref[0] = low(triple[:, :cols] + bias[:, cols : 2 * cols])
    kv_ref[0, 0] = low(triple[:, cols : 2 * cols])
    kv_ref[0, 1] = low(triple[:, 2 * cols :] + bias[:, 2 * cols : 3 * cols])


def project_call(rows, mixers, pack, start, count):
    _, _, depth, cols = mixers.shape
    tokens = rows.shape[0]
    extra = pack.shape[1] - cols
    return pl.pallas_call(
        project_kernel,
        grid=(count,),
        in_specs=[
            fixed((tokens, depth)),
            per_block((3, depth, cols), start),
            per_block((extra, depth), start, cols // extra, 0),
        ],
        out_specs=[per_block((tokens, cols)), per_block((2, tokens, cols))],
        out_shape=[
            struct((count, tokens, cols), BF16),
            struct((count, 2, tokens, cols), BF16),
        ],
        compiler_params=params(),
        cost_estimate=cost(9 * count * tokens * depth * cols, 3 << 20),
        name="project",
    )(rows, mixers, pack)


def project_back_kernel(first, xt_ref, w_ref, gq_ref, gkv_ref, *rest):
    before_ref, gx_ref, gw_ref, sums_ref = rest[1:] if not first else (None,) + rest[1:]
    cols = gq_ref.shape[2]
    grads = jnp.concatenate([gq_ref[0], gkv_ref[0, 0], gkv_ref[0, 1]], 1)
    total = dot(grads, beside(w_ref), NT)
    products = low(dot(xt_ref[...], grads))
    for i in range(3):
        gw_ref[0, i] = products[:, i * cols : (i + 1) * cols]
    sums_ref[0] = jnp.sum(grads.astype(F32), 0, keepdims=True)

    @pl.when(pl.program_id(0) == 0)
    def _():
        if first:
            gx_ref[...] = total
        else:
            gx_ref[...] = before_ref[...] + total

    @pl.when(pl.program_id(0) > 0)
    def _():
        gx_ref[...] += total


def project_back_call(rows_t, mixers, grad_query, grad_pair, start, grad_mixers, before):
    _, _, depth, cols = mixers.shape
    count, tokens, _ = grad_query.shape
    in_specs = [
        fixed((depth, tokens)),
        per_block((3, depth, cols), start),
        per_block((tokens, cols)),
        per_block((2, tokens, cols)),
        pl.BlockSpec(memory_space=pl.ANY),
    ]
    operands = [rows_t, mixers, grad_query, grad_pair, grad_mixers]
    if before is not None:
        in_specs.append(fixed((tokens, depth)))
        operands.append(before)
    return pl.pallas_call(
        lambda *refs: project_back_kernel(before is None, *refs),
        grid=(count,),
        in_specs=in_specs,
        out_specs=[
            fixed((tokens, depth)),
            per_block((3, depth, cols), start),
            per_block((1, 3 * cols)),
        ],
        out_shape=[
            struct((tokens, depth), F32),
            struct(grad_mixers.shape, BF16),
            struct((count, 1, 3 * cols), F32),
        ],
        input_output_aliases={4: 1},
        compiler_params=params(),
        cost_estimate=cost(15 * count * tokens * depth * cols, 8 << 20),
        name="project_back",
    )(*operands)


def leave_kernel(g_ref, s_ref, before_ref, gain_ref, o_ref, ot_ref, sums_ref):
    through, gain, shift = normalise_back(g_ref[...], s_ref[...], gain_ref[...])
    total = before_ref[...] + through
    rounded = low(total)
    o_ref[...] = rounded
    ot_ref[...] = low(total.T)
    bias = jnp.sum(rounded.astype(F32), 0, keepdims=True)
    sums_ref[...] = jnp.concatenate([gain, shift, bias], 0)


def leave_call(grad_normed, stream, before, gain):
    tokens, depth = stream.shape
    return pl.pallas_call(
        leave_kernel,
        out_shape=[
            struct((tokens, depth), BF16),
            struct((depth, tokens), BF16),
            struct((3, depth), F32),
        ],
        compiler_params=params(),
        cost_estimate=cost(1 << 30, 10 << 20),
        name="leave",
    )(grad_normed, stream, before, gain)


def attend_kernel(count, q_ref, *refs):
    sources, (o_ref, total_ref) = refs[:count], refs[count:]
    cols = q_ref.shape[2]
    heads = cols // HEAD_DIM
    scaled = q_ref[0] * SCALE
    lane = lax.broadcasted_iota(jnp.int32, scaled.shape, 1)
    values_t = [source[0, 1].T for source in sources]
    parts = []
    for h in range(heads):
        own = jnp.where(lane // HEAD_DIM == h, scaled, 0) if heads > 1 else scaled
        logits = [dot(source[0, 0], own, NT) for source in sources]
        peak = jnp.max(logits[0], 0, keepdims=True)
        for piece in logits[1:]:
            peak = jnp.maximum(peak, jnp.max(piece, 0, keepdims=True))
        norm = jnp.zeros_like(peak)
        out = jnp.zeros((HEAD_DIM, peak.shape[1]), F32)
        for piece, value in zip(logits, values_t):
            weight = jnp.exp(piece - peak)
            norm = norm + jnp.sum(weight, 0, keepdims=True)
            out = out + dot(value[h * HEAD_DIM : (h + 1) * HEAD_DIM], low(weight))
        parts.append(out / norm)
        total_ref[0, h] = peak + jnp.log(norm)
    full = jnp.concatenate(parts, 0) if heads > 1 else parts[0]
    o_ref[0] = full.T


def attend_call(queries, sources):
    count, tokens, cols = queries.shape
    heads = cols // HEAD_DIM
    keys = sum(array.shape[2] for array in sources)
    work = count * tokens * keys * cols
    return pl.pallas_call(
        lambda *refs: attend_kernel(len(sources), *refs),
        grid=(count,),
        in_specs=[per_block((tokens, cols))] + [per_block(array.shape[1:]) for array in sources],
        out_specs=[per_block((tokens, cols)), per_block((heads, 1, tokens))],
        out_shape=[
            struct((count, tokens, cols), F32),
            struct((count, heads, 1, tokens), F32),
        ],
        compiler_params=params(),
        cost_estimate=cost(25 * work, 4 << 20),
        name="attend",
    )(queries, *sources)


def middle_kernel(count, s_ref, *refs):
    o_refs, (w_ref, bias_ref, gain_ref, shift_ref, s1_ref, x_ref, xt_ref) = (
        refs[:count],
        refs[count:],
    )
    stream = s_ref[...] + bias_ref[...]
    index = 0
    for o_ref in o_refs:
        for i in range(o_ref.shape[0]):
            stream = stream + dot(low(o_ref[i]), w_ref[index], NT)
            index += 1
    s1_ref[...] = stream
    hat, _ = normalise(stream)
    rows = hat * gain_ref[...] + shift_ref[...]
    x_ref[...] = low(rows)
    xt_ref[...] = low(rows.T)


def middle_call(stream, attended, weights, bias, gain, shift):
    tokens, depth = stream.shape
    return pl.pallas_call(
        lambda *refs: middle_kernel(len(attended), *refs),
        out_shape=[
            struct((tokens, depth), F32),
            struct((tokens, depth), BF16),
            struct((depth, tokens), BF16),
        ],
        compiler_params=params(),
        cost_estimate=cost(2 << 30, 12 << 20),
        name="middle",
    )(stream, *attended, weights, bias, gain, shift)


def middle_back_kernel(g_ref, gt_ref, w_ref, o_ref, go_ref, gw_ref, delta_ref):
    cols = o_ref.shape[2]
    heads = cols // HEAD_DIM
    grads = low(dot(g_ref[...], w_ref[0]))
    go_ref[0] = grads
    attended = o_ref[0]
    gw_ref[0, 0] = low(dot(gt_ref[...], low(attended)))
    lane = lax.broadcasted_iota(jnp.int32, (8, cols), 1)
    row = lax.broadcasted_iota(jnp.int32, (8, cols), 0)
    mask = jnp.where(lane // HEAD_DIM == row, 1.0, 0.0)
    sums = dot(mask, grads.astype(F32) * attended, NT, precision=highest)
    for h in range(heads):
        delta_ref[0, h] = sums[h : h + 1]


def middle_back_call(grads, grads_t, weights, attended):
    blocks, tokens, cols = attended.shape
    depth = grads.shape[1]
    heads = cols // HEAD_DIM
    return pl.pallas_call(
        middle_back_kernel,
        grid=(blocks,),
        in_specs=[
            fixed((tokens, depth)),
            fixed((depth, tokens)),
            per_block((depth, cols)),
            per_block((tokens, cols)),
        ],
        out_specs=[
            per_block((tokens, cols)),
            per_block((1, depth, cols), 0, 3, 0, 0),
            per_block((heads, 1, tokens)),
        ],
        out_shape=[
            struct((blocks, tokens, cols), BF16),
            struct((blocks, 4, depth, cols), BF16),
            struct((blocks, heads, 1, tokens), F32),
        ],
        compiler_params=params(),
        cost_estimate=cost(6 << 30, 8 << 20),
        name="middle_back",
    )(grads, grads_t, weights, attended)


def attend_back_kernel(count, first, last, q_ref, g_ref, total_ref, delta_ref, *refs):
    sources, rest = refs[:count], refs[count:]
    before_ref, gq_ref, targets = (
        (None, rest[0], rest[1:]) if first else (rest[0], rest[1], rest[2:])
    )
    cols = q_ref.shape[2]
    heads = cols // HEAD_DIM
    scaled = q_ref[0] * SCALE
    grads = g_ref[0]
    lane = lax.broadcasted_iota(jnp.int32, scaled.shape, 1)
    pick = lambda tensor, h: jnp.where(lane // HEAD_DIM == h, tensor, 0) if heads > 1 else tensor
    own_q = [pick(scaled, h) for h in range(heads)]
    own_g = [pick(grads, h) for h in range(heads)]
    queries_t = [jnp.zeros((HEAD_DIM, scaled.shape[0]), F32) for h in range(heads)]
    for source, target in zip(sources, targets):
        keys, values = source[0, 0], source[0, 1]
        keys_t = keys.T
        grad_keys = jnp.zeros(keys.shape, F32)
        grad_values = jnp.zeros(keys.shape, F32)
        for h in range(heads):
            weight = jnp.exp(dot(keys, own_q[h], NT) - total_ref[0, h])
            grad_weight = dot(values, own_g[h], NT)
            grad_logit = low(weight * (grad_weight - delta_ref[0, h]))
            grad_values = grad_values + dot(low(weight), own_g[h])
            grad_keys = grad_keys + dot(grad_logit, own_q[h])
            queries_t[h] = queries_t[h] + dot(
                keys_t[h * HEAD_DIM : (h + 1) * HEAD_DIM], grad_logit
            )
        target[0, 0] = low(grad_keys)
        target[0, 1] = low(grad_values)
    full = jnp.concatenate(queries_t, 0) if heads > 1 else queries_t[0]
    if before_ref is not None:
        full = full + before_ref[0]
    gq_ref[0] = low(full * SCALE).T if last else full


def attend_back_call(queries, grads, totals, deltas, sources, start, before, last):
    count, tokens, cols = queries.shape
    heads = cols // HEAD_DIM
    keys = sum(array.shape[2] for array in sources)
    work = count * tokens * keys * cols
    block = sources[0].shape[1:]
    first = before is None
    result = struct((count, tokens, cols), BF16) if last else struct((count, cols, tokens), F32)
    return pl.pallas_call(
        lambda *refs: attend_back_kernel(len(sources), first, last, *refs),
        grid=(count,),
        in_specs=[
            per_block((tokens, cols)),
            per_block((tokens, cols), start),
            per_block((heads, 1, tokens)),
            per_block((heads, 1, tokens), start),
        ]
        + [per_block(block) for _ in sources]
        + ([] if first else [per_block((cols, tokens))]),
        out_specs=[per_block(result.shape[1:])] + [per_block(block) for _ in sources],
        out_shape=[result] + [struct((count,) + block, BF16) for _ in sources],
        compiler_params=params(),
        cost_estimate=cost(40 * work, 8 << 20),
        name="attend_back",
    )(queries, grads, totals, deltas, *sources, *([] if first else [before]))


def feed_kernel(
    cols,
    x_ref,
    xt_ref,
    g_ref,
    gt_ref,
    w_ref,
    extra_ref,
    s_ref,
    bias_ref,
    gain_ref,
    y_ref,
    gw_ref,
    gb_ref,
    gs_ref,
    g1_ref,
    g1t_ref,
    sums_ref,
    y_sum,
    gx_sum,
):
    parts, rows, wide = w_ref.shape
    depth, hidden = parts * rows, wide // 2
    heads = cols // HEAD_DIM
    step = pl.program_id(0)

    @pl.when(step == 0)
    def _():
        y_sum[...] = s_ref[...] + bias_ref[...]
        gx_sum[...] = jnp.zeros_like(gx_sum)

    up = w_ref[:, :, :hidden].reshape(depth, hidden)
    down = w_ref[:, :, hidden:].reshape(depth, hidden)
    up_bias = join(extra_ref[0], 5 * heads, 1, 1)[:, 3 * cols : 3 * cols + hidden]
    before = dot(x_ref[...], up) + up_bias
    bell = 0.5 * (1.0 + lax.erf(before * 0.7071067811865476))
    active = low(before * bell)
    slope = bell + before * (0.3989422804014327 * jnp.exp(-0.5 * before * before))
    grad_hidden = low(slope * dot(g_ref[...], down))
    y_sum[...] += dot(active, down, NT)
    gx_sum[...] += dot(grad_hidden, up, NT)
    gw_ref[:, :, :hidden] = low(dot(xt_ref[...], grad_hidden)).reshape(parts, rows, hidden)
    gw_ref[:, :, hidden:] = low(dot(gt_ref[...], active)).reshape(parts, rows, hidden)
    gb_ref[0] = jnp.sum(grad_hidden.astype(F32), 0, keepdims=True)

    @pl.when(step == pl.num_programs(0) - 1)
    def _():
        y_ref[...] = low(y_sum[...])
        through, gain, shift = normalise_back(gx_sum[...], s_ref[...], gain_ref[...])
        grads = g_ref[...].astype(F32)
        total = grads + through
        gs_ref[...] = total
        rounded = low(total)
        g1_ref[...] = rounded
        g1t_ref[...] = low(total.T)
        add = lambda tensor: jnp.sum(tensor, 0, keepdims=True)
        sums_ref[...] = jnp.concatenate([gain, shift, add(grads), add(rounded.astype(F32))], 0)


def feed_call(cols, rows, rows_t, grads, grads_t, weights, hidden, pack, stream, bias, gain, parts):
    tokens, depth = rows.shape
    pieces, slab, _ = weights.shape
    blocks = pieces // parts
    extra = pack.shape[1] - cols
    whole = fixed((tokens, depth))
    flipped = fixed((depth, tokens))
    row = fixed((1, depth))
    slabs = pl.BlockSpec((parts, slab, 2 * hidden), lambda n: (n, 0, 0))
    return pl.pallas_call(
        lambda *refs: feed_kernel(cols, *refs),
        grid=(blocks,),
        in_specs=[
            whole,
            flipped,
            whole,
            flipped,
            slabs,
            per_block((extra, depth), 0, cols // extra, 0),
            whole,
            row,
            row,
        ],
        out_specs=[whole, slabs, per_block((1, hidden)), whole, whole, flipped, fixed((4, depth))],
        out_shape=[
            struct((tokens, depth), BF16),
            struct((pieces, slab, 2 * hidden), BF16),
            struct((blocks, 1, hidden), F32),
            struct((tokens, depth), F32),
            struct((tokens, depth), BF16),
            struct((depth, tokens), BF16),
            struct((4, depth), F32),
        ],
        scratch_shapes=[pltpu.VMEM((tokens, depth), F32), pltpu.VMEM((tokens, depth), F32)],
        compiler_params=params(),
        cost_estimate=cost(18 * blocks * tokens * depth * hidden, 40 << 20),
        name="feed",
    )(rows, rows_t, grads, grads_t, weights, pack, stream, bias, gain)


def assemble_kernel(w_ref, *refs):
    pieces, (up_ref, down_ref) = refs[:-2], refs[-2:]
    hidden = up_ref.shape[1]
    for index, piece in enumerate(pieces):

        @pl.when(pl.program_id(0) == index)
        def _():
            up_ref[...] = piece[:, :hidden].astype(F32)
            down_ref[...] = piece[:, hidden:].astype(F32).T


def assemble_call(w, pieces):
    count = len(pieces)
    slab, lanes = pieces[0].shape
    hidden = lanes // 2
    direct = slab % 128 == 0
    down_shape = (hidden, count * slab) if direct else (count * hidden, slab)
    down_spec = (
        pl.BlockSpec((hidden, slab), lambda i, w_ref: (0, w_ref[0] ^ i))
        if direct
        else pl.BlockSpec((hidden, slab), lambda i, w_ref: (w_ref[0] ^ i, 0))
    )
    up, down = pl.pallas_call(
        assemble_kernel,
        grid_spec=pltpu.PrefetchScalarGridSpec(
            num_scalar_prefetch=1,
            grid=(count,),
            in_specs=[pl.BlockSpec((slab, lanes), lambda i, w_ref: (0, 0)) for _ in pieces],
            out_specs=[pl.BlockSpec((slab, hidden), lambda i, w_ref: (w_ref[0] ^ i, 0)), down_spec],
        ),
        out_shape=[struct((count * slab, hidden), F32), struct(down_shape, F32)],
        compiler_params=params(),
        cost_estimate=cost(1 << 28, 8 << 20),
        name="assemble",
    )(w.reshape(1), *pieces)
    if not direct:
        down = down.reshape(count, hidden, slab).transpose(1, 0, 2).reshape(hidden, count * slab)
    return up, down


def on_device(
    wide_size,
    narrow_size,
    variables,
    valid_slots,
    out_grad,
    patch_embed,
    variable_embed,
    pool_query,
    pool_key,
    pool_value,
    value_shift,
    pool_output,
    pool_bias,
    first_gain,
    first_shift,
    self_weights,
    query_bias,
    value_bias,
    self_output,
    output_bias,
    second_gain,
    second_shift,
    feed_up,
    up_bias,
    feed_down,
    down_bias,
):
    ring = Ring(wide_size, narrow_size)
    samples, token_count, input_width = variables.shape
    model_width = patch_embed.shape[1]
    local_dim = pool_query.shape[0]
    heads = local_dim // HEAD_DIM
    hidden = up_bias.shape[0]
    slab = model_width // wide_size
    shares = narrow_size // samples
    tokens = token_count // shares
    row = lambda vector: vector.reshape(1, -1)
    place = (ring.n // shares, (ring.n % shares) * tokens, 0)
    pixels = lax.dynamic_slice(variables, place, (1, tokens, input_width))[0]
    grads = lax.dynamic_slice(out_grad, place, (1, tokens, model_width))[0]
    valid = lax.dynamic_index_in_dim(valid_slots, ring.n // shares, 0, keepdims=False)
    valid = valid.reshape(VARS, 1)

    filler = jnp.zeros((model_width - input_width - VARS, model_width), BF16)
    table_full = jnp.concatenate([patch_embed, variable_embed, filler], 0)
    table_low = table_full[: input_width + VARS]
    bias_own = jnp.concatenate([value_shift, query_bias, value_bias, up_bias])
    bias_own = row(jnp.pad(bias_own, (0, model_width - bias_own.shape[0])))
    pack_own, mixers_own = prepare_call(
        heads,
        pool_key,
        row(pool_query),
        table_full,
        pool_value,
        pool_output,
        self_weights.transpose(1, 0, 2),
        bias_own,
    )
    pack = GatherShared(ring, pack_own).finish()
    gather = GatherShared(ring, tie(mixers_own, pack))
    pixels_one, pixels_t, grads_t = arrange_call(pixels, grads)
    rows_of = lambda tensor: lax.dynamic_slice_in_dim(tensor, ring.w * slab, slab, 0)
    columns_of = lambda tensor: lax.dynamic_slice_in_dim(tensor, ring.w * slab, slab, 1)
    feed_own = stage_call(
        rows_of(feed_up), columns_of(feed_down), columns_of(self_output), rows_of(pool_value)
    )
    feed_all = lax.all_gather(tie(feed_own, pack), ("narrow", "wide"))

    half = narrow_size // 2
    head_a = pool_call(pixels_one, pixels_t, valid, pack, local_dim, 0, half)
    head_b = pool_call(
        tie(pixels_one, gather.step(), head_a[1]), pixels_t, valid, pack, local_dim, half, half
    )
    pooled = [head_a[1], tie(head_b[1], gather.step())]
    mixers = gather.finish()
    stream_zero, normed_one, normed_one_t = enter_call(
        pooled, mixers, row(pool_bias), row(first_gain), row(first_shift)
    )

    permuted = wide_size == 4 and shares == 1
    groups = 4
    size = narrow_size // groups
    subsets = [[s * shares + i for i in range(shares)] for s in range(samples)]
    queries, sources = [], []
    for g in range(groups):
        mine, pair = project_call(normed_one, mixers, pack, g * size, size)
        queries.append(mine)
        if permuted:
            across = ring.swap(pair, 2)
            sources.append([pair, ring.swap(pair, 1), across, ring.swap(across, 1)])
        else:
            full = lax.all_gather(pair, "wide", axis=2, tiled=True)
            if shares > 1:
                full = lax.all_gather(
                    full, "narrow", axis=2, tiled=True, axis_index_groups=subsets
                )
            sources.append([full])
    attended, totals = [], []
    for g in range(groups):
        start = queries[g]
        if attended:
            start = tie(start, attended[-1])
        if permuted and g + 1 < groups:
            start = tie(start, sources[g + 1][2])
        got = attend_call(start, sources[g])
        attended.append(got[0])
        totals.append(got[1])
    part_of = lambda start, length: feed_all[:, :, start : start + length].reshape(
        narrow_size, model_width, length
    )
    self_all = part_of(2 * hidden, local_dim)
    value_all = part_of(2 * hidden + local_dim, local_dim)
    stream_one, normed_two, normed_two_t = middle_call(
        stream_zero, attended, self_all, row(output_bias), row(second_gain), row(second_shift)
    )

    block_own, grad_feed, grad_up_bias, grad_stream_one, grad_one, grad_one_t, sums_two = feed_call(
        local_dim,
        normed_two,
        normed_two_t,
        grads,
        grads_t,
        feed_all,
        hidden,
        pack,
        stream_one,
        row(down_bias),
        row(second_gain),
        wide_size,
    )
    gather_out = GatherOwn(ring, block_own, BF16)
    grad_feed = lax.psum_scatter(grad_feed, ("narrow", "wide"), scatter_dimension=0, tiled=True)
    grad_attended, grad_mixers, deltas = middle_back_call(
        grad_one, grad_one_t, self_all, jnp.concatenate(attended, 0)
    )

    token = grad_attended
    waiting = []
    for g in range(groups):
        back = lambda sources, before, last: attend_back_call(
            queries[g], token, totals[g], deltas, sources, g * size, before, last
        )
        if permuted:
            own, core, across, diagonal = sources[g]
            some, grad_core, grad_diagonal = back([core, diagonal], None, False)
            from_core = ring.swap(grad_core)
            from_diagonal = ring.swap(grad_diagonal)
            grad_query, grad_own, grad_across = back([own, across], some, True)
            far = low(grad_across.astype(F32) + from_diagonal.astype(F32))
            near = grad_own.astype(F32) + from_core.astype(F32)
            grad_pair = low(near + ring.swap(far, 2).astype(F32))
            token = tie(grad_attended, far)
        else:
            grad_query, full = back(sources[g], None, True)
            if shares > 1:
                full = lax.psum_scatter(
                    full, "narrow", scatter_dimension=2, tiled=True, axis_index_groups=subsets
                )
            grad_pair = lax.psum_scatter(full, "wide", scatter_dimension=2, tiled=True)
            token = tie(grad_attended, grad_query)
        if g == 1:
            token = tie(token, *gather_out.step())
        waiting.append((grad_query, grad_pair))
    grad_normed_one, sums_triple = None, []
    for g in range(groups):
        grad_query, grad_pair = waiting[g]
        if g == 1:
            grad_query = tie(grad_query, *gather_out.step())
        grad_normed_one, grad_mixers, sums = project_back_call(
            normed_one_t, mixers, grad_query, grad_pair, g * size, grad_mixers, grad_normed_one
        )
        sums_triple.append(sums)
    scatter = ScatterShared(ring, grad_mixers)
    grad_zero, grad_zero_t, sums_one = leave_call(
        grad_normed_one, stream_zero, grad_stream_one, row(first_gain)
    )

    quarter = half // 2 if half > 1 else half
    backs, before = [], None
    for start in range(0, narrow_size, quarter):
        weights, mixed = [piece[start % half : start % half + quarter] for piece in (
            head_a if start < half else head_b
        )]
        last = start + quarter == narrow_size
        first = pixels_one
        if start == quarter:
            first = tie(first, *gather_out.step())
        if start == 2 * quarter:
            first = tie(first, scatter.step())
        if last:
            first = tie(first, *gather_out.step())
        backs.append(
            pool_back_call(
                first,
                pixels_t,
                weights,
                pack,
                mixers,
                mixed,
                grad_zero,
                grad_zero_t,
                start,
                before,
                last,
            )
        )
        before = backs[-1][:2]
    grad_last, grad_pixels = before
    scatter_last = ScatterShared(ring, grad_last)
    scatter_last.step()
    scatter.step()
    gather_pixels = GatherOwn(ring, grad_pixels, F32)
    gather_pixels.step()
    block_out = gather_out.finish().reshape(samples, token_count, model_width)
    grad_pool_output, product = ring.finish_shared(scatter_last.finish())
    grad_pool_output = grad_pool_output[0].T
    product = low(product[0, : input_width + VARS])
    gather_product = GatherShared(ring, product)
    grad_variables = gather_pixels.finish().reshape(samples, token_count, input_width)
    grad_pool_value = dot(table_low, product, TN)
    grad_first, grad_second = ring.finish_shared(scatter.finish())
    grad_triple = jnp.concatenate([grad_first, grad_second[:1]], 0).transpose(1, 0, 2)
    grad_self_output = grad_second[1].T
    product_all = gather_product.finish()

    sums_triple = jnp.concatenate(sums_triple, 0).reshape(narrow_size, 3, local_dim)
    small = [
        sums_one,
        sums_two,
        jnp.concatenate([back[3] for back in backs], 0),
        sums_triple[:, 0],
        sums_triple[:, 2],
        grad_up_bias,
        jnp.concatenate([back[2] for back in backs], 0),
    ]
    lengths = [piece.size for piece in small]
    summed = jnp.concatenate([piece.reshape(-1) for piece in small])
    summed = ring.add_everywhere(summed.reshape(-1, 128)).reshape(-1)
    pieces, start = [], 0
    for length in lengths:
        pieces.append(summed[start : start + length])
        start += length
    grad_first_gain, grad_first_shift, grad_pool_bias = pieces[0].reshape(3, model_width)
    grad_second_gain, grad_second_shift, grad_down_bias, grad_output_bias = pieces[1].reshape(
        4, model_width
    )
    own_part = lambda piece, length: lax.dynamic_slice_in_dim(piece, ring.n * length, length, 0)
    grad_value_shift = own_part(pieces[2], local_dim)
    grad_query_bias = own_part(pieces[3], local_dim)
    grad_value_bias = own_part(pieces[4], local_dim)
    grad_up_bias = own_part(pieces[5], hidden)
    grad_terms = SCALE * pieces[6].reshape(narrow_size * heads, -1)
    grad_proj = own_part(grad_terms, heads)
    grad_folded = jnp.einsum("hr,rd->hd", grad_proj, table_low.astype(F32), precision=highest)
    query_heads = pool_query.reshape(heads, HEAD_DIM)
    key_heads = pool_key.astype(F32).reshape(model_width, heads, HEAD_DIM)
    grad_pool_key = (grad_folded.T[:, :, None] * query_heads).reshape(model_width, local_dim)
    grad_pool_query = jnp.einsum("dhe,hd->he", key_heads, grad_folded, precision=highest).reshape(
        local_dim
    )
    first_fold = local_dim + 3 * heads
    folded_all = pack[:, first_fold : first_fold + heads].astype(F32)
    folded_all = folded_all + pack[:, first_fold + heads : first_fold + 2 * heads].astype(F32)
    grad_table = jnp.einsum(
        "nrc,ndc->rd", product_all, value_all, preferred_element_type=F32
    ) + dot(
        grad_terms, folded_all.reshape(narrow_size * heads, model_width), TN, precision=highest
    )

    grad_feed_up, grad_feed_down = assemble_call(ring.w, ring.gather_wide(grad_feed[0]))
    return (
        block_out,
        grad_variables,
        grad_table[:input_width],
        grad_table[input_width:],
        grad_pool_query,
        grad_pool_key,
        grad_pool_value,
        grad_value_shift,
        grad_pool_output,
        grad_pool_bias,
        grad_first_gain,
        grad_first_shift,
        grad_triple,
        grad_query_bias,
        grad_value_bias,
        grad_self_output,
        grad_output_bias,
        grad_second_gain,
        grad_second_shift,
        grad_feed_up,
        grad_up_bias,
        grad_feed_down,
        grad_down_bias,
    )


def solution(mesh):
    wide_size, narrow_size = mesh.shape["wide"], mesh.shape["narrow"]

    def body(*arrays):
        return on_device(wide_size, narrow_size, *arrays)

    return jax.shard_map(
        body,
        mesh=mesh,
        in_specs=(
            P(None, "wide", None),
            P(),
            P(None, "wide", None),
            P(),
            P(),
            P("narrow"),
            P(None, "narrow"),
            P(None, "narrow"),
            P("narrow"),
            P("narrow", None),
            P(),
            P(),
            P(),
            P(None, None, "narrow"),
            P("narrow"),
            P("narrow"),
            P("narrow", None),
            P(),
            P(),
            P(),
            P(None, "narrow"),
            P("narrow"),
            P("narrow", None),
            P(),
        ),
        out_specs=(
            P(None, "wide", None),
            P(None, "wide", None),
            P(),
            P(),
            P("narrow"),
            P(None, "narrow"),
            P(None, "narrow"),
            P("narrow"),
            P("narrow", None),
            P(),
            P(),
            P(),
            P(None, None, "narrow"),
            P("narrow"),
            P("narrow"),
            P("narrow", None),
            P(),
            P(),
            P(),
            P(None, "narrow"),
            P("narrow"),
            P("narrow", None),
            P(),
        ),
        check_vma=False,
    )
```

```python
import math

import jax
import jax.numpy as jnp
from jax import lax
from jax.experimental import pallas as pl
from jax.experimental.pallas import tpu as pltpu
from jax.sharding import PartitionSpec as P

HEAD_DIM = 64
VARS = 48
PIX = 16
SCALE = HEAD_DIM ** (-0.5)

highest = lax.Precision.HIGHEST
AXES = ("wide", "narrow")
F32 = jnp.float32
BF16 = jnp.bfloat16


def low(tensor):
    return tensor.astype(BF16)


def dot(left, right, dims=((1,), (0,)), precision=None):
    return lax.dot_general(
        left, right, (dims, ((), ())), precision=precision, preferred_element_type=F32
    )


NT = ((1,), (1,))
TN = ((0,), (0,))


def struct(shape, dtype):
    return jax.ShapeDtypeStruct(shape, dtype)


class Gate:
    waits, hands, handed = [], [], []


def wait_for(*arrays):
    Gate.waits += arrays


def hand_on(*arrays):
    Gate.hands += arrays


def whole_block():
    return pl.BlockSpec(memory_space=pltpu.VMEM)


def pallas(
    kernel,
    out_shape,
    grid=(),
    in_specs=None,
    out_specs=None,
    scratch_shapes=(),
    prefetch=0,
    input_output_aliases=None,
    us=1,
    mib=28,
    name=None,
):
    single = not isinstance(out_shape, (list, tuple))
    shapes = [out_shape] if single else list(out_shape)
    if out_specs is None:
        outs = [whole_block() for _ in shapes]
    else:
        outs = [out_specs] if single else list(out_specs)

    def call(*operands):
        waits, hands = Gate.waits, Gate.hands
        Gate.waits, Gate.hands = [], []
        given = len(operands)
        specs = list(in_specs) if in_specs is not None else [whole_block() for _ in operands]
        aliases = dict(input_output_aliases or {})
        aliases |= {given + len(waits) + i: len(shapes) + i for i in range(len(hands))}
        extra = len(waits) + len(hands)

        def body(*refs):
            kept = refs[:given] + refs[given + extra : given + extra + len(shapes)]
            kernel(*kept, *refs[given + extra + len(shapes) + len(hands) :])

        got = pl.pallas_call(
            body,
            grid_spec=pltpu.PrefetchScalarGridSpec(
                num_scalar_prefetch=prefetch,
                grid=grid,
                in_specs=specs + [anywhere() for _ in range(extra)],
                out_specs=outs + [anywhere() for _ in hands],
                scratch_shapes=scratch_shapes,
            ),
            out_shape=shapes + [struct(array.shape, array.dtype) for array in hands],
            input_output_aliases=aliases,
            compiler_params=pltpu.CompilerParams(vmem_limit_bytes=mib << 20),
            cost_estimate=pl.CostEstimate(
                flops=int(us * 1.15e9), bytes_accessed=0, transcendentals=0
            ),
            name=name,
        )(*operands, *waits, *hands)
        Gate.handed = list(got[len(shapes) :])
        return got[0] if single else list(got[: len(shapes)])

    return call


def fixed(shape, *start):
    start = start or (0,) * len(shape)
    return pl.BlockSpec(shape, lambda *_: start)


def per_block(shape, offset=0, *rest):
    rest = rest or (0,) * len(shape)
    return pl.BlockSpec((1,) + shape, lambda n: (n + offset,) + rest)


def anywhere():
    return pl.BlockSpec(memory_space=pl.ANY)


class Ring:
    def __init__(self, wide_size, narrow_size, in_order):
        self.wide, self.narrow, self.sorted = wide_size, narrow_size, in_order
        self.order = list(range(0, narrow_size, 2)) + list(range(1, narrow_size, 2))[::-1]
        place = {device: index for index, device in enumerate(self.order)}
        self.w = lax.axis_index("wide")
        self.n = lax.axis_index("narrow")
        self.core = self.w % 2
        self.pos = jnp.where(self.n % 2 == 0, self.n // 2, narrow_size - 1 - self.n // 2)

        def step(device, hops):
            return self.order[(place[device] + hops) % narrow_size]

        every = [(w, n) for w in range(wide_size) for n in range(narrow_size)]
        flat = lambda w, n: w * narrow_size + n
        bits = lambda size: [1 << i for i in range(size.bit_length() - 1)]
        self.forward = [(flat(w, n), flat(w, step(n, 1))) for w, n in every]
        self.backward = [(flat(w, n), flat(w, step(n, -1))) for w, n in every]
        self.by_core = [(flat(w, n), flat(w, step(n, 1 - 2 * (w % 2)))) for w, n in every]
        self.by_core_back = [(dst, src) for src, dst in self.by_core]
        self.wide_swap = {
            bit: [(flat(w, n), flat(w ^ bit, n)) for w, n in every] for bit in bits(wide_size)
        }
        self.narrow_swap = {
            bit: [(flat(w, n), flat(w, n ^ bit)) for w, n in every] for bit in bits(narrow_size)
        }

    def move(self, tensor, pairs):
        return lax.ppermute(tensor, AXES, pairs)

    def swap(self, tensor, bit=1):
        return self.move(tensor, self.wide_swap[bit])

    def at(self, hops):
        index = (self.pos + hops + 2 * self.narrow) % self.narrow
        return jnp.where(2 * index < self.narrow, 2 * index, 2 * (self.narrow - 1 - index) + 1)

    def ordered(self, first, second):
        if not self.sorted:
            return first, second
        pick = lambda a, b: jnp.where(self.core == 0, a, b)
        return pick(first, second), pick(second, first)

    def places(self):
        size = self.narrow
        sign = 1 if self.sorted else jnp.where(self.core == 0, 1, -1)
        order = [self.n, self.at(size // 2)]
        for hops in range(1, size // 2):
            order += [self.at(-sign * hops), self.at(sign * hops)]
        return order

    def scatter_wide(self, parts):
        parts = list(parts)
        for bit in self.wide_swap:
            kept = [index for index in range(self.wide) if index % (2 * bit) == 0]
            moved = [self.swap(parts[index | bit], bit) for index in kept]
            if len(kept) == 1:
                return parts[0], moved[0]
            sums = add_groups([[parts[index], got] for index, got in zip(kept, moved)])
            for index, total in zip(kept, sums):
                parts[index] = total

    def gather_wide(self, block):
        pieces = {0: block}
        for bit in self.wide_swap:
            for shift in list(pieces):
                pieces[shift | bit] = self.swap(pieces[shift], bit)
        return [pieces[shift] for shift in range(self.wide)]


def blank(shape, dtype):
    return pallas(
        lambda o_ref: None,
        out_shape=struct(shape, dtype),
        out_specs=anywhere(),
        us=0.1,
        name="blank",
    )()


def put(out, piece, index):
    return lax.dynamic_update_index_in_dim(out, piece, index, 0)


def add_kernel(groups, *refs):
    refs, outs = refs[: -len(groups)], refs[-len(groups) :]
    for size, out_ref in zip(groups, outs):
        total = refs[0][...].astype(F32)
        for ref in refs[1:size]:
            total = total + ref[...].astype(F32)
        out_ref[...] = low(total)
        refs = refs[size:]


def add_groups(groups):
    first = groups[0][0]
    shape = first[0].shape[1:] if isinstance(first, tuple) else first.shape
    width, size = shape[-1], math.prod(shape)
    rows = size // width
    steps = max(1, size * 2 >> 20)
    specs, flat = [], []
    for item in [item for group in groups for item in group]:
        array, part = item if isinstance(item, tuple) else (item, 0)
        start = part * steps
        specs.append(pl.BlockSpec((rows // steps, width), lambda i, start=start: (start + i, 0)))
        flat.append(array.reshape(-1, width))
    sums = pallas(
        lambda *refs: add_kernel([len(group) for group in groups], *refs),
        grid=(steps,),
        in_specs=specs,
        out_specs=[pl.BlockSpec((rows // steps, width), lambda i: (i, 0))] * len(groups),
        out_shape=[struct((rows, width), BF16)] * len(groups),
        us=2,
        mib=20,
        name="add",
    )(*flat)
    return [total.reshape(shape) for total in sums]


def add_up(*arrays):
    return add_groups([arrays])[0]


def pass_kernel(o_ref):
    o_ref[...] = jnp.zeros_like(o_ref)


def pass_on(arrays, *earlier):
    wait_for(*earlier)
    hand_on(*arrays)
    pallas(pass_kernel, out_shape=struct((8, 128), F32), us=0.5, mib=4, name="pass")()
    return Gate.handed


class GatherShared:
    def __init__(self, ring, block):
        self.ring, self.current, self.own = ring, block, block
        self.pairs, self.far = [], None

    def step(self, *earlier):
        ring = self.ring
        self.current = ring.move(self.current, ring.by_core)
        if earlier:
            (self.current,) = pass_on([self.current], *earlier)
        if 2 * (len(self.pairs) + 1) < ring.narrow:
            self.pairs.append(ring.ordered(self.current, ring.swap(self.current)))
            return self.pairs[-1]
        self.far = self.current
        return [self.far]

    def finish(self):
        while self.far is None:
            self.step()
        return [self.own, self.far] + [piece for pair in self.pairs for piece in pair]


class ScatterOwn:
    def __init__(self, ring, blocks):
        self.ring, self.blocks, self.hops = ring, blocks, ring.narrow // 2
        self.ahead, self.behind = self.pick(self.hops), None

    def pick(self, hops):
        return lax.dynamic_index_in_dim(self.blocks, self.ring.at(hops), 0, keepdims=False)

    def step(self):
        ring, self.hops = self.ring, self.hops - 1
        ahead = ring.move(self.ahead, ring.backward)
        behind = [] if self.behind is None else [ring.move(self.behind, ring.forward)]
        if not self.hops:
            self.ahead = add_up(ahead, *behind, self.pick(0))
        elif behind:
            self.ahead, self.behind = add_groups(
                [[ahead, self.pick(-self.hops)], [behind[0], self.pick(self.hops)]]
            )
        else:
            self.ahead, self.behind = add_up(ahead, self.pick(-self.hops)), self.pick(self.hops)
        return self.ahead


class GatherOwn:
    def __init__(self, ring, block, dtype):
        self.ring, self.hops, self.dtype = ring, 0, dtype
        self.moving = [block, block]
        self.out = blank((ring.narrow,) + block.shape, dtype)
        self.out = put(self.out, block.astype(dtype), ring.n)
        self.send()

    def send(self):
        ring, self.hops = self.ring, self.hops + 1
        ways = [ring.forward, ring.backward] if 2 * self.hops < ring.narrow else [ring.forward]
        self.moving = [ring.move(block, way) for block, way in zip(self.moving, ways)]

    def place(self):
        for block, sign in zip(self.moving, (-1, 1)):
            index = self.ring.at(sign * self.hops)
            self.out = put(self.out, block.astype(self.dtype), index)
        self.done = 2 * self.hops >= self.ring.narrow
        if not self.done:
            self.send()

    def beside(self, kernel):
        hand_on(*self.moving)
        got = kernel()
        self.moving = list(Gate.handed)
        self.place()
        return got

    def after(self, *earlier):
        self.moving = list(pass_on(self.moving, *earlier))
        self.place()

    def finish(self):
        while not self.done:
            self.place()
        return self.out


class ScatterShared:
    def __init__(self, ring, own, far):
        self.ring, self.own, self.current, self.got = ring, own, far, far

    def step(self, pair=None):
        ring = self.ring
        moved = ring.move(self.current, ring.by_core_back)
        if pair:
            first, second = ring.ordered(*pair)
            self.current = add_up(moved, first, ring.swap(second))
        else:
            self.current = add_up(moved, self.own)
        return self.current


class FinishShared:
    def __init__(self, ring, partial):
        self.ring, half = ring, partial.shape[0] // 2
        cut = lambda side: lax.dynamic_slice_in_dim(partial, side * half, half, 0)
        self.current, self.theirs = cut(ring.core), cut(1 - ring.core)
        self.bits = list(ring.wide_swap)

    def step(self):
        ring, bit = self.ring, self.bits.pop(0)
        sent = self.theirs if bit == 1 else self.current
        self.current = add_up(self.current, ring.swap(sent, bit))
        return self.current

    def finish(self):
        while self.bits:
            self.step()
        other = self.ring.swap(self.current)
        first = jnp.where(self.ring.core == 0, self.current, other).astype(F32)
        second = jnp.where(self.ring.core == 0, other, self.current).astype(F32)
        return first, second


class AddEverywhere:
    def __init__(self, ring, tensor):
        self.ring, self.current = ring, tensor
        self.pairs = list(ring.wide_swap.values()) + list(ring.narrow_swap.values())

    def step(self):
        self.current = self.current + self.ring.move(self.current, self.pairs.pop(0))
        return self.current

    def finish(self):
        while self.pairs:
            self.step()
        return self.current


def split_three(tensor):
    top = low(tensor)
    rest = tensor - top.astype(F32)
    middle = low(rest)
    return top, middle, low(rest - middle.astype(F32))


def lanes_to_rows(vector, cols):
    length = vector.shape[1]
    count = -(-length // cols)
    if count * cols > length:
        vector = jnp.concatenate([vector, jnp.zeros((1, count * cols - length), F32)], 1)
    return jnp.concatenate([vector[:, i * cols : (i + 1) * cols] for i in range(count)], 0)


def rows_to_lanes(rows, start, length):
    count = -(-length // rows.shape[1])
    return jnp.concatenate([rows[start + i : start + i + 1] for i in range(count)], 1)[:, :length]


class Extra:
    def __init__(self, cols, depth):
        self.heads, self.full = cols // HEAD_DIM, VARS * PIX + VARS
        self.term_rows, self.fold_rows = -(-self.full // cols), depth // cols
        self.fold_start = 3 * self.heads * self.term_rows
        self.bias_start = self.fold_start + 2 * self.heads * self.fold_rows

    def term(self, rows, part, head):
        return rows_to_lanes(rows, (part * self.heads + head) * self.term_rows, self.full)

    def folded(self, rows, head):
        place = lambda part: self.fold_start + (part * self.heads + head) * self.fold_rows
        length = self.fold_rows * rows.shape[1]
        return rows_to_lanes(rows, place(0), length) + rows_to_lanes(rows, place(1), length)

    def bias(self, rows, index):
        parts = [rows[self.bias_start + 3 * i + index :][:1] for i in range(3)]
        return parts[0] + (parts[1] + parts[2])


def prepare_kernel(
    key_ref, query_ref, table_ref, value_ref, output_ref, triple_ref, bias_ref, o_ref
):
    depth, cols = key_ref.shape
    extra = Extra(cols, depth)
    heads, full = extra.heads, extra.full
    keys, table = key_ref[...], table_ref[...]
    lane = lax.broadcasted_iota(jnp.int32, (8, cols), 1)
    row = lax.broadcasted_iota(jnp.int32, (8, cols), 0)
    masked = jnp.where(lane // HEAD_DIM == row, query_ref[...], 0.0)
    folded = sum(dot(part, keys, NT) for part in split_three(masked)[::-1])
    folded_parts = split_three(folded)
    terms = sum(dot(part, table, NT) for part in folded_parts[::-1]) * SCALE
    rows = [
        lanes_to_rows(part[h : h + 1, :full].astype(F32), cols)
        for part in split_three(terms)
        for h in range(heads)
    ]
    rows += [
        lanes_to_rows(part[h : h + 1].astype(F32), cols)
        for part in folded_parts[:2]
        for h in range(heads)
    ]
    rows += [lanes_to_rows(part.astype(F32), cols) for part in split_three(bias_ref[...])]
    rows.append(jnp.zeros((depth - full - sum(part.shape[0] for part in rows), cols), F32))
    o_ref[:3] = triple_ref[...]
    o_ref[3] = output_ref[...].astype(F32).T.astype(BF16)
    o_ref[4, :full] = low(dot(table, value_ref[...])[:full])
    o_ref[4, full:] = low(jnp.concatenate(rows, 0))


def prepare_call(keys, query, table, values, output, triple, bias):
    depth, cols = keys.shape
    return pallas(
        prepare_kernel,
        out_shape=struct((5, depth, cols), BF16),
        us=5.7,
        mib=40,
        name="prepare",
    )(keys, query, table, values, output, triple, bias)


def stage_kernel(up_ref, down_ref, value_ref, bias_ref, o_ref):
    depth, hidden = up_ref.shape
    cols = value_ref.shape[1]
    flip = lambda ref: ref[...].astype(F32).T.astype(BF16)
    o_ref[:cols] = flip(value_ref)
    o_ref[cols : cols + hidden] = flip(up_ref)
    o_ref[cols + hidden : cols + 2 * hidden] = down_ref[...]
    parts = [part.astype(F32) for part in split_three(bias_ref[...])]
    block = jnp.concatenate(parts + [jnp.zeros((13, hidden), F32)], 0)
    if hidden < depth:
        block = jnp.concatenate([block, jnp.zeros((16, depth - hidden), F32)], 1)
    o_ref[cols + 2 * hidden :] = low(block)


def stage_call(up, down, value, bias):
    depth, hidden = up.shape
    return pallas(
        stage_kernel,
        out_shape=struct((value.shape[1] + 2 * hidden + 16, depth), BF16),
        us=2,
        mib=40,
        name="stage",
    )(up, down, value, bias)


def arrange_kernel(x_ref, x1_ref, xt_ref):
    pixels = x_ref[...]
    x1_ref[...] = jnp.concatenate([pixels, jnp.ones((pixels.shape[0], VARS), BF16)], 1)
    xt_ref[...] = pixels.astype(F32).T.astype(BF16)


def arrange_call(pixels):
    tokens, width = pixels.shape
    return pallas(
        arrange_kernel,
        out_shape=[
            struct((tokens, width + VARS), BF16),
            struct((width, tokens), BF16),
        ],
        us=3.3,
        mib=40,
        name="arrange",
    )(pixels)


def slot_mask():
    slot = lax.broadcasted_iota(jnp.int32, (VARS, VARS * PIX + VARS), 0)
    column = lax.broadcasted_iota(jnp.int32, (VARS, VARS * PIX + VARS), 1)
    return slot == jnp.where(column < VARS * PIX, column // PIX, column - VARS * PIX)


def mix(weights, pixels_wide):
    tokens = weights.shape[1]
    spread = weights[:, None, :] * pixels_wide
    return jnp.concatenate([low(spread.reshape(VARS * PIX, tokens)), low(weights)], 0)


def pool_kernel(count, x_ref, xt_ref, valid_ref, *refs):
    p_refs, w_refs, o_refs = refs[:count], refs[count : 2 * count], refs[2 * count :]
    tokens, width = x_ref.shape
    pixels = x_ref[...]
    pixels_wide = xt_ref[...].astype(F32).reshape(VARS, PIX, tokens)
    valid = valid_ref[...] > 0
    mask = slot_mask()
    for p_ref, w_ref, o_ref in zip(p_refs, w_refs, o_refs):
        _, depth, cols = p_ref.shape
        extra = Extra(cols, depth)
        rows = p_ref[0, width:].astype(F32)
        table_value = p_ref[0, :width].astype(F32).T.astype(BF16)
        parts = []
        for h in range(extra.heads):
            scores = jnp.zeros((VARS, tokens), F32)
            for part in (2, 1, 0):
                spread = low(jnp.where(mask, extra.term(rows, part, h), 0.0))
                scores = scores + dot(spread, pixels, NT)
            scores = jnp.where(valid, scores, -1e30)
            weights = jnp.exp(scores - jnp.max(scores, 0, keepdims=True))
            weights = weights / jnp.sum(weights, 0, keepdims=True)
            w_ref[h] = weights
            mixed = mix(weights, pixels_wide)
            parts.append(dot(table_value[h * HEAD_DIM : (h + 1) * HEAD_DIM], mixed))
        pooled = jnp.concatenate(parts, 0) if len(parts) > 1 else parts[0]
        o_ref[...] = low(pooled.T + extra.bias(rows, 0))


def slot_of(piece, first, count=1):
    return fixed((count,) + piece.shape[1:], first // count, 0, 0)


def pool_call(pixels, pixels_t, valid, pieces):
    tokens = pixels.shape[0]
    cols = pieces[0].shape[2]
    count = len(pieces)
    weights, pooled = (cols // HEAD_DIM, VARS, tokens), (tokens, cols)
    got = pallas(
        lambda *refs: pool_kernel(count, *refs),
        grid=(1,),
        in_specs=[fixed(pixels.shape), fixed(pixels_t.shape), fixed((VARS, 1))]
        + [slot_of(piece, 4) for piece in pieces],
        out_specs=[fixed(weights)] * count + [fixed(pooled)] * count,
        out_shape=[struct(weights, F32)] * count + [struct(pooled, BF16)] * count,
        us=7,
        mib=40,
        name="pool",
    )(pixels, pixels_t, valid, *pieces)
    return list(zip(got[:count], got[count:]))


def pool_back_kernel(count, first, last, x_ref, xt_ref, g_ref, gt_ref, *refs):
    groups = [refs[i * count : (i + 1) * count] for i in range(4)]
    rest = refs[4 * count :]
    if not first:
        before_ref, rest = rest[0], rest[1:]
    pack_refs, (gx_ref, terms_ref, shift_ref) = rest[:count], rest[count:]
    tokens, full = x_ref.shape
    width = VARS * PIX
    pixels = x_ref[...]
    pixels_wide = xt_ref[...].astype(F32).reshape(VARS, PIX, tokens)
    mask = slot_mask()
    total = jnp.zeros((width, tokens), F32) if first else before_ref[...]
    for index, (v_ref, out_ref, w_ref, p_ref) in enumerate(zip(*groups)):
        _, depth, cols = v_ref.shape
        extra = Extra(cols, depth)
        rows = v_ref[0, full:].astype(F32)
        grads = low(dot(g_ref[...], out_ref[0]))
        shift_ref[index] = jnp.sum(grads.astype(F32), 0, keepdims=True)
        lane = lax.broadcasted_iota(jnp.int32, grads.shape, 1)
        table_value = v_ref[0, :full]
        product = jnp.zeros((full, cols), F32)
        for h in range(extra.heads):
            weights = w_ref[h]
            own = jnp.where(lane // HEAD_DIM == h, grads, 0) if extra.heads > 1 else grads
            grad_mixed = dot(table_value, own, NT)
            grad_wide = grad_mixed[:width].reshape(VARS, PIX, tokens)
            grad_weights = jnp.sum(grad_wide * pixels_wide, 1) + grad_mixed[width:]
            inner = jnp.sum(weights * grad_weights, 0, keepdims=True)
            grad_scores = weights * (grad_weights - inner)
            product = product + dot(mix(weights, pixels_wide), own)
            total = total + (weights[:, None, :] * grad_wide).reshape(width, tokens)
            gs_top = low(grad_scores)
            gs_rest = low(grad_scores - gs_top.astype(F32))
            top, middle = [
                low(jnp.where(mask, extra.term(rows, part, h), 0.0))[:, :width] for part in (0, 1)
            ]
            stacked = jnp.concatenate([top, top, middle], 0)
            total = total + dot(stacked, jnp.concatenate([gs_top, gs_rest, gs_top], 0), TN)
            both = dot(jnp.concatenate([gs_top, gs_rest], 0), pixels)
            by_slot = jnp.where(mask, both[:VARS] + both[VARS:], 0.0)
            terms_ref[index, h : h + 1, :] = jnp.sum(by_slot, 0, keepdims=True)
        pack_ref = pack_refs[index]
        pack_ref[0] = low(dot(gt_ref[...], p_ref[...]))
        pack_ref[1, :full] = low(product)
        pack_ref[1, full:] = jnp.zeros((depth - full, cols), BF16)
    gx_ref[...] = low(total.T) if last else total


def pool_back_call(pixels, pixels_t, heads, pieces, grads, grads_t, before, last):
    count = len(pieces)
    tokens, full = pixels.shape
    width = pixels_t.shape[0]
    _, depth, cols = pieces[0].shape
    in_specs = [fixed(array.shape) for array in (pixels, pixels_t, grads, grads_t)]
    in_specs += [slot_of(piece, 4) for piece in pieces] + [slot_of(piece, 3) for piece in pieces]
    in_specs += [fixed(head[0].shape) for head in heads] + [fixed(head[1].shape) for head in heads]
    operands = [pixels, pixels_t, grads, grads_t, *pieces, *pieces]
    operands += [head[0] for head in heads] + [head[1] for head in heads]
    if before is not None:
        in_specs.append(fixed((width, tokens)))
        operands.append(before)
    shapes = [struct((2, depth, cols), BF16)] * count
    shapes.append(struct((tokens, width), BF16) if last else struct((width, tokens), F32))
    shapes.append(struct((count, cols // HEAD_DIM, full), F32))
    shapes.append(struct((count, 1, cols), F32))
    got = pallas(
        lambda *refs: pool_back_kernel(count, before is None, last, *refs),
        grid=(1,),
        in_specs=in_specs,
        out_specs=[fixed(shape.shape) for shape in shapes],
        out_shape=shapes,
        us=21,
        name="pool_back",
    )(*operands)
    return list(got[:count]), *got[count:]


def normalise(stream):
    centered = stream - jnp.mean(stream, -1, keepdims=True)
    scale = lax.rsqrt(jnp.mean(centered * centered, -1, keepdims=True) + 1e-05)
    return centered * scale, scale


def normalise_back(grad, stream, gain):
    hat, scale = normalise(stream)
    through = grad * gain
    inner = through - jnp.mean(through, -1, keepdims=True)
    inner = inner - hat * jnp.mean(through * hat, -1, keepdims=True)
    add = lambda tensor: jnp.sum(tensor, 0, keepdims=True)
    return scale * inner, add(grad * hat), add(grad)


def enter_kernel(count, *refs):
    p_refs, w_refs = refs[:count], refs[count : 2 * count]
    bias_ref, gain_ref, shift_ref, s_ref, x_ref, xt_ref = refs[2 * count :]
    stream = jnp.zeros(s_ref.shape, F32) + bias_ref[...]
    for p_ref, w_ref in zip(p_refs, w_refs):
        stream = stream + dot(p_ref[...], w_ref[0], NT)
    s_ref[...] = stream
    hat, _ = normalise(stream)
    rows = hat * gain_ref[...] + shift_ref[...]
    x_ref[...] = low(rows)
    xt_ref[...] = low(rows.T)


def enter_call(pooled, pieces, bias, gain, shift):
    tokens = pooled[0].shape[0]
    depth = pieces[0].shape[1]
    row = fixed((1, depth))
    return pallas(
        lambda *refs: enter_kernel(len(pieces), *refs),
        grid=(1,),
        in_specs=[fixed(part.shape) for part in pooled]
        + [slot_of(piece, 3) for piece in pieces]
        + [row, row, row],
        out_specs=[fixed((tokens, depth)), fixed((tokens, depth)), fixed((depth, tokens))],
        out_shape=[
            struct((tokens, depth), F32),
            struct((tokens, depth), BF16),
            struct((depth, tokens), BF16),
        ],
        us=7,
        mib=40,
        name="enter",
    )(*pooled, *pieces, bias, gain, shift)


def beside(ref):
    return jnp.concatenate([ref[i] for i in range(3)], 1)


def project_kernel(count, x_ref, *refs):
    w_refs, e_refs, q_refs = refs[:count], refs[count : 2 * count], refs[2 * count : -1]
    kv_ref = refs[-1]
    for index, (w_ref, e_ref) in enumerate(zip(w_refs, e_refs)):
        _, depth, cols = w_ref.shape
        extra = Extra(cols, depth)
        rows = e_ref[0, extra.full :].astype(F32)
        triple = dot(x_ref[...], beside(w_ref))
        q_refs[index // 2][index % 2] = low(triple[:, :cols] + extra.bias(rows, 1))
        kv_ref[index, 0] = low(triple[:, cols : 2 * cols])
        kv_ref[index, 1] = low(triple[:, 2 * cols :] + extra.bias(rows, 2))


def project_call(rows, pieces):
    count = len(pieces)
    cols = pieces[0].shape[2]
    tokens = rows.shape[0]
    shapes = [struct((2, tokens, cols), BF16)] * (count // 2)
    shapes.append(struct((count, 2, tokens, cols), BF16))
    got = pallas(
        lambda *refs: project_kernel(count, *refs),
        grid=(1,),
        in_specs=[fixed(rows.shape)]
        + [slot_of(piece, 0, 3) for piece in pieces]
        + [slot_of(piece, 4) for piece in pieces],
        out_specs=[fixed(shape.shape) for shape in shapes],
        out_shape=shapes,
        us=1.2 * count,
        mib=40,
        name="project",
    )(rows, *pieces, *pieces)
    return got[:-1], got[-1]


def project_back_kernel(count, first, xt_ref, gq_ref, gkv_ref, *refs):
    w_refs, rest = refs[:count], refs[2 * count :]
    if not first:
        before_ref, rest = rest[0], rest[1:]
    gw_refs, (gx_ref, sums_ref) = rest[:count], rest[count:]
    cols = gq_ref.shape[2]
    total = jnp.zeros(gx_ref.shape, F32) if first else before_ref[...]
    for index, (w_ref, gw_ref) in enumerate(zip(w_refs, gw_refs)):
        grads = jnp.concatenate([gq_ref[index], gkv_ref[index, 0], gkv_ref[index, 1]], 1)
        total = total + dot(grads, beside(w_ref), NT)
        products = low(dot(xt_ref[...], grads))
        for i in range(3):
            gw_ref[i] = products[:, i * cols : (i + 1) * cols]
        sums_ref[index] = jnp.sum(grads.astype(F32), 0, keepdims=True)
    gx_ref[...] = total


def project_back_call(rows_t, pieces, grad_query, grad_pair, grad_pieces, before):
    count = len(pieces)
    depth, tokens = rows_t.shape
    cols = pieces[0].shape[2]
    in_specs = [fixed(array.shape) for array in (rows_t, grad_query, grad_pair)]
    in_specs += [slot_of(piece, 0, 3) for piece in pieces] + [anywhere()] * count
    operands = [rows_t, grad_query, grad_pair, *pieces, *grad_pieces]
    if before is not None:
        in_specs.append(fixed((tokens, depth)))
        operands.append(before)
    shapes = [struct(piece.shape, BF16) for piece in grad_pieces]
    shapes += [struct((tokens, depth), F32), struct((count, 1, 3 * cols), F32)]
    got = pallas(
        lambda *refs: project_back_kernel(count, before is None, *refs),
        grid=(1,),
        in_specs=in_specs,
        out_specs=[slot_of(piece, 0, 3) for piece in grad_pieces]
        + [fixed(shape.shape) for shape in shapes[count:]],
        out_shape=shapes,
        input_output_aliases={3 + count + i: i for i in range(count)},
        us=13.6,
        name="project_back",
    )(*operands)
    return list(got[:count]), *got[count:]


def leave_kernel(g_ref, s_ref, before_ref, gain_ref, o_ref, ot_ref, sums_ref):
    through, gain, shift = normalise_back(g_ref[...], s_ref[...], gain_ref[...])
    total = before_ref[...] + through
    rounded = low(total)
    o_ref[...] = rounded
    ot_ref[...] = low(total.T)
    bias = jnp.sum(rounded.astype(F32), 0, keepdims=True)
    sums_ref[...] = jnp.concatenate([gain, shift, bias], 0)


def leave_call(grad_normed, stream, before, gain):
    tokens, depth = stream.shape
    return pallas(
        leave_kernel,
        out_shape=[
            struct((tokens, depth), BF16),
            struct((depth, tokens), BF16),
            struct((3, depth), F32),
        ],
        us=12,
        name="leave",
    )(grad_normed, stream, before, gain)


def attend_kernel(count, q_ref, *refs):
    sources, (o_ref, total_ref) = refs[:count], refs[count:]
    cols = q_ref.shape[2]
    heads = cols // HEAD_DIM
    scaled = q_ref[0] * SCALE
    lane = lax.broadcasted_iota(jnp.int32, scaled.shape, 1)
    values_t = [source[0, 1].T for source in sources]
    parts = []
    for h in range(heads):
        own = jnp.where(lane // HEAD_DIM == h, scaled, 0) if heads > 1 else scaled
        logits = [dot(source[0, 0], own, NT) for source in sources]
        peak = jnp.max(logits[0], 0, keepdims=True)
        for piece in logits[1:]:
            peak = jnp.maximum(peak, jnp.max(piece, 0, keepdims=True))
        norm = jnp.zeros_like(peak)
        out = jnp.zeros((HEAD_DIM, peak.shape[1]), F32)
        for piece, value in zip(logits, values_t):
            weight = jnp.exp(piece - peak)
            norm = norm + jnp.sum(weight, 0, keepdims=True)
            out = out + dot(value[h * HEAD_DIM : (h + 1) * HEAD_DIM], low(weight))
        parts.append(out / norm)
        total_ref[0, h] = peak + jnp.log(norm)
    full = jnp.concatenate(parts, 0) if heads > 1 else parts[0]
    o_ref[0] = full.T


def pair_spec(shape, flip, start=0):
    place = lambda n: (start + (1 - n if flip else n),) + (0,) * len(shape)
    return pl.BlockSpec((1,) + shape, place)


def attend_call(queries, sources, flips, start):
    count, tokens, cols = queries.shape
    heads = cols // HEAD_DIM
    keys = sum(array.shape[2] for array in sources)
    work = count * tokens * keys * cols
    return pallas(
        lambda *refs: attend_kernel(len(sources), *refs),
        grid=(count,),
        in_specs=[per_block((tokens, cols))]
        + [pair_spec(array.shape[1:], flip, start) for array, flip in zip(sources, flips)],
        out_specs=[per_block((tokens, cols)), per_block((heads, 1, tokens))],
        out_shape=[
            struct((count, tokens, cols), F32),
            struct((count, heads, 1, tokens), F32),
        ],
        us=8.7,
        name="attend",
    )(queries, *sources)


def middle_kernel(count, s_ref, *refs):
    o_refs, w_refs = refs[:count], refs[count : 3 * count]
    bias_ref, gain_ref, shift_ref, s1_ref, x_ref, xt_ref = refs[3 * count :]
    stream = s_ref[...] + bias_ref[...]
    for index, w_ref in enumerate(w_refs):
        stream = stream + dot(low(o_refs[index // 2][index % 2]), w_ref[...])
    s1_ref[...] = stream
    hat, _ = normalise(stream)
    rows = hat * gain_ref[...] + shift_ref[...]
    x_ref[...] = low(rows)
    xt_ref[...] = low(rows.T)


def middle_call(stream, attended, weights, bias, gain, shift):
    tokens, depth = stream.shape
    operands = [stream, *attended, *weights, bias, gain, shift]
    shapes = [
        struct((tokens, depth), F32),
        struct((tokens, depth), BF16),
        struct((depth, tokens), BF16),
    ]
    return pallas(
        lambda *refs: middle_kernel(len(attended), *refs),
        grid=(1,),
        in_specs=[fixed(array.shape) for array in operands],
        out_specs=[fixed(shape.shape) for shape in shapes],
        out_shape=shapes,
        us=5,
        mib=40,
        name="middle",
    )(*operands)


def middle_back_kernel(g_ref, gt_ref, o_ref, wa_ref, wb_ref, go_ref, delta_ref, ga_ref, gb_ref):
    _, tokens, cols = o_ref.shape
    heads = cols // HEAD_DIM
    lane = lax.broadcasted_iota(jnp.int32, (8, cols), 1)
    row = lax.broadcasted_iota(jnp.int32, (8, cols), 0)
    mask = jnp.where(lane // HEAD_DIM == row, 1.0, 0.0)
    for index, (w_ref, gw_ref) in enumerate(((wa_ref, ga_ref), (wb_ref, gb_ref))):
        grads = low(dot(g_ref[...], w_ref[...], NT))
        go_ref[index] = grads
        attended = o_ref[index]
        gw_ref[0] = low(dot(gt_ref[...], low(attended)))
        sums = dot(mask, grads.astype(F32) * attended, NT, precision=highest)
        for h in range(heads):
            delta_ref[index, h] = sums[h : h + 1]


def middle_back_call(grads, grads_t, attended, weights):
    count, tokens, cols = attended.shape
    depth = grads.shape[1]
    heads = cols // HEAD_DIM
    piece = struct((4, depth, cols), BF16)
    operands = [grads, grads_t, attended, *weights]
    return pallas(
        middle_back_kernel,
        grid=(1,),
        in_specs=[fixed(array.shape) for array in operands],
        out_specs=[fixed(attended.shape), fixed((count, heads, 1, tokens))]
        + [slot_of(piece, 3)] * 2,
        out_shape=[
            struct(attended.shape, BF16),
            struct((count, heads, 1, tokens), F32),
            piece,
            piece,
        ],
        us=4,
        name="middle_back",
    )(*operands)


def attend_back_kernel(count, first, last, together, q_ref, g_ref, total_ref, delta_ref, *refs):
    sources, rest = refs[:count], refs[count:]
    before_ref, gq_ref, targets = (
        (None, rest[0], rest[1:]) if first else (rest[0], rest[1], rest[2:])
    )
    if together:
        targets = [targets[0].at[i] for i in range(count)]
    cols = q_ref.shape[2]
    heads = cols // HEAD_DIM
    scaled = q_ref[0] * SCALE
    grads = g_ref[0]
    lane = lax.broadcasted_iota(jnp.int32, scaled.shape, 1)
    pick = lambda tensor, h: jnp.where(lane // HEAD_DIM == h, tensor, 0) if heads > 1 else tensor
    own_q = [pick(scaled, h) for h in range(heads)]
    own_g = [pick(grads, h) for h in range(heads)]
    queries_t = [jnp.zeros((HEAD_DIM, scaled.shape[0]), F32) for h in range(heads)]
    for source, target in zip(sources, targets):
        keys, values = source[0, 0], source[0, 1]
        keys_t = keys.T
        grad_keys = jnp.zeros(keys.shape, F32)
        grad_values = jnp.zeros(keys.shape, F32)
        for h in range(heads):
            weight = jnp.exp(dot(keys, own_q[h], NT) - total_ref[0, h])
            grad_weight = dot(values, own_g[h], NT)
            grad_logit = low(weight * (grad_weight - delta_ref[0, h]))
            grad_values = grad_values + dot(low(weight), own_g[h])
            grad_keys = grad_keys + dot(grad_logit, own_q[h])
            queries_t[h] = queries_t[h] + dot(
                keys_t[h * HEAD_DIM : (h + 1) * HEAD_DIM], grad_logit
            )
        target[0, 0] = low(grad_keys)
        target[0, 1] = low(grad_values)
    full = jnp.concatenate(queries_t, 0) if heads > 1 else queries_t[0]
    if before_ref is not None:
        full = full + before_ref[0]
    gq_ref[0] = low(full * SCALE).T if last else full


def attend_back_call(queries, grads, totals, deltas, sources, flips, start, before, last, together):
    count, tokens, cols = queries.shape
    heads = cols // HEAD_DIM
    keys = sum(array.shape[2] for array in sources)
    work = count * tokens * keys * cols
    block = sources[0].shape[1:]
    first = before is None
    outs = [pair_spec(block, flip) for flip in flips]
    shapes = [struct((count,) + block, BF16) for _ in sources]
    if together:
        flip = flips[0]
        place = lambda n: (0, 1 - n if flip else n) + (0,) * len(block)
        outs = [pl.BlockSpec((len(sources), 1) + block, place)]
        shapes = [struct((len(sources), count) + block, BF16)]
    result = struct((count, tokens, cols), BF16) if last else struct((count, cols, tokens), F32)
    return pallas(
        lambda *refs: attend_back_kernel(len(sources), first, last, together, *refs),
        grid=(count,),
        in_specs=[
            per_block((tokens, cols)),
            per_block((tokens, cols)),
            per_block((heads, 1, tokens)),
            per_block((heads, 1, tokens)),
        ]
        + [pair_spec(block, flip, start) for flip in flips]
        + ([] if first else [per_block((cols, tokens))]),
        out_specs=[per_block(result.shape[1:])] + outs,
        out_shape=[result] + shapes,
        us=15.2,
        name="attend_back",
    )(queries, grads, totals, deltas, *sources, *([] if first else [before]))


def feed_kernel(first, cols, x_ref, g_ref, w_ref, *refs):
    if not first:
        before_ref, refs = refs[0], refs[1:]
    y_ref, gx_ref, gb_ref, gw_ref, y_sum, gx_sum = refs
    hidden = (w_ref.shape[1] - 16 - cols) // 2
    step = pl.program_id(0)

    @pl.when(step == 0)
    def _():
        y_sum[...] = jnp.zeros_like(y_sum)
        gx_sum[...] = jnp.zeros_like(gx_sum)

    rows_of = lambda start: jnp.concatenate([w_ref[i, start : start + hidden] for i in range(2)], 0)
    up, down = rows_of(cols), rows_of(cols + hidden)
    bias = []
    for i in range(2):
        rows = w_ref[i, cols + 2 * hidden :, :hidden].astype(F32)
        bias.append(rows[0:1] + (rows[1:2] + rows[2:3]))
    rows, grads = x_ref[...], g_ref[...]
    before = dot(rows, up, NT) + jnp.concatenate(bias, 1)
    bell = 0.5 * (1.0 + lax.erf(before * 0.7071067811865476))
    active = low(before * bell)
    slope = bell + before * (0.3989422804014327 * jnp.exp(-0.5 * before * before))
    grad_hidden = low(slope * dot(grads, down, NT))
    y_sum[...] += dot(active, down)
    gx_sum[...] += dot(grad_hidden, up)
    grad_up = dot(grad_hidden, rows, TN)
    grad_down = dot(active, grads, TN)
    gb_ref[0] = jnp.sum(grad_hidden.astype(F32), 0, keepdims=True)
    for i in range(2):
        part = slice(i * hidden, (i + 1) * hidden)
        made = jnp.concatenate([grad_up[part], grad_down[part]], 0)
        made = made if first else made + before_ref[i].astype(F32)
        gw_ref[i] = low(made)

    @pl.when(step == pl.num_programs(0) - 1)
    def _():
        y_ref[...] = low(y_sum[...])
        gx_ref[...] = low(gx_sum[...])


def feed_call(cols, rows, grads, staged, before):
    count, lines, depth = staged.shape
    tokens = rows.shape[0]
    lines = lines - 16 - cols
    whole = fixed((tokens, depth))
    pair = pl.BlockSpec((2, lines, depth), lambda n: (n, 0, 0))
    first = before is None
    return pallas(
        lambda *refs: feed_kernel(first, cols, *refs),
        grid=(count // 2,),
        in_specs=[whole, whole, pl.BlockSpec((2,) + staged.shape[1:], lambda n: (n, 0, 0))]
        + ([] if first else [pair]),
        out_specs=[whole, whole, pl.BlockSpec((1, 1, lines), lambda n: (n, 0, 0)), pair],
        out_shape=[
            struct((tokens, depth), BF16),
            struct((tokens, depth), BF16),
            struct((count // 2, 1, lines), F32),
            struct((count, lines, depth), BF16),
        ],
        scratch_shapes=[pltpu.VMEM((tokens, depth), F32), pltpu.VMEM((tokens, depth), F32)],
        us=11,
        mib=40,
        name="feed",
    )(rows, grads, staged, *([] if first else [before]))


def turn_kernel(count, *refs):
    g_ref, s_ref, gain_ref, gs_ref, g1_ref, g1t_ref, sums_ref = refs[count:]
    grad = refs[0][...].astype(F32)
    for ref in refs[1:count]:
        grad = grad + ref[...].astype(F32)
    through, gain, shift = normalise_back(grad, s_ref[...], gain_ref[...])
    grads = g_ref[...].astype(F32)
    total = grads + through
    gs_ref[...] = total
    rounded = low(total)
    g1_ref[...] = rounded
    g1t_ref[...] = low(total.T)
    add = lambda tensor: jnp.sum(tensor, 0, keepdims=True)
    sums_ref[...] = jnp.concatenate([gain, shift, add(grads), add(rounded.astype(F32))], 0)


def turn_call(parts, grads, stream, gain):
    tokens, depth = stream.shape
    return pallas(
        lambda *refs: turn_kernel(len(parts), *refs),
        out_shape=[
            struct((tokens, depth), F32),
            struct((tokens, depth), BF16),
            struct((depth, tokens), BF16),
            struct((4, depth), F32),
        ],
        us=8,
        name="turn",
    )(*parts, grads, stream, gain)


def assemble_kernel(w_ref, *refs):
    pieces, (up_ref, down_ref) = refs[:-2], refs[-2:]
    hidden = pieces[0].shape[0] // 2
    for index, piece in enumerate(pieces):

        @pl.when(pl.program_id(0) == index)
        def _():
            up_ref[...] = piece[:hidden].astype(F32).T
            down_ref[...] = piece[hidden:].astype(F32)


def assemble_call(w, pieces):
    count = len(pieces)
    lines, depth = pieces[0].shape
    hidden = lines // 2
    direct = hidden % 128 == 0
    up_place = (
        (lambda i, w_ref: (0, w_ref[0] ^ i)) if direct else (lambda i, w_ref: (w_ref[0] ^ i, 0))
    )
    up, down = pallas(
        assemble_kernel,
        prefetch=1,
        grid=(count,),
        in_specs=[pl.BlockSpec((lines, depth), lambda i, w_ref: (0, 0)) for _ in pieces],
        out_specs=[
            pl.BlockSpec((depth, hidden), up_place),
            pl.BlockSpec((hidden, depth), lambda i, w_ref: (w_ref[0] ^ i, 0)),
        ],
        out_shape=[
            struct((depth, count * hidden) if direct else (count * depth, hidden), F32),
            struct((count * hidden, depth), F32),
        ],
        us=3.3,
        name="assemble",
    )(w.reshape(1), *pieces)
    if not direct:
        up = up.reshape(count, depth, hidden).transpose(1, 0, 2).reshape(depth, count * hidden)
    return up, down


def table_kernel(count, order_ref, terms_ref, v_ref, *refs):
    p_refs, e_refs = refs[:count], refs[count : 2 * count]
    patch_ref, slot_ref = refs[2 * count :]
    depth = patch_ref.shape[1]
    cols = p_refs[0].shape[1]
    extra = Extra(cols, depth)
    folded = []
    total = jnp.zeros((extra.full, depth), F32)
    for index, (p_ref, e_ref) in enumerate(zip(p_refs, e_refs)):
        rows = e_ref[0, extra.full :].astype(F32)
        folded += [extra.folded(rows, h) for h in range(extra.heads)]
        total = total + dot(p_ref[...], v_ref[order_ref[index]])
    total = total + dot(terms_ref[...], jnp.concatenate(folded, 0), TN, precision=highest)
    width = patch_ref.shape[0]
    patch_ref[...] = total[:width]
    slot_ref[...] = total[width:]


def table_call(order, terms, values, products, pieces):
    _, depth, cols = pieces[0].shape
    width = VARS * PIX
    return pallas(
        lambda *refs: table_kernel(len(pieces), *refs),
        prefetch=1,
        grid=(1,),
        in_specs=[fixed(terms.shape), fixed((values.shape[0], cols, depth))]
        + [fixed(part.shape) for part in products]
        + [slot_of(piece, 4) for piece in pieces],
        out_specs=[fixed((width, depth)), fixed((VARS, depth))],
        out_shape=[struct((width, depth), F32), struct((VARS, depth), F32)],
        us=9,
        name="table_back",
    )(order, terms, values, *products, *pieces)


def on_device(
    wide_size,
    narrow_size,
    variables,
    valid_slots,
    out_grad,
    patch_embed,
    variable_embed,
    pool_query,
    pool_key,
    pool_value,
    value_shift,
    pool_output,
    pool_bias,
    first_gain,
    first_shift,
    self_weights,
    query_bias,
    value_bias,
    self_output,
    output_bias,
    second_gain,
    second_shift,
    feed_up,
    up_bias,
    feed_down,
    down_bias,
):
    samples, token_count, input_width = variables.shape
    model_width = patch_embed.shape[1]
    local_dim = pool_query.shape[0]
    heads = local_dim // HEAD_DIM
    hidden = up_bias.shape[0]
    shares = narrow_size // samples
    permuted = wide_size == 4 and shares == 1
    ring = Ring(wide_size, narrow_size, not permuted)
    tokens = token_count // shares
    groups = narrow_size // 2
    row = lambda vector: vector.reshape(1, -1)
    pair_of = lambda pieces, g: pieces[2 * g : 2 * g + 2]
    place = (ring.n // shares, (ring.n % shares) * tokens, 0)
    pixels = lax.dynamic_slice(variables, place, (1, tokens, input_width))[0]
    grads = lax.dynamic_slice(out_grad, place, (1, tokens, model_width))[0]
    valid = lax.dynamic_index_in_dim(valid_slots, ring.n // shares, 0, keepdims=False)
    valid = valid.reshape(VARS, 1)

    filler = jnp.zeros((model_width - input_width - VARS, model_width), BF16)
    table_full = jnp.concatenate([patch_embed, variable_embed, filler], 0)
    gather = GatherShared(
        ring,
        prepare_call(
            pool_key,
            row(pool_query),
            table_full,
            pool_value,
            pool_output,
            self_weights.transpose(1, 0, 2),
            row(jnp.concatenate([value_shift, query_bias, value_bias])),
        ),
    )
    pixels_one, pixels_t = arrange_call(pixels)
    all_grads = ring.gather_wide(grads)
    quarter = hidden // wide_size
    cut_out = lambda tensor, axis: lax.dynamic_slice_in_dim(tensor, ring.w * quarter, quarter, axis)
    feed_own = stage_call(
        cut_out(feed_up, 1), cut_out(feed_down, 0), pool_value, row(cut_out(up_bias, 0))
    )
    pool = lambda pieces: pool_call(pixels_one, pixels_t, valid, pieces)
    wait_for(feed_own)
    pooled = pool([gather.own])
    for g in range(1, groups):
        got = list(gather.step())
        wait_for(pooled[-1][1])
        if g == 2:
            wait_for(*all_grads)
        pooled += pool(got)
    gather.step()
    wait_for(pooled[-1][1])
    hand_on(feed_own, self_output)
    far = pool([gather.far])
    feed_all = lax.all_gather(Gate.handed[0], "narrow")
    gather_mixer = GatherShared(ring, Gate.handed[1])
    pooled = [pooled[0], far[0]] + pooled[1:]
    pieces = gather.finish()
    stream_zero, normed_one, normed_one_t = enter_call(
        [head[1] for head in pooled], pieces, row(pool_bias), row(first_gain), row(first_shift)
    )

    subsets = [[s * shares + i for i in range(shares)] for s in range(samples)]
    chunks = [[g] for g in range(groups)]
    gather_mixer.step(stream_zero)
    queries, sources, flips, starts = [], [], [], []
    for chunk in chunks:
        if queries:
            wait_for(queries[-1])
        mine, pair = project_call(normed_one, pieces[2 * chunk[0] : 2 * chunk[-1] + 2])
        queries += mine
        if permuted:
            across = ring.swap(pair, 2)
            got = [pair, ring.swap(pair, 1), across, ring.swap(across, 1)]
        else:
            full = lax.all_gather(pair, "wide", axis=2, tiled=True)
            if shares > 1:
                full = lax.all_gather(
                    full, "narrow", axis=2, tiled=True, axis_index_groups=subsets
                )
            got = [full]
        for g in chunk:
            sources.append(got)
            flips.append([False, g > 0, False, g > 0] if permuted else [False])
            starts.append(2 * (g - chunk[0]))
    gather_mixer.step(queries[-1])
    attended, totals = [], []
    for g in range(groups):
        if attended:
            wait_for(attended[-1])
        got = attend_call(queries[g], sources[g], flips[g], starts[g])
        attended.append(got[0])
        totals.append(got[1])
        if g < 2:
            gather_mixer.step(got[0])
    self_pieces = gather_mixer.finish()
    order = jnp.stack(ring.places()).astype(jnp.int32)
    stream_one, normed_two, _ = middle_call(
        stream_zero, attended, self_pieces, row(output_bias), row(second_gain), row(second_shift)
    )

    all_rows = ring.gather_wide(normed_two)
    y_all, gx_all, gb_all, grad_feed = [], [], [], None
    for index in range(wide_size):
        if grad_feed is not None:
            wait_for(gx_all[-1])
        got = feed_call(
            local_dim, all_rows[index], all_grads[index], feed_all, grad_feed
        )
        y_all.append(got[0])
        gx_all.append(got[1])
        gb_all.append(got[2])
        grad_feed = got[3]
    scatter_feed = ScatterOwn(ring, grad_feed)
    grad_parts = ring.scatter_wide(gx_all)
    wait_for(grad_parts[0])
    for _ in range(narrow_size // 2 - 2):
        scatter_feed.step()
    y_parts = ring.scatter_wide(pass_on(y_all, grad_parts[1]))
    grad_up_bias = sum(gb_all).reshape(narrow_size, quarter)
    wait_for(scatter_feed.ahead)
    grad_stream_one, grad_one, grad_one_t, sums_two = turn_call(
        grad_parts, grads, stream_one, row(second_gain)
    )
    block_own = low(stream_one + down_bias + (y_parts[0].astype(F32) + y_parts[1].astype(F32)))
    gather_out = GatherOwn(ring, block_own, BF16)

    waiting = {}
    backward = [0] + list(range(groups - 1, 0, -1))
    for turn, g in enumerate(backward):
        if turn == 1:
            wait_for(block_own)
        back = lambda: middle_back_call(
            grad_one, grad_one_t, attended[g], pair_of(self_pieces, g)
        )
        got = gather_out.beside(back) if turn in (2, 3) else back()
        grad_attended, deltas, *grad_pair_mixers = got
        back = lambda chosen, before, last, together: attend_back_call(
            queries[g],
            grad_attended,
            totals[g],
            deltas,
            [sources[g][i] for i in chosen],
            [flips[g][i] for i in chosen],
            starts[g],
            before,
            last,
            together,
        )
        if permuted:
            some, crossing = back([1, 3], None, False, True)
            crossed = ring.swap(crossing)
            grad_query, grad_own, grad_across = back([0, 2], some, True, False)
            far = add_up(grad_across, (crossed, 1))
            grad_pair = [grad_own, (crossed, 0), ring.swap(far, 2)]
        else:
            grad_query, full = back([0], None, True, False)
            if shares > 1:
                full = lax.psum_scatter(
                    full, "narrow", scatter_dimension=2, tiled=True, axis_index_groups=subsets
                )
            far = lax.psum_scatter(full, "wide", scatter_dimension=2, tiled=True)
            grad_pair = [far]
        waiting[g] = (grad_query, grad_pair, grad_pair_mixers)
        wait_for(far)
        if turn < 2:
            wait_for(scatter_feed.step())
    grad_normed_one, grad_pieces, sums_triple = None, {}, [None] * groups
    for turn, g in enumerate(backward):
        grad_query, grad_pair, grad_pair_mixers = waiting[g]
        if grad_normed_one is not None:
            wait_for(grad_normed_one)
        grad_pair = add_up(*grad_pair)
        back = lambda: project_back_call(
            normed_one_t,
            pair_of(pieces, g),
            grad_query,
            grad_pair,
            grad_pair_mixers,
            grad_normed_one,
        )
        made, grad_normed_one, sums = gather_out.beside(back) if turn in (0, 3) else back()
        grad_pieces[g], sums_triple[g] = made, sums
    scatter = ScatterShared(ring, *grad_pieces[0])
    grad_zero, grad_zero_t, sums_one = leave_call(
        grad_normed_one, stream_zero, grad_stream_one, row(first_gain)
    )

    grad_pixels, grad_terms, grad_shifts = None, [None] * groups, [None] * groups
    for turn, g in enumerate(backward):
        if turn > 1:
            wait_for(grad_pixels)
            added = scatter.step(grad_pieces[backward[turn - 1]])
            wait_for(added)
            wait_for(scatter_last.step(made))
        back = lambda: pool_back_call(
            pixels_one,
            pixels_t,
            pair_of(pooled, g),
            pair_of(pieces, g),
            grad_zero,
            grad_zero_t,
            grad_pixels,
            turn == groups - 1,
        )
        made, grad_pixels, terms, shifts = back()
        if turn == 0:
            scatter_last = ScatterShared(ring, *made)
        grad_terms[g], grad_shifts[g] = terms, shifts

    def sort_into(places, tensor, back=False):
        same = jnp.stack([jnp.stack([p == i for p in places]) for i in range(narrow_size)])
        same = same.T if back else same
        return jnp.sum(jnp.where(same[:, :, None], tensor[None], 0.0), 1)

    places = ring.places()
    sums_triple = jnp.concatenate(sums_triple, 0).reshape(narrow_size, -1)
    up_bias_row = lax.dynamic_update_slice(
        jnp.zeros((narrow_size, hidden), F32),
        grad_up_bias,
        (0, ring.w * quarter),
    )
    own_sums = jnp.concatenate(
        [
            jnp.concatenate(grad_shifts, 0).reshape(narrow_size, -1),
            sums_triple[:, :local_dim],
            sums_triple[:, 2 * local_dim :],
            jnp.concatenate(grad_terms, 0).reshape(narrow_size, -1),
        ],
        1,
    )
    own_sums = jnp.concatenate([up_bias_row, sort_into(places, own_sums)], 1)
    own_length = own_sums.shape[1]
    shared_sums = jnp.concatenate([sums_one, sums_two], 0)
    all_sums = jnp.concatenate([own_sums.reshape(-1), shared_sums.reshape(-1)]).reshape(-1, 128)
    scatter_last.step(made)
    hand_on(grad_pixels)
    scatter_last.step()
    gather_pixels = GatherOwn(ring, Gate.handed[0], F32)
    finish_last = FinishShared(ring, scatter_last.current)
    finish_last.step()
    finish_last.step()
    grad_pool_output, product = finish_last.finish()
    product = low(product[0, : input_width + VARS])
    gather_product = GatherShared(ring, product)
    adder = AddEverywhere(ring, *pass_on([all_sums], product))
    adder.step()
    block_out = gather_out.finish().reshape(samples, token_count, model_width)
    gather_pixels.after(product)
    wait_for(product)
    scatter.step(grad_pieces[backward[-1]])
    adder.step()
    hop = gather_product.step()[0]
    gather_pixels.after(hop)
    wait_for(hop)
    scatter.step()
    finish = FinishShared(ring, scatter.current)
    hop = gather_product.step()[0]
    gather_pixels.after(hop)
    wait_for(hop)
    finish.step()
    finish.step()
    products = gather_product.finish()
    grad_feed_pieces = ring.gather_wide(scatter_feed.ahead)
    grad_feed_up, grad_feed_down = assemble_call(ring.w, grad_feed_pieces)
    grad_first, grad_second = finish.finish()
    adder.finish()
    grad_variables = gather_pixels.finish().reshape(samples, token_count, input_width)
    grad_triple = jnp.concatenate([grad_first, grad_second[:1]], 0).transpose(1, 0, 2)
    grad_self_output = grad_second[1].T
    grad_pool_output = grad_pool_output[0].T
    grad_pool_value = dot(patch_embed, product[:input_width], TN)
    grad_pool_value = grad_pool_value + dot(variable_embed, product[input_width:], TN)

    summed = adder.current.reshape(-1)
    own_all = summed[: narrow_size * own_length].reshape(narrow_size, own_length)
    shared_all = summed[narrow_size * own_length :].reshape(-1, model_width)
    grad_first_gain, grad_first_shift, grad_pool_bias = shared_all[:3]
    grad_second_gain, grad_second_shift, grad_down_bias, grad_output_bias = shared_all[3:]
    own = lax.dynamic_index_in_dim(own_all, ring.n, 0, keepdims=False)
    grad_up_bias = own[:hidden]
    grad_value_shift, grad_query_bias, grad_value_bias = own[hidden : hidden + 3 * local_dim].reshape(
        3, local_dim
    )
    terms_start = 3 * local_dim + hidden
    grad_proj = SCALE * own[terms_start:].reshape(heads, -1)
    grad_folded = dot(grad_proj[:, :input_width], patch_embed.astype(F32), precision=highest)
    grad_folded = grad_folded + dot(
        grad_proj[:, input_width:], variable_embed.astype(F32), precision=highest
    )
    query_heads = pool_query.reshape(heads, HEAD_DIM)
    key_heads = pool_key.astype(F32).reshape(model_width, heads, HEAD_DIM)
    grad_pool_key = (grad_folded.T[:, :, None] * query_heads).reshape(model_width, local_dim)
    grad_pool_query = jnp.einsum("dhe,hd->he", key_heads, grad_folded, precision=highest).reshape(
        local_dim
    )
    grad_terms = SCALE * sort_into(places, own_all[:, terms_start:], True)
    grad_patch, grad_slot = table_call(
        order,
        grad_terms.reshape(narrow_size * heads, -1),
        feed_all,
        products,
        pieces,
    )
    return (
        block_out,
        grad_variables,
        grad_patch,
        grad_slot,
        grad_pool_query,
        grad_pool_key,
        grad_pool_value,
        grad_value_shift,
        grad_pool_output,
        grad_pool_bias,
        grad_first_gain,
        grad_first_shift,
        grad_triple,
        grad_query_bias,
        grad_value_bias,
        grad_self_output,
        grad_output_bias,
        grad_second_gain,
        grad_second_shift,
        grad_feed_up,
        grad_up_bias,
        grad_feed_down,
        grad_down_bias,
    )


def solution(mesh):
    wide_size, narrow_size = mesh.shape["wide"], mesh.shape["narrow"]

    def body(*arrays):
        return on_device(wide_size, narrow_size, *arrays)

    return jax.shard_map(
        body,
        mesh=mesh,
        in_specs=(
            P(None, "wide", None),
            P(),
            P(None, "wide", None),
            P(),
            P(),
            P("narrow"),
            P(None, "narrow"),
            P(None, "narrow"),
            P("narrow"),
            P("narrow", None),
            P(),
            P(),
            P(),
            P(None, None, "narrow"),
            P("narrow"),
            P("narrow"),
            P("narrow", None),
            P(),
            P(),
            P(),
            P(None, "narrow"),
            P("narrow"),
            P("narrow", None),
            P(),
        ),
        out_specs=(
            P(None, "wide", None),
            P(None, "wide", None),
            P(),
            P(),
            P("narrow"),
            P(None, "narrow"),
            P(None, "narrow"),
            P("narrow"),
            P("narrow", None),
            P(),
            P(),
            P(),
            P(None, None, "narrow"),
            P("narrow"),
            P("narrow"),
            P("narrow", None),
            P(),
            P(),
            P(),
            P(None, "narrow"),
            P("narrow"),
            P("narrow", None),
            P(),
        ),
        check_vma=False,
    )
```

```python
import math

import jax
import jax.numpy as jnp
from jax import lax
from jax.experimental import pallas as pl
from jax.experimental.pallas import tpu as pltpu
from jax.sharding import PartitionSpec as P

HEAD_DIM = 64
VARS = 48
PIX = 16
SCALE = HEAD_DIM ** (-0.5)

highest = lax.Precision.HIGHEST
AXES = ("wide", "narrow")
F32 = jnp.float32
BF16 = jnp.bfloat16


def low(tensor):
    return tensor.astype(BF16)


def dot(left, right, dims=((1,), (0,)), precision=None):
    return lax.dot_general(
        left, right, (dims, ((), ())), precision=precision, preferred_element_type=F32
    )


NT = ((1,), (1,))
TN = ((0,), (0,))


def struct(shape, dtype):
    return jax.ShapeDtypeStruct(shape, dtype)


class Gate:
    waits, hands, handed = [], [], []


def wait_for(*arrays):
    Gate.waits += arrays


def hand_on(*arrays):
    Gate.hands += arrays


def whole_block():
    return pl.BlockSpec(memory_space=pltpu.VMEM)


def pallas(
    kernel,
    out_shape,
    grid=(),
    in_specs=None,
    out_specs=None,
    scratch_shapes=(),
    prefetch=0,
    input_output_aliases=None,
    us=1,
    mib=28,
    name=None,
):
    single = not isinstance(out_shape, (list, tuple))
    shapes = [out_shape] if single else list(out_shape)
    if out_specs is None:
        outs = [whole_block() for _ in shapes]
    else:
        outs = [out_specs] if single else list(out_specs)

    def call(*operands):
        waits, hands = Gate.waits, Gate.hands
        Gate.waits, Gate.hands = [], []
        given = len(operands)
        specs = list(in_specs) if in_specs is not None else [whole_block() for _ in operands]
        aliases = dict(input_output_aliases or {})
        aliases |= {given + len(waits) + i: len(shapes) + i for i in range(len(hands))}
        extra = len(waits) + len(hands)

        def body(*refs):
            kept = refs[:given] + refs[given + extra : given + extra + len(shapes)]
            kernel(*kept, *refs[given + extra + len(shapes) + len(hands) :])

        got = pl.pallas_call(
            body,
            grid_spec=pltpu.PrefetchScalarGridSpec(
                num_scalar_prefetch=prefetch,
                grid=grid,
                in_specs=specs + [anywhere() for _ in range(extra)],
                out_specs=outs + [anywhere() for _ in hands],
                scratch_shapes=scratch_shapes,
            ),
            out_shape=shapes + [struct(array.shape, array.dtype) for array in hands],
            input_output_aliases=aliases,
            compiler_params=pltpu.CompilerParams(vmem_limit_bytes=mib << 20),
            cost_estimate=pl.CostEstimate(
                flops=int(us * 1.15e9), bytes_accessed=0, transcendentals=0
            ),
            name=name,
        )(*operands, *waits, *hands)
        Gate.handed = list(got[len(shapes) :])
        return got[0] if single else list(got[: len(shapes)])

    return call


def fixed(shape, *start):
    start = start or (0,) * len(shape)
    return pl.BlockSpec(shape, lambda *_: start)


def per_block(shape, offset=0, *rest):
    rest = rest or (0,) * len(shape)
    return pl.BlockSpec((1,) + shape, lambda n: (n + offset,) + rest)


def anywhere():
    return pl.BlockSpec(memory_space=pl.ANY)


class Ring:
    def __init__(self, wide_size, narrow_size, in_order):
        self.wide, self.narrow, self.sorted = wide_size, narrow_size, in_order
        self.order = list(range(0, narrow_size, 2)) + list(range(1, narrow_size, 2))[::-1]
        place = {device: index for index, device in enumerate(self.order)}
        self.w = lax.axis_index("wide")
        self.n = lax.axis_index("narrow")
        self.core = self.w % 2
        self.pos = jnp.where(self.n % 2 == 0, self.n // 2, narrow_size - 1 - self.n // 2)

        def step(device, hops):
            return self.order[(place[device] + hops) % narrow_size]

        every = [(w, n) for w in range(wide_size) for n in range(narrow_size)]
        flat = lambda w, n: w * narrow_size + n
        bits = lambda size: [1 << i for i in range(size.bit_length() - 1)]
        self.forward = [(flat(w, n), flat(w, step(n, 1))) for w, n in every]
        self.backward = [(flat(w, n), flat(w, step(n, -1))) for w, n in every]
        self.by_core = [(flat(w, n), flat(w, step(n, 1 - 2 * (w % 2)))) for w, n in every]
        self.far_by_core = lambda hops: [
            (flat(w, n), flat(w, step(n, hops * (1 - 2 * (w % 2))))) for w, n in every
        ]
        self.by_core_back = [(dst, src) for src, dst in self.by_core]
        self.wide_swap = {
            bit: [(flat(w, n), flat(w ^ bit, n)) for w, n in every] for bit in bits(wide_size)
        }
        self.narrow_swap = {
            bit: [(flat(w, n), flat(w, n ^ bit)) for w, n in every] for bit in bits(narrow_size)
        }

    def move(self, tensor, pairs):
        return lax.ppermute(tensor, AXES, pairs)

    def swap(self, tensor, bit=1):
        return self.move(tensor, self.wide_swap[bit])

    def at(self, hops):
        index = (self.pos + hops + 2 * self.narrow) % self.narrow
        return jnp.where(2 * index < self.narrow, 2 * index, 2 * (self.narrow - 1 - index) + 1)

    def ordered(self, first, second):
        if not self.sorted:
            return first, second
        pick = lambda a, b: jnp.where(self.core == 0, a, b)
        return pick(first, second), pick(second, first)

    def places(self):
        size = self.narrow
        sign = 1 if self.sorted else jnp.where(self.core == 0, 1, -1)
        order = [self.n, self.at(size // 2)]
        for hops in range(1, size // 2):
            order += [self.at(-sign * hops), self.at(sign * hops)]
        return order

    def scatter_wide(self, parts):
        parts = list(parts)
        for bit in self.wide_swap:
            kept = [index for index in range(self.wide) if index % (2 * bit) == 0]
            moved = [self.swap(parts[index | bit], bit) for index in kept]
            if len(kept) == 1:
                return parts[0], moved[0]
            sums = add_groups([[parts[index], got] for index, got in zip(kept, moved)])
            for index, total in zip(kept, sums):
                parts[index] = total

    def gather_wide(self, block):
        pieces = {0: block}
        for bit in self.wide_swap:
            for shift in list(pieces):
                pieces[shift | bit] = self.swap(pieces[shift], bit)
        return [pieces[shift] for shift in range(self.wide)]


def blank(shape, dtype):
    return pallas(
        lambda o_ref: None,
        out_shape=struct(shape, dtype),
        out_specs=anywhere(),
        us=0.1,
        name="blank",
    )()


def put(out, piece, index):
    return lax.dynamic_update_index_in_dim(out, piece, index, 0)


def add_kernel(groups, *refs):
    refs, outs = refs[: -len(groups)], refs[-len(groups) :]
    for size, out_ref in zip(groups, outs):
        total = refs[0][...].astype(F32)
        for ref in refs[1:size]:
            total = total + ref[...].astype(F32)
        out_ref[...] = low(total)
        refs = refs[size:]


def add_groups(groups):
    first = groups[0][0]
    shape = first[0].shape[1:] if isinstance(first, tuple) else first.shape
    width, size = shape[-1], math.prod(shape)
    rows = size // width
    steps = max(1, size * 2 >> 20)
    specs, flat = [], []
    for item in [item for group in groups for item in group]:
        array, part = item if isinstance(item, tuple) else (item, 0)
        start = part * steps
        specs.append(pl.BlockSpec((rows // steps, width), lambda i, start=start: (start + i, 0)))
        flat.append(array.reshape(-1, width))
    sums = pallas(
        lambda *refs: add_kernel([len(group) for group in groups], *refs),
        grid=(steps,),
        in_specs=specs,
        out_specs=[pl.BlockSpec((rows // steps, width), lambda i: (i, 0))] * len(groups),
        out_shape=[struct((rows, width), BF16)] * len(groups),
        us=2,
        mib=20,
        name="add",
    )(*flat)
    return [total.reshape(shape) for total in sums]


def add_up(*arrays):
    return add_groups([arrays])[0]


def pass_kernel(o_ref):
    o_ref[...] = jnp.zeros_like(o_ref)


def pass_on(arrays, *earlier):
    wait_for(*earlier)
    hand_on(*arrays)
    pallas(pass_kernel, out_shape=struct((8, 128), F32), us=0.5, mib=4, name="pass")()
    return Gate.handed


class GatherShared:
    def __init__(self, ring, block):
        self.ring, self.current, self.own = ring, block, block
        self.pairs, self.far = [], None

    def send(self):
        self.moved = self.ring.move(self.current, self.ring.by_core)

    def take(self, moved):
        ring, self.current = self.ring, moved
        if 2 * (len(self.pairs) + 1) < ring.narrow:
            self.pairs.append(ring.ordered(self.current, ring.swap(self.current)))
            return self.pairs[-1]
        self.far = self.current
        return [self.far]

    def step(self, *earlier):
        self.send()
        return self.take(pass_on([self.moved], *earlier)[0] if earlier else self.moved)

    def finish(self):
        while self.far is None:
            self.step()
        return [self.own, self.far] + [piece for pair in self.pairs for piece in pair]


class ScatterOwn:
    def __init__(self, ring, blocks):
        self.ring, self.blocks, self.hops = ring, blocks, ring.narrow // 2
        self.ahead, self.behind = self.pick(self.hops), None

    def pick(self, hops):
        return lax.dynamic_index_in_dim(self.blocks, self.ring.at(hops), 0, keepdims=False)

    def step(self):
        ring, self.hops = self.ring, self.hops - 1
        ahead = ring.move(self.ahead, ring.backward)
        behind = [] if self.behind is None else [ring.move(self.behind, ring.forward)]
        if not self.hops:
            self.ahead = add_up(ahead, *behind, self.pick(0))
        elif behind:
            self.ahead, self.behind = add_groups(
                [[ahead, self.pick(-self.hops)], [behind[0], self.pick(self.hops)]]
            )
        else:
            self.ahead, self.behind = add_up(ahead, self.pick(-self.hops)), self.pick(self.hops)
        return self.ahead


def gather_direct(ring, block):
    half = ring.narrow // 2
    came = [ring.move(block, ring.far_by_core(hops)) for hops in range(1, half + 1)]
    pairs = [ring.ordered(piece, ring.swap(piece)) for piece in came[:-1]]
    return [block, came[-1]] + [piece for pair in pairs for piece in pair]


class GatherOwn:
    def __init__(self, ring, block, dtype):
        self.ring, self.hops, self.dtype = ring, 0, dtype
        self.moving = [block, block]
        self.out = blank((ring.narrow,) + block.shape, dtype)
        self.out = put(self.out, block.astype(dtype), ring.n)
        self.send()

    def send(self):
        ring, self.hops = self.ring, self.hops + 1
        ways = [ring.forward, ring.backward] if 2 * self.hops < ring.narrow else [ring.forward]
        self.moving = [ring.move(block, way) for block, way in zip(self.moving, ways)]

    def place(self):
        for block, sign in zip(self.moving, (-1, 1)):
            index = self.ring.at(sign * self.hops)
            self.out = put(self.out, block.astype(self.dtype), index)
        self.done = 2 * self.hops >= self.ring.narrow
        if not self.done:
            self.send()

    def beside(self, kernel):
        hand_on(*self.moving)
        got = kernel()
        self.moving = list(Gate.handed)
        self.place()
        return got

    def after(self, *earlier):
        self.moving = self.handed = list(pass_on(self.moving, *earlier))
        self.place()

    def finish(self):
        while not self.done:
            self.place()
        return self.out


class ScatterShared:
    def __init__(self, ring, own, far):
        self.ring, self.own, self.current, self.got = ring, own, far, far

    def step(self, pair=None):
        ring = self.ring
        moved = ring.move(self.current, ring.by_core_back)
        if pair:
            first, second = ring.ordered(*pair)
            self.current = add_up(moved, first, ring.swap(second))
        else:
            self.current = add_up(moved, self.own)
        return self.current


class FinishShared:
    def __init__(self, ring, partial):
        self.ring, half = ring, partial.shape[0] // 2
        cut = lambda side: lax.dynamic_slice_in_dim(partial, side * half, half, 0)
        self.current, self.theirs = cut(ring.core), cut(1 - ring.core)
        self.bits = list(ring.wide_swap)

    def step(self):
        ring, bit = self.ring, self.bits.pop(0)
        sent = self.theirs if bit == 1 else self.current
        self.current = add_up(self.current, ring.swap(sent, bit))
        return self.current

    def finish(self):
        while self.bits:
            self.step()
        self.other = other = self.ring.swap(self.current)
        first = jnp.where(self.ring.core == 0, self.current, other).astype(F32)
        second = jnp.where(self.ring.core == 0, other, self.current).astype(F32)
        return first, second


class AddEverywhere:
    def __init__(self, ring, tensor):
        self.ring, self.current = ring, tensor
        self.pairs = list(ring.wide_swap.values()) + list(ring.narrow_swap.values())

    def send(self):
        self.moved = self.ring.move(self.current, self.pairs.pop(0))

    def take(self, *earlier):
        moved = pass_on([self.moved], *earlier)[0] if earlier else self.moved
        self.current = self.current + moved

    def step(self):
        self.send()
        self.take()

    def finish(self):
        while self.pairs:
            self.step()
        return self.current


def split_three(tensor):
    top = low(tensor)
    rest = tensor - top.astype(F32)
    middle = low(rest)
    return top, middle, low(rest - middle.astype(F32))


def lanes_to_rows(vector, cols):
    length = vector.shape[1]
    count = -(-length // cols)
    if count * cols > length:
        vector = jnp.concatenate([vector, jnp.zeros((1, count * cols - length), F32)], 1)
    return jnp.concatenate([vector[:, i * cols : (i + 1) * cols] for i in range(count)], 0)


def rows_to_lanes(rows, start, length):
    count = -(-length // rows.shape[1])
    return jnp.concatenate([rows[start + i : start + i + 1] for i in range(count)], 1)[:, :length]


class Extra:
    def __init__(self, cols, depth):
        self.heads, self.full = cols // HEAD_DIM, VARS * PIX + VARS
        self.term_rows, self.fold_rows = -(-self.full // cols), depth // cols
        self.fold_start = 3 * self.heads * self.term_rows
        self.bias_start = self.fold_start + 2 * self.heads * self.fold_rows

    def term(self, rows, part, head):
        return rows_to_lanes(rows, (part * self.heads + head) * self.term_rows, self.full)

    def folded(self, rows, head):
        place = lambda part: self.fold_start + (part * self.heads + head) * self.fold_rows
        length = self.fold_rows * rows.shape[1]
        return rows_to_lanes(rows, place(0), length) + rows_to_lanes(rows, place(1), length)

    def bias(self, rows, index):
        parts = [rows[self.bias_start + 3 * i + index :][:1] for i in range(3)]
        return parts[0] + (parts[1] + parts[2])


def prepare_kernel(
    key_ref, query_ref, table_ref, value_ref, output_ref, triple_ref, bias_ref, o_ref
):
    depth, cols = key_ref.shape
    extra = Extra(cols, depth)
    heads, full = extra.heads, extra.full
    keys, table = key_ref[...], table_ref[...]
    lane = lax.broadcasted_iota(jnp.int32, (8, cols), 1)
    row = lax.broadcasted_iota(jnp.int32, (8, cols), 0)
    masked = jnp.where(lane // HEAD_DIM == row, query_ref[...], 0.0)
    folded = sum(dot(part, keys, NT) for part in split_three(masked)[::-1])
    folded_parts = split_three(folded)
    terms = sum(dot(part, table, NT) for part in folded_parts[::-1]) * SCALE
    rows = [
        lanes_to_rows(part[h : h + 1, :full].astype(F32), cols)
        for part in split_three(terms)
        for h in range(heads)
    ]
    rows += [
        lanes_to_rows(part[h : h + 1].astype(F32), cols)
        for part in folded_parts[:2]
        for h in range(heads)
    ]
    rows += [lanes_to_rows(part.astype(F32), cols) for part in split_three(bias_ref[...])]
    rows.append(jnp.zeros((depth - full - sum(part.shape[0] for part in rows), cols), F32))
    o_ref[:3] = triple_ref[...]
    o_ref[3] = output_ref[...].astype(F32).T.astype(BF16)
    o_ref[4, :full] = low(dot(table, value_ref[...])[:full])
    o_ref[4, full:] = low(jnp.concatenate(rows, 0))


def prepare_call(keys, query, table, values, output, triple, bias):
    depth, cols = keys.shape
    return pallas(
        prepare_kernel,
        out_shape=struct((5, depth, cols), BF16),
        us=5.7,
        mib=40,
        name="prepare",
    )(keys, query, table, values, output, triple, bias)


def stage_kernel(up_ref, down_ref, value_ref, bias_ref, o_ref):
    depth, hidden = up_ref.shape
    cols = value_ref.shape[1]
    flip = lambda ref: ref[...].astype(F32).T.astype(BF16)
    o_ref[:cols] = flip(value_ref)
    o_ref[cols : cols + hidden] = flip(up_ref)
    o_ref[cols + hidden : cols + 2 * hidden] = down_ref[...]
    parts = [part.astype(F32) for part in split_three(bias_ref[...])]
    block = jnp.concatenate(parts + [jnp.zeros((13, hidden), F32)], 0)
    if hidden < depth:
        block = jnp.concatenate([block, jnp.zeros((16, depth - hidden), F32)], 1)
    o_ref[cols + 2 * hidden :] = low(block)


def stage_call(up, down, value, bias):
    depth, hidden = up.shape
    return pallas(
        stage_kernel,
        out_shape=struct((value.shape[1] + 2 * hidden + 16, depth), BF16),
        us=2,
        mib=40,
        name="stage",
    )(up, down, value, bias)


def arrange_kernel(x_ref, x1_ref, xt_ref):
    pixels = x_ref[...]
    x1_ref[...] = jnp.concatenate([pixels, jnp.ones((pixels.shape[0], VARS), BF16)], 1)
    xt_ref[...] = pixels.astype(F32).T.astype(BF16)


def arrange_call(pixels):
    tokens, width = pixels.shape
    return pallas(
        arrange_kernel,
        out_shape=[
            struct((tokens, width + VARS), BF16),
            struct((width, tokens), BF16),
        ],
        us=3.3,
        mib=40,
        name="arrange",
    )(pixels)


def slot_mask():
    slot = lax.broadcasted_iota(jnp.int32, (VARS, VARS * PIX + VARS), 0)
    column = lax.broadcasted_iota(jnp.int32, (VARS, VARS * PIX + VARS), 1)
    return slot == jnp.where(column < VARS * PIX, column // PIX, column - VARS * PIX)


def mix(weights, pixels_wide):
    tokens = weights.shape[1]
    spread = weights[:, None, :] * pixels_wide
    return jnp.concatenate([low(spread.reshape(VARS * PIX, tokens)), low(weights)], 0)


def pool_kernel(count, x_ref, xt_ref, valid_ref, *refs):
    p_refs, w_refs, o_refs = refs[:count], refs[count : 2 * count], refs[2 * count :]
    tokens, width = x_ref.shape
    pixels = x_ref[...]
    pixels_wide = xt_ref[...].astype(F32).reshape(VARS, PIX, tokens)
    valid = valid_ref[...] > 0
    mask = slot_mask()
    for p_ref, w_ref, o_ref in zip(p_refs, w_refs, o_refs):
        _, depth, cols = p_ref.shape
        extra = Extra(cols, depth)
        rows = p_ref[0, width:].astype(F32)
        table_value = p_ref[0, :width].astype(F32).T.astype(BF16)
        parts = []
        for h in range(extra.heads):
            scores = jnp.zeros((VARS, tokens), F32)
            for part in (2, 1, 0):
                spread = low(jnp.where(mask, extra.term(rows, part, h), 0.0))
                scores = scores + dot(spread, pixels, NT)
            scores = jnp.where(valid, scores, -1e30)
            weights = jnp.exp(scores - jnp.max(scores, 0, keepdims=True))
            weights = weights / jnp.sum(weights, 0, keepdims=True)
            w_ref[h] = weights
            mixed = mix(weights, pixels_wide)
            parts.append(dot(table_value[h * HEAD_DIM : (h + 1) * HEAD_DIM], mixed))
        pooled = jnp.concatenate(parts, 0) if len(parts) > 1 else parts[0]
        o_ref[...] = low(pooled.T + extra.bias(rows, 0))


def slot_of(piece, first, count=1):
    return fixed((count,) + piece.shape[1:], first // count, 0, 0)


def pool_call(pixels, pixels_t, valid, pieces):
    tokens = pixels.shape[0]
    cols = pieces[0].shape[2]
    count = len(pieces)
    weights, pooled = (cols // HEAD_DIM, VARS, tokens), (tokens, cols)
    got = pallas(
        lambda *refs: pool_kernel(count, *refs),
        grid=(1,),
        in_specs=[fixed(pixels.shape), fixed(pixels_t.shape), fixed((VARS, 1))]
        + [slot_of(piece, 4) for piece in pieces],
        out_specs=[fixed(weights)] * count + [fixed(pooled)] * count,
        out_shape=[struct(weights, F32)] * count + [struct(pooled, BF16)] * count,
        us=7,
        mib=40,
        name="pool",
    )(pixels, pixels_t, valid, *pieces)
    return list(zip(got[:count], got[count:]))


def pool_back_kernel(count, first, last, x_ref, xt_ref, g_ref, gt_ref, *refs):
    groups = [refs[i * count : (i + 1) * count] for i in range(4)]
    rest = refs[4 * count :]
    if not first:
        before_ref, rest = rest[0], rest[1:]
    pack_refs, (gx_ref, terms_ref, shift_ref) = rest[:count], rest[count:]
    tokens, full = x_ref.shape
    width = VARS * PIX
    pixels = x_ref[...]
    pixels_wide = xt_ref[...].astype(F32).reshape(VARS, PIX, tokens)
    mask = slot_mask()
    total = jnp.zeros((width, tokens), F32) if first else before_ref[...]
    for index, (v_ref, out_ref, w_ref, p_ref) in enumerate(zip(*groups)):
        _, depth, cols = v_ref.shape
        extra = Extra(cols, depth)
        rows = v_ref[0, full:].astype(F32)
        grads = low(dot(g_ref[...], out_ref[0]))
        shift_ref[index] = jnp.sum(grads.astype(F32), 0, keepdims=True)
        lane = lax.broadcasted_iota(jnp.int32, grads.shape, 1)
        table_value = v_ref[0, :full]
        product = jnp.zeros((full, cols), F32)
        for h in range(extra.heads):
            weights = w_ref[h]
            own = jnp.where(lane // HEAD_DIM == h, grads, 0) if extra.heads > 1 else grads
            grad_mixed = dot(table_value, own, NT)
            grad_wide = grad_mixed[:width].reshape(VARS, PIX, tokens)
            grad_weights = jnp.sum(grad_wide * pixels_wide, 1) + grad_mixed[width:]
            inner = jnp.sum(weights * grad_weights, 0, keepdims=True)
            grad_scores = weights * (grad_weights - inner)
            product = product + dot(mix(weights, pixels_wide), own)
            total = total + (weights[:, None, :] * grad_wide).reshape(width, tokens)
            gs_top = low(grad_scores)
            gs_rest = low(grad_scores - gs_top.astype(F32))
            top, middle = [
                low(jnp.where(mask, extra.term(rows, part, h), 0.0))[:, :width] for part in (0, 1)
            ]
            stacked = jnp.concatenate([top, top, middle], 0)
            total = total + dot(stacked, jnp.concatenate([gs_top, gs_rest, gs_top], 0), TN)
            both = dot(jnp.concatenate([gs_top, gs_rest], 0), pixels)
            by_slot = jnp.where(mask, both[:VARS] + both[VARS:], 0.0)
            terms_ref[index, h : h + 1, :] = jnp.sum(by_slot, 0, keepdims=True)
        pack_ref = pack_refs[index]
        pack_ref[0] = low(dot(gt_ref[...], p_ref[...]))
        pack_ref[1, :full] = low(product)
        pack_ref[1, full:] = jnp.zeros((depth - full, cols), BF16)
    gx_ref[...] = low(total.T) if last else total


def pool_back_call(pixels, pixels_t, heads, pieces, grads, grads_t, before, last):
    count = len(pieces)
    tokens, full = pixels.shape
    width = pixels_t.shape[0]
    _, depth, cols = pieces[0].shape
    in_specs = [fixed(array.shape) for array in (pixels, pixels_t, grads, grads_t)]
    in_specs += [slot_of(piece, 4) for piece in pieces] + [slot_of(piece, 3) for piece in pieces]
    in_specs += [fixed(head[0].shape) for head in heads] + [fixed(head[1].shape) for head in heads]
    operands = [pixels, pixels_t, grads, grads_t, *pieces, *pieces]
    operands += [head[0] for head in heads] + [head[1] for head in heads]
    if before is not None:
        in_specs.append(fixed((width, tokens)))
        operands.append(before)
    shapes = [struct((2, depth, cols), BF16)] * count
    shapes.append(struct((tokens, width), BF16) if last else struct((width, tokens), F32))
    shapes.append(struct((count, cols // HEAD_DIM, full), F32))
    shapes.append(struct((count, 1, cols), F32))
    got = pallas(
        lambda *refs: pool_back_kernel(count, before is None, last, *refs),
        grid=(1,),
        in_specs=in_specs,
        out_specs=[fixed(shape.shape) for shape in shapes],
        out_shape=shapes,
        us=21,
        name="pool_back",
    )(*operands)
    return list(got[:count]), *got[count:]


def normalise(stream):
    centered = stream - jnp.mean(stream, -1, keepdims=True)
    scale = lax.rsqrt(jnp.mean(centered * centered, -1, keepdims=True) + 1e-05)
    return centered * scale, scale


def normalise_back(grad, stream, gain):
    hat, scale = normalise(stream)
    through = grad * gain
    inner = through - jnp.mean(through, -1, keepdims=True)
    inner = inner - hat * jnp.mean(through * hat, -1, keepdims=True)
    add = lambda tensor: jnp.sum(tensor, 0, keepdims=True)
    return scale * inner, add(grad * hat), add(grad)


def enter_kernel(count, *refs):
    p_refs, w_refs = refs[:count], refs[count : 2 * count]
    bias_ref, gain_ref, shift_ref, s_ref, x_ref, xt_ref = refs[2 * count :]
    stream = jnp.zeros(s_ref.shape, F32) + bias_ref[...]
    for p_ref, w_ref in zip(p_refs, w_refs):
        stream = stream + dot(p_ref[...], w_ref[0], NT)
    s_ref[...] = stream
    hat, _ = normalise(stream)
    rows = hat * gain_ref[...] + shift_ref[...]
    x_ref[...] = low(rows)
    xt_ref[...] = low(rows.T)


def enter_call(pooled, pieces, bias, gain, shift):
    tokens = pooled[0].shape[0]
    depth = pieces[0].shape[1]
    row = fixed((1, depth))
    return pallas(
        lambda *refs: enter_kernel(len(pieces), *refs),
        grid=(1,),
        in_specs=[fixed(part.shape) for part in pooled]
        + [slot_of(piece, 3) for piece in pieces]
        + [row, row, row],
        out_specs=[fixed((tokens, depth)), fixed((tokens, depth)), fixed((depth, tokens))],
        out_shape=[
            struct((tokens, depth), F32),
            struct((tokens, depth), BF16),
            struct((depth, tokens), BF16),
        ],
        us=7,
        mib=56,
        name="enter",
    )(*pooled, *pieces, bias, gain, shift)


def beside(ref):
    return jnp.concatenate([ref[i] for i in range(3)], 1)


def project_kernel(count, x_ref, *refs):
    w_refs, e_refs, q_refs = refs[:count], refs[count : 2 * count], refs[2 * count : -1]
    kv_ref = refs[-1]
    for index, (w_ref, e_ref) in enumerate(zip(w_refs, e_refs)):
        _, depth, cols = w_ref.shape
        extra = Extra(cols, depth)
        rows = e_ref[0, extra.full :].astype(F32)
        triple = dot(x_ref[...], beside(w_ref))
        q_refs[index // 2][index % 2] = low(triple[:, :cols] + extra.bias(rows, 1))
        kv_ref[index, 0] = low(triple[:, cols : 2 * cols])
        kv_ref[index, 1] = low(triple[:, 2 * cols :] + extra.bias(rows, 2))


def project_call(rows, pieces):
    count = len(pieces)
    cols = pieces[0].shape[2]
    tokens = rows.shape[0]
    shapes = [struct((2, tokens, cols), BF16)] * (count // 2)
    shapes.append(struct((count, 2, tokens, cols), BF16))
    got = pallas(
        lambda *refs: project_kernel(count, *refs),
        grid=(1,),
        in_specs=[fixed(rows.shape)]
        + [slot_of(piece, 0, 3) for piece in pieces]
        + [slot_of(piece, 4) for piece in pieces],
        out_specs=[fixed(shape.shape) for shape in shapes],
        out_shape=shapes,
        us=1.2 * count,
        mib=40,
        name="project",
    )(rows, *pieces, *pieces)
    return got[:-1], got[-1]


def project_back_kernel(count, first, xt_ref, gq_ref, gkv_ref, *refs):
    w_refs, rest = refs[:count], refs[2 * count :]
    if not first:
        before_ref, rest = rest[0], rest[1:]
    gw_refs, (gx_ref, sums_ref) = rest[:count], rest[count:]
    cols = gq_ref.shape[2]
    total = jnp.zeros(gx_ref.shape, F32) if first else before_ref[...]
    for index, (w_ref, gw_ref) in enumerate(zip(w_refs, gw_refs)):
        grads = jnp.concatenate([gq_ref[index], gkv_ref[index, 0], gkv_ref[index, 1]], 1)
        total = total + dot(grads, beside(w_ref), NT)
        products = low(dot(xt_ref[...], grads))
        for i in range(3):
            gw_ref[i] = products[:, i * cols : (i + 1) * cols]
        sums_ref[index] = jnp.sum(grads.astype(F32), 0, keepdims=True)
    gx_ref[...] = total


def project_back_call(rows_t, pieces, grad_query, grad_pair, grad_pieces, before):
    count = len(pieces)
    depth, tokens = rows_t.shape
    cols = pieces[0].shape[2]
    in_specs = [fixed(array.shape) for array in (rows_t, grad_query, grad_pair)]
    in_specs += [slot_of(piece, 0, 3) for piece in pieces] + [anywhere()] * count
    operands = [rows_t, grad_query, grad_pair, *pieces, *grad_pieces]
    if before is not None:
        in_specs.append(fixed((tokens, depth)))
        operands.append(before)
    shapes = [struct(piece.shape, BF16) for piece in grad_pieces]
    shapes += [struct((tokens, depth), F32), struct((count, 1, 3 * cols), F32)]
    got = pallas(
        lambda *refs: project_back_kernel(count, before is None, *refs),
        grid=(1,),
        in_specs=in_specs,
        out_specs=[slot_of(piece, 0, 3) for piece in grad_pieces]
        + [fixed(shape.shape) for shape in shapes[count:]],
        out_shape=shapes,
        input_output_aliases={3 + count + i: i for i in range(count)},
        us=13.6,
        name="project_back",
    )(*operands)
    return list(got[:count]), *got[count:]


def leave_kernel(g_ref, s_ref, before_ref, gain_ref, o_ref, ot_ref, sums_ref):
    through, gain, shift = normalise_back(g_ref[...], s_ref[...], gain_ref[...])
    total = before_ref[...] + through
    rounded = low(total)
    o_ref[...] = rounded
    ot_ref[...] = low(total.T)
    bias = jnp.sum(rounded.astype(F32), 0, keepdims=True)
    sums_ref[...] = jnp.concatenate([gain, shift, bias], 0)


def leave_call(grad_normed, stream, before, gain):
    tokens, depth = stream.shape
    return pallas(
        leave_kernel,
        out_shape=[
            struct((tokens, depth), BF16),
            struct((depth, tokens), BF16),
            struct((3, depth), F32),
        ],
        us=12,
        name="leave",
    )(grad_normed, stream, before, gain)


def attend_kernel(count, q_ref, *refs):
    sources, (o_ref, total_ref) = refs[:count], refs[count:]
    cols = q_ref.shape[2]
    heads = cols // HEAD_DIM
    scaled = q_ref[0] * SCALE
    lane = lax.broadcasted_iota(jnp.int32, scaled.shape, 1)
    values_t = [source[0, 1].T for source in sources]
    parts = []
    for h in range(heads):
        own = jnp.where(lane // HEAD_DIM == h, scaled, 0) if heads > 1 else scaled
        logits = [dot(source[0, 0], own, NT) for source in sources]
        peak = jnp.max(logits[0], 0, keepdims=True)
        for piece in logits[1:]:
            peak = jnp.maximum(peak, jnp.max(piece, 0, keepdims=True))
        norm = jnp.zeros_like(peak)
        out = jnp.zeros((HEAD_DIM, peak.shape[1]), F32)
        for piece, value in zip(logits, values_t):
            weight = jnp.exp(piece - peak)
            norm = norm + jnp.sum(weight, 0, keepdims=True)
            out = out + dot(value[h * HEAD_DIM : (h + 1) * HEAD_DIM], low(weight))
        parts.append(out / norm)
        total_ref[0, h] = peak + jnp.log(norm)
    full = jnp.concatenate(parts, 0) if heads > 1 else parts[0]
    o_ref[0] = full.T


def pair_spec(shape, flip, start=0):
    place = lambda n: (start + (1 - n if flip else n),) + (0,) * len(shape)
    return pl.BlockSpec((1,) + shape, place)


def attend_call(queries, sources, flips, start):
    count, tokens, cols = queries.shape
    heads = cols // HEAD_DIM
    keys = sum(array.shape[2] for array in sources)
    work = count * tokens * keys * cols
    return pallas(
        lambda *refs: attend_kernel(len(sources), *refs),
        grid=(count,),
        in_specs=[per_block((tokens, cols))]
        + [pair_spec(array.shape[1:], flip, start) for array, flip in zip(sources, flips)],
        out_specs=[per_block((tokens, cols)), per_block((heads, 1, tokens))],
        out_shape=[
            struct((count, tokens, cols), F32),
            struct((count, heads, 1, tokens), F32),
        ],
        us=8.7,
        name="attend",
    )(queries, *sources)


def middle_kernel(count, s_ref, *refs):
    o_refs, w_refs = refs[:count], refs[count : 3 * count]
    bias_ref, gain_ref, shift_ref, s1_ref, x_ref, xt_ref = refs[3 * count :]
    stream = s_ref[...] + bias_ref[...]
    for index, w_ref in enumerate(w_refs):
        stream = stream + dot(low(o_refs[index // 2][index % 2]), w_ref[...])
    s1_ref[...] = stream
    hat, _ = normalise(stream)
    rows = hat * gain_ref[...] + shift_ref[...]
    x_ref[...] = low(rows)
    xt_ref[...] = low(rows.T)


def middle_call(stream, attended, weights, bias, gain, shift):
    tokens, depth = stream.shape
    operands = [stream, *attended, *weights, bias, gain, shift]
    shapes = [
        struct((tokens, depth), F32),
        struct((tokens, depth), BF16),
        struct((depth, tokens), BF16),
    ]
    return pallas(
        lambda *refs: middle_kernel(len(attended), *refs),
        grid=(1,),
        in_specs=[fixed(array.shape) for array in operands],
        out_specs=[fixed(shape.shape) for shape in shapes],
        out_shape=shapes,
        us=5,
        mib=40,
        name="middle",
    )(*operands)


def middle_back_kernel(g_ref, gt_ref, o_ref, wa_ref, wb_ref, go_ref, delta_ref, ga_ref, gb_ref):
    _, tokens, cols = o_ref.shape
    heads = cols // HEAD_DIM
    lane = lax.broadcasted_iota(jnp.int32, (8, cols), 1)
    row = lax.broadcasted_iota(jnp.int32, (8, cols), 0)
    mask = jnp.where(lane // HEAD_DIM == row, 1.0, 0.0)
    for index, (w_ref, gw_ref) in enumerate(((wa_ref, ga_ref), (wb_ref, gb_ref))):
        grads = low(dot(g_ref[...], w_ref[...], NT))
        go_ref[index] = grads
        attended = o_ref[index]
        gw_ref[0] = low(dot(gt_ref[...], low(attended)))
        sums = dot(mask, grads.astype(F32) * attended, NT, precision=highest)
        for h in range(heads):
            delta_ref[index, h] = sums[h : h + 1]


def middle_back_call(grads, grads_t, attended, weights):
    count, tokens, cols = attended.shape
    depth = grads.shape[1]
    heads = cols // HEAD_DIM
    piece = struct((4, depth, cols), BF16)
    operands = [grads, grads_t, attended, *weights]
    return pallas(
        middle_back_kernel,
        grid=(1,),
        in_specs=[fixed(array.shape) for array in operands],
        out_specs=[fixed(attended.shape), fixed((count, heads, 1, tokens))]
        + [slot_of(piece, 3)] * 2,
        out_shape=[
            struct(attended.shape, BF16),
            struct((count, heads, 1, tokens), F32),
            piece,
            piece,
        ],
        us=4,
        name="middle_back",
    )(*operands)


def attend_back_kernel(count, first, last, together, q_ref, g_ref, total_ref, delta_ref, *refs):
    sources, rest = refs[:count], refs[count:]
    before_ref, gq_ref, targets = (
        (None, rest[0], rest[1:]) if first else (rest[0], rest[1], rest[2:])
    )
    if together:
        targets = [targets[0].at[i] for i in range(count)]
    cols = q_ref.shape[2]
    heads = cols // HEAD_DIM
    scaled = q_ref[0] * SCALE
    grads = g_ref[0]
    lane = lax.broadcasted_iota(jnp.int32, scaled.shape, 1)
    pick = lambda tensor, h: jnp.where(lane // HEAD_DIM == h, tensor, 0) if heads > 1 else tensor
    own_q = [pick(scaled, h) for h in range(heads)]
    own_g = [pick(grads, h) for h in range(heads)]
    queries_t = [jnp.zeros((HEAD_DIM, scaled.shape[0]), F32) for h in range(heads)]
    for source, target in zip(sources, targets):
        keys, values = source[0, 0], source[0, 1]
        keys_t = keys.T
        grad_keys = jnp.zeros(keys.shape, F32)
        grad_values = jnp.zeros(keys.shape, F32)
        for h in range(heads):
            weight = jnp.exp(dot(keys, own_q[h], NT) - total_ref[0, h])
            grad_weight = dot(values, own_g[h], NT)
            grad_logit = low(weight * (grad_weight - delta_ref[0, h]))
            grad_values = grad_values + dot(low(weight), own_g[h])
            grad_keys = grad_keys + dot(grad_logit, own_q[h])
            queries_t[h] = queries_t[h] + dot(
                keys_t[h * HEAD_DIM : (h + 1) * HEAD_DIM], grad_logit
            )
        target[0, 0] = low(grad_keys)
        target[0, 1] = low(grad_values)
    full = jnp.concatenate(queries_t, 0) if heads > 1 else queries_t[0]
    if before_ref is not None:
        full = full + before_ref[0]
    gq_ref[0] = low(full * SCALE).T if last else full


def attend_back_call(queries, grads, totals, deltas, sources, flips, start, before, last, together):
    count, tokens, cols = queries.shape
    heads = cols // HEAD_DIM
    keys = sum(array.shape[2] for array in sources)
    work = count * tokens * keys * cols
    block = sources[0].shape[1:]
    first = before is None
    outs = [pair_spec(block, flip) for flip in flips]
    shapes = [struct((count,) + block, BF16) for _ in sources]
    if together:
        flip = flips[0]
        place = lambda n: (0, 1 - n if flip else n) + (0,) * len(block)
        outs = [pl.BlockSpec((len(sources), 1) + block, place)]
        shapes = [struct((len(sources), count) + block, BF16)]
    result = struct((count, tokens, cols), BF16) if last else struct((count, cols, tokens), F32)
    return pallas(
        lambda *refs: attend_back_kernel(len(sources), first, last, together, *refs),
        grid=(count,),
        in_specs=[
            per_block((tokens, cols)),
            per_block((tokens, cols)),
            per_block((heads, 1, tokens)),
            per_block((heads, 1, tokens)),
        ]
        + [pair_spec(block, flip, start) for flip in flips]
        + ([] if first else [per_block((cols, tokens))]),
        out_specs=[per_block(result.shape[1:])] + outs,
        out_shape=[result] + shapes,
        us=15.2,
        name="attend_back",
    )(queries, grads, totals, deltas, *sources, *([] if first else [before]))


def feed_parts(w_ref, cols):
    hidden = (w_ref.shape[1] - 16 - cols) // 2
    rows_of = lambda start: jnp.concatenate([w_ref[i, start : start + hidden] for i in range(2)], 0)
    bias = []
    for i in range(2):
        rows = w_ref[i, cols + 2 * hidden :, :hidden].astype(F32)
        bias.append(rows[0:1] + (rows[1:2] + rows[2:3]))
    return rows_of(cols), rows_of(cols + hidden), jnp.concatenate(bias, 1)


def gate_of(before):
    return 0.5 * (1.0 + lax.erf(before * 0.7071067811865476))


def feed_kernel(cols, x_ref, w_ref, y_ref, y_sum):
    step = pl.program_id(0)
    up, down, bias = feed_parts(w_ref, cols)
    before = dot(x_ref[...], up, NT) + bias
    part = dot(low(before * gate_of(before)), down)

    @pl.when(step == 0)
    def _():
        y_sum[...] = part

    @pl.when(step > 0)
    def _():
        y_sum[...] += part

    @pl.when(step == pl.num_programs(0) - 1)
    def _():
        y_ref[...] = low(y_sum[...])


def feed_call(cols, rows, staged):
    whole = fixed(rows.shape)
    return pallas(
        lambda *refs: feed_kernel(cols, *refs),
        grid=(staged.shape[0] // 2,),
        in_specs=[whole, pl.BlockSpec((2,) + staged.shape[1:], lambda n: (n, 0, 0))],
        out_specs=whole,
        out_shape=struct(rows.shape, BF16),
        scratch_shapes=[pltpu.VMEM(rows.shape, F32)],
        us=4,
        mib=40,
        name="feed",
    )(rows, staged)


def feed_back_kernel(first, cols, x_ref, g_ref, w_ref, *refs):
    if not first:
        before_ref, refs = refs[0], refs[1:]
    gx_ref, gb_ref, gw_ref, gx_sum = refs
    step = pl.program_id(0)
    up, down, bias = feed_parts(w_ref, cols)
    hidden = up.shape[0] // 2
    rows, grads = x_ref[...], g_ref[...]
    before = dot(rows, up, NT) + bias
    bell = gate_of(before)
    active = low(before * bell)
    slope = bell + before * (0.3989422804014327 * jnp.exp(-0.5 * before * before))
    grad_hidden = low(slope * dot(grads, down, NT))
    part_sum = dot(grad_hidden, up)
    grad_up = dot(grad_hidden, rows, TN)
    grad_down = dot(active, grads, TN)
    gb_ref[0] = jnp.sum(grad_hidden.astype(F32), 0, keepdims=True)
    for i in range(2):
        part = slice(i * hidden, (i + 1) * hidden)
        made = jnp.concatenate([grad_up[part], grad_down[part]], 0)
        made = made if first else made + before_ref[i].astype(F32)
        gw_ref[i] = low(made)

    @pl.when(step == 0)
    def _():
        gx_sum[...] = part_sum

    @pl.when(step > 0)
    def _():
        gx_sum[...] += part_sum

    @pl.when(step == pl.num_programs(0) - 1)
    def _():
        gx_ref[...] = low(gx_sum[...])


def feed_back_call(cols, rows, grads, staged, before):
    count, lines, depth = staged.shape
    lines = lines - 16 - cols
    whole = fixed(rows.shape)
    pair = pl.BlockSpec((2, lines, depth), lambda n: (n, 0, 0))
    first = before is None
    return pallas(
        lambda *refs: feed_back_kernel(first, cols, *refs),
        grid=(count // 2,),
        in_specs=[whole, whole, pl.BlockSpec((2,) + staged.shape[1:], lambda n: (n, 0, 0))]
        + ([] if first else [pair]),
        out_specs=[whole, pl.BlockSpec((1, 1, lines), lambda n: (n, 0, 0)), pair],
        out_shape=[
            struct(rows.shape, BF16),
            struct((count // 2, 1, lines), F32),
            struct((count, lines, depth), BF16),
        ],
        scratch_shapes=[pltpu.VMEM(rows.shape, F32)],
        us=9,
        mib=40,
        name="feed_back",
    )(rows, grads, staged, *([] if first else [before]))


def turn_kernel(count, *refs):
    g_ref, s_ref, gain_ref, gs_ref, g1_ref, g1t_ref, sums_ref = refs[count:]
    grad = refs[0][...].astype(F32)
    for ref in refs[1:count]:
        grad = grad + ref[...].astype(F32)
    through, gain, shift = normalise_back(grad, s_ref[...], gain_ref[...])
    grads = g_ref[...].astype(F32)
    total = grads + through
    gs_ref[...] = total
    rounded = low(total)
    g1_ref[...] = rounded
    g1t_ref[...] = low(total.T)
    add = lambda tensor: jnp.sum(tensor, 0, keepdims=True)
    sums_ref[...] = jnp.concatenate([gain, shift, add(grads), add(rounded.astype(F32))], 0)


def turn_call(parts, grads, stream, gain):
    tokens, depth = stream.shape
    return pallas(
        lambda *refs: turn_kernel(len(parts), *refs),
        out_shape=[
            struct((tokens, depth), F32),
            struct((tokens, depth), BF16),
            struct((depth, tokens), BF16),
            struct((4, depth), F32),
        ],
        us=8,
        name="turn",
    )(*parts, grads, stream, gain)


def assemble_kernel(w_ref, *refs):
    pieces, (up_ref, down_ref) = refs[:-2], refs[-2:]
    hidden = pieces[0].shape[0] // 2
    for index, piece in enumerate(pieces):

        @pl.when(pl.program_id(0) == index)
        def _():
            up_ref[...] = piece[:hidden].astype(F32).T
            down_ref[...] = piece[hidden:].astype(F32)


def assemble_call(w, pieces):
    count = len(pieces)
    lines, depth = pieces[0].shape
    hidden = lines // 2
    direct = hidden % 128 == 0
    up_place = (
        (lambda i, w_ref: (0, w_ref[0] ^ i)) if direct else (lambda i, w_ref: (w_ref[0] ^ i, 0))
    )
    up, down = pallas(
        assemble_kernel,
        prefetch=1,
        grid=(count,),
        in_specs=[pl.BlockSpec((lines, depth), lambda i, w_ref: (0, 0)) for _ in pieces],
        out_specs=[
            pl.BlockSpec((depth, hidden), up_place),
            pl.BlockSpec((hidden, depth), lambda i, w_ref: (w_ref[0] ^ i, 0)),
        ],
        out_shape=[
            struct((depth, count * hidden) if direct else (count * depth, hidden), F32),
            struct((count * hidden, depth), F32),
        ],
        us=3.3,
        name="assemble",
    )(w.reshape(1), *pieces)
    if not direct:
        up = up.reshape(count, depth, hidden).transpose(1, 0, 2).reshape(depth, count * hidden)
    return up, down


def table_kernel(count, order_ref, terms_ref, v_ref, *refs):
    p_refs, e_refs = refs[:count], refs[count : 2 * count]
    patch_ref, slot_ref = refs[2 * count :]
    depth = patch_ref.shape[1]
    cols = p_refs[0].shape[1]
    extra = Extra(cols, depth)
    folded = []
    total = jnp.zeros((extra.full, depth), F32)
    for index, (p_ref, e_ref) in enumerate(zip(p_refs, e_refs)):
        rows = e_ref[0, extra.full :].astype(F32)
        folded += [extra.folded(rows, h) for h in range(extra.heads)]
        total = total + dot(p_ref[...], v_ref[order_ref[index]])
    total = total + dot(terms_ref[...], jnp.concatenate(folded, 0), TN, precision=highest)
    width = patch_ref.shape[0]
    patch_ref[...] = total[:width]
    slot_ref[...] = total[width:]


def table_call(order, terms, values, products, pieces):
    _, depth, cols = pieces[0].shape
    width = VARS * PIX
    return pallas(
        lambda *refs: table_kernel(len(pieces), *refs),
        prefetch=1,
        grid=(1,),
        in_specs=[fixed(terms.shape), fixed((values.shape[0], cols, depth))]
        + [fixed(part.shape) for part in products]
        + [slot_of(piece, 4) for piece in pieces],
        out_specs=[fixed((width, depth)), fixed((VARS, depth))],
        out_shape=[struct((width, depth), F32), struct((VARS, depth), F32)],
        us=9,
        mib=56,
        name="table_back",
    )(order, terms, values, *products, *pieces)


def on_device(
    wide_size,
    narrow_size,
    variables,
    valid_slots,
    out_grad,
    patch_embed,
    variable_embed,
    pool_query,
    pool_key,
    pool_value,
    value_shift,
    pool_output,
    pool_bias,
    first_gain,
    first_shift,
    self_weights,
    query_bias,
    value_bias,
    self_output,
    output_bias,
    second_gain,
    second_shift,
    feed_up,
    up_bias,
    feed_down,
    down_bias,
):
    samples, token_count, input_width = variables.shape
    model_width = patch_embed.shape[1]
    local_dim = pool_query.shape[0]
    heads = local_dim // HEAD_DIM
    hidden = up_bias.shape[0]
    shares = narrow_size // samples
    permuted = wide_size == 4 and shares == 1
    ring = Ring(wide_size, narrow_size, not permuted)
    tokens = token_count // shares
    groups = narrow_size // 2
    row = lambda vector: vector.reshape(1, -1)
    pair_of = lambda pieces, g: pieces[2 * g : 2 * g + 2]
    place = (ring.n // shares, (ring.n % shares) * tokens, 0)
    pixels = lax.dynamic_slice(variables, place, (1, tokens, input_width))[0]
    grads = lax.dynamic_slice(out_grad, place, (1, tokens, model_width))[0]
    valid = lax.dynamic_index_in_dim(valid_slots, ring.n // shares, 0, keepdims=False)
    valid = valid.reshape(VARS, 1)

    filler = jnp.zeros((model_width - input_width - VARS, model_width), BF16)
    table_full = jnp.concatenate([patch_embed, variable_embed, filler], 0)
    gather = GatherShared(
        ring,
        prepare_call(
            pool_key,
            row(pool_query),
            table_full,
            pool_value,
            pool_output,
            self_weights.transpose(1, 0, 2),
            row(jnp.concatenate([value_shift, query_bias, value_bias])),
        ),
    )
    pixels_one, pixels_t = arrange_call(pixels)
    all_grads = ring.gather_wide(grads)
    quarter = hidden // wide_size
    cut_out = lambda tensor, axis: lax.dynamic_slice_in_dim(tensor, ring.w * quarter, quarter, axis)
    feed_own = stage_call(
        cut_out(feed_up, 1), cut_out(feed_down, 0), pool_value, row(cut_out(up_bias, 0))
    )
    pool = lambda pieces: pool_call(pixels_one, pixels_t, valid, pieces)
    wait_for(feed_own)
    pooled = pool([gather.own])
    for g in range(1, groups):
        got = list(gather.step())
        wait_for(pooled[-1][1])
        if g == 2:
            wait_for(*all_grads)
        pooled += pool(got)
    gather.step()
    wait_for(pooled[-1][1])
    hand_on(feed_own, self_output)
    far = pool([gather.far])
    feed_all = lax.all_gather(Gate.handed[0], "narrow")
    gather_mixer = GatherShared(ring, Gate.handed[1])
    pooled = [pooled[0], far[0]] + pooled[1:]
    pieces = gather.finish()
    stream_zero, normed_one, normed_one_t = enter_call(
        [head[1] for head in pooled], pieces, row(pool_bias), row(first_gain), row(first_shift)
    )

    subsets = [[s * shares + i for i in range(shares)] for s in range(samples)]
    chunks = [[g] for g in range(groups)]
    gather_mixer.step(stream_zero)
    queries, sources, flips, starts = [], [], [], []
    for chunk in chunks:
        if queries:
            wait_for(queries[-1])
        mine, pair = project_call(normed_one, pieces[2 * chunk[0] : 2 * chunk[-1] + 2])
        queries += mine
        if permuted:
            across = ring.swap(pair, 2)
            got = [pair, ring.swap(pair, 1), across, ring.swap(across, 1)]
        else:
            full = lax.all_gather(pair, "wide", axis=2, tiled=True)
            if shares > 1:
                full = lax.all_gather(
                    full, "narrow", axis=2, tiled=True, axis_index_groups=subsets
                )
            got = [full]
        for g in chunk:
            sources.append(got)
            flips.append([False, g > 0, False, g > 0] if permuted else [False])
            starts.append(2 * (g - chunk[0]))
    gather_mixer.step(queries[-1])
    attended, totals = [], []
    for g in range(groups):
        if attended:
            wait_for(attended[-1])
        got = attend_call(queries[g], sources[g], flips[g], starts[g])
        attended.append(got[0])
        totals.append(got[1])
        if g < 2:
            gather_mixer.step(got[0])
    self_pieces = gather_mixer.finish()
    order = jnp.stack(ring.places()).astype(jnp.int32)
    stream_one, normed_two, _ = middle_call(
        stream_zero, attended, self_pieces, row(output_bias), row(second_gain), row(second_shift)
    )

    all_rows = ring.gather_wide(normed_two)
    y_all, gx_all, gb_all, grad_feed = [], [], [], None
    near = max(1, wide_size // 2)
    plan = [(False, i) for i in range(near)] + [(True, 0)]
    plan += [(False, i) for i in range(near, wide_size)]
    plan += [(True, i) for i in range(1, wide_size)]
    latest = None
    for way_back, index in plan:
        if latest is not None:
            wait_for(latest)
        if not way_back:
            y_all.append(feed_call(local_dim, all_rows[index], feed_all))
            latest = y_all[-1]
            if index == wide_size - 1:
                y_parts = ring.scatter_wide(y_all)
                block_own = y_parts[0].astype(F32) + y_parts[1].astype(F32)
                block_own = low(stream_one + down_bias + block_own)
            continue
        if index == wide_size - 1:
            wait_for(block_own)
        got = feed_back_call(
            local_dim, all_rows[index], all_grads[index], feed_all, grad_feed
        )
        gx_all.append(got[0])
        gb_all.append(got[1])
        grad_feed = got[2]
        latest = got[0]
    gather_out = GatherOwn(ring, block_own, BF16)
    scatter_feed = ScatterOwn(ring, grad_feed)
    grad_parts = ring.scatter_wide(gx_all)
    grad_up_bias = sum(gb_all).reshape(narrow_size, quarter)
    grad_stream_one, grad_one, grad_one_t, sums_two = turn_call(
        grad_parts, grads, stream_one, row(second_gain)
    )

    waiting = {}
    backward = [0] + list(range(groups - 1, 0, -1))
    for turn, g in enumerate(backward):
        grad_attended, deltas, *grad_pair_mixers = middle_back_call(
            grad_one, grad_one_t, attended[g], pair_of(self_pieces, g)
        )
        back = lambda chosen, before, last, together: attend_back_call(
            queries[g],
            grad_attended,
            totals[g],
            deltas,
            [sources[g][i] for i in chosen],
            [flips[g][i] for i in chosen],
            starts[g],
            before,
            last,
            together,
        )
        if permuted:
            some, crossing = back([1, 3], None, False, True)
            crossed = ring.swap(crossing)
            grad_query, grad_own, grad_across = back([0, 2], some, True, False)
            far = add_up(grad_across, (crossed, 1))
            grad_pair = [grad_own, (crossed, 0), ring.swap(far, 2)]
        else:
            grad_query, full = back([0], None, True, False)
            if shares > 1:
                full = lax.psum_scatter(
                    full, "narrow", scatter_dimension=2, tiled=True, axis_index_groups=subsets
                )
            far = lax.psum_scatter(full, "wide", scatter_dimension=2, tiled=True)
            grad_pair = [far]
        waiting[g] = (grad_query, grad_pair, grad_pair_mixers)
        wait_for(far)
        if turn in (0, 2):
            wait_for(gather_out.beside(scatter_feed.step))
    grad_normed_one, grad_pieces, sums_triple = None, {}, [None] * groups
    for turn, g in enumerate(backward):
        grad_query, grad_pair, grad_pair_mixers = waiting[g]
        if grad_normed_one is not None:
            wait_for(grad_normed_one)
        grad_pair = add_up(*grad_pair)
        back = lambda: project_back_call(
            normed_one_t,
            pair_of(pieces, g),
            grad_query,
            grad_pair,
            grad_pair_mixers,
            grad_normed_one,
        )
        if turn == 3:
            wait_for(gather_out.beside(scatter_feed.step))
        made, grad_normed_one, sums = back()
        grad_pieces[g], sums_triple[g] = made, sums
    scatter = ScatterShared(ring, *grad_pieces[0])
    grad_zero, grad_zero_t, sums_one = leave_call(
        grad_normed_one, stream_zero, grad_stream_one, row(first_gain)
    )

    grad_pixels, grad_terms, grad_shifts = None, [None] * groups, [None] * groups
    for turn, g in enumerate(backward):
        if turn > 1:
            wait_for(grad_pixels)
            added = scatter.step(grad_pieces[backward[turn - 1]])
            wait_for(added)
            wait_for(scatter_last.step(made))
        back = lambda: pool_back_call(
            pixels_one,
            pixels_t,
            pair_of(pooled, g),
            pair_of(pieces, g),
            grad_zero,
            grad_zero_t,
            grad_pixels,
            turn == groups - 1,
        )
        if turn == 1:
            wait_for(grad_pixels)
            wait_for(gather_out.beside(scatter_feed.step))
        made, grad_pixels, terms, shifts = back()
        if turn == 0:
            scatter_last = ScatterShared(ring, *made)
        grad_terms[g], grad_shifts[g] = terms, shifts

    def sort_into(places, tensor, back=False):
        same = jnp.stack([jnp.stack([p == i for p in places]) for i in range(narrow_size)])
        same = same.T if back else same
        return jnp.sum(jnp.where(same[:, :, None], tensor[None], 0.0), 1)

    places = ring.places()
    sums_triple = jnp.concatenate(sums_triple, 0).reshape(narrow_size, -1)
    up_bias_row = lax.dynamic_update_slice(
        jnp.zeros((narrow_size, hidden), F32),
        grad_up_bias,
        (0, ring.w * quarter),
    )
    own_sums = jnp.concatenate(
        [
            jnp.concatenate(grad_shifts, 0).reshape(narrow_size, -1),
            sums_triple[:, :local_dim],
            sums_triple[:, 2 * local_dim :],
            jnp.concatenate(grad_terms, 0).reshape(narrow_size, -1),
        ],
        1,
    )
    own_sums = jnp.concatenate([up_bias_row, sort_into(places, own_sums)], 1)
    own_length = own_sums.shape[1]
    shared_sums = jnp.concatenate([sums_one, sums_two], 0)
    all_sums = jnp.concatenate([own_sums.reshape(-1), shared_sums.reshape(-1)]).reshape(-1, 128)
    adder = AddEverywhere(ring, all_sums)
    adder.step()
    adder.step()
    scatter_last.step(made)
    hand_on(grad_pixels, scatter.current)
    scatter_last.step()
    grad_pixels, scatter.current = Gate.handed
    gather_pixels = GatherOwn(ring, grad_pixels, F32)
    finish_last = FinishShared(ring, scatter_last.current)
    finish_last.step()
    finish_last.step()
    grad_pool_output, product = finish_last.finish()
    product = low(product[0, : input_width + VARS])
    products = gather_direct(ring, product)
    scatter.step(grad_pieces[backward[-1]])
    passes = narrow_size // 2 - 1
    for hop in range(passes):
        gather_pixels.after()
        if hop:
            adder.take(gather_pixels.handed[0])
        if adder.pairs:
            adder.send()
        wait_for(gather_pixels.handed[0])
        if hop == 0:
            scatter.step()
            finish = FinishShared(ring, scatter.current)
            (grad_feed_own,) = pass_on([scatter_feed.ahead], gather_pixels.handed[0])
            grad_feed_pieces = ring.gather_wide(grad_feed_own)
        elif finish.bits:
            finish.step()
        else:
            Gate.waits = []
        if hop == passes - 1:
            grad_pool_output, late_product, block_out = pass_on(
                [grad_pool_output, product, gather_out.finish()], gather_pixels.handed[0]
            )
    adder.take()
    while adder.pairs:
        adder.step()
    block_out = block_out.reshape(samples, token_count, model_width)
    grad_first, grad_second = finish.finish()
    grad_feed_up, grad_feed_down = assemble_call(ring.w, grad_feed_pieces)
    grad_variables = gather_pixels.finish().reshape(samples, token_count, input_width)
    grad_triple = jnp.concatenate([grad_first, grad_second[:1]], 0).transpose(1, 0, 2)
    grad_self_output = grad_second[1].T
    grad_pool_output = grad_pool_output[0].T
    grad_pool_value = dot(patch_embed, late_product[:input_width], TN)
    grad_pool_value = grad_pool_value + dot(variable_embed, late_product[input_width:], TN)

    summed = adder.current.reshape(-1)
    own_all = summed[: narrow_size * own_length].reshape(narrow_size, own_length)
    shared_all = summed[narrow_size * own_length :].reshape(-1, model_width)
    grad_first_gain, grad_first_shift, grad_pool_bias = shared_all[:3]
    grad_second_gain, grad_second_shift, grad_down_bias, grad_output_bias = shared_all[3:]
    own = lax.dynamic_index_in_dim(own_all, ring.n, 0, keepdims=False)
    grad_up_bias = own[:hidden]
    grad_value_shift, grad_query_bias, grad_value_bias = own[hidden : hidden + 3 * local_dim].reshape(
        3, local_dim
    )
    terms_start = 3 * local_dim + hidden
    grad_proj = SCALE * own[terms_start:].reshape(heads, -1)
    grad_folded = dot(grad_proj[:, :input_width], patch_embed.astype(F32), precision=highest)
    grad_folded = grad_folded + dot(
        grad_proj[:, input_width:], variable_embed.astype(F32), precision=highest
    )
    query_heads = pool_query.reshape(heads, HEAD_DIM)
    key_heads = pool_key.astype(F32).reshape(model_width, heads, HEAD_DIM)
    grad_pool_key = (grad_folded.T[:, :, None] * query_heads).reshape(model_width, local_dim)
    grad_pool_query = jnp.einsum("dhe,hd->he", key_heads, grad_folded, precision=highest).reshape(
        local_dim
    )
    grad_terms = SCALE * sort_into(places, own_all[:, terms_start:], True)
    wait_for(finish.other, grad_pool_value, grad_feed_up)
    grad_patch, grad_slot = table_call(
        order,
        grad_terms.reshape(narrow_size * heads, -1),
        feed_all,
        products,
        pieces,
    )
    return (
        block_out,
        grad_variables,
        grad_patch,
        grad_slot,
        grad_pool_query,
        grad_pool_key,
        grad_pool_value,
        grad_value_shift,
        grad_pool_output,
        grad_pool_bias,
        grad_first_gain,
        grad_first_shift,
        grad_triple,
        grad_query_bias,
        grad_value_bias,
        grad_self_output,
        grad_output_bias,
        grad_second_gain,
        grad_second_shift,
        grad_feed_up,
        grad_up_bias,
        grad_feed_down,
        grad_down_bias,
    )


def solution(mesh):
    wide_size, narrow_size = mesh.shape["wide"], mesh.shape["narrow"]

    def body(*arrays):
        return on_device(wide_size, narrow_size, *arrays)

    return jax.shard_map(
        body,
        mesh=mesh,
        in_specs=(
            P(None, "wide", None),
            P(),
            P(None, "wide", None),
            P(),
            P(),
            P("narrow"),
            P(None, "narrow"),
            P(None, "narrow"),
            P("narrow"),
            P("narrow", None),
            P(),
            P(),
            P(),
            P(None, None, "narrow"),
            P("narrow"),
            P("narrow"),
            P("narrow", None),
            P(),
            P(),
            P(),
            P(None, "narrow"),
            P("narrow"),
            P("narrow", None),
            P(),
        ),
        out_specs=(
            P(None, "wide", None),
            P(None, "wide", None),
            P(),
            P(),
            P("narrow"),
            P(None, "narrow"),
            P(None, "narrow"),
            P("narrow"),
            P("narrow", None),
            P(),
            P(),
            P(),
            P(None, None, "narrow"),
            P("narrow"),
            P("narrow"),
            P("narrow", None),
            P(),
            P(),
            P(),
            P(None, "narrow"),
            P("narrow"),
            P("narrow", None),
            P(),
        ),
        check_vma=False,
    )
```

```python
import math

import jax
import jax.numpy as jnp
from jax import lax
from jax.experimental import pallas as pl
from jax.experimental.pallas import tpu as pltpu
from jax.sharding import PartitionSpec as P

HEAD_DIM = 64
VARS = 48
PIX = 16
SCALE = HEAD_DIM ** (-0.5)

highest = lax.Precision.HIGHEST
AXES = ("wide", "narrow")
F32 = jnp.float32
BF16 = jnp.bfloat16


def low(tensor):
    return tensor.astype(BF16)


def dot(left, right, dims=((1,), (0,)), precision=None):
    return lax.dot_general(
        left, right, (dims, ((), ())), precision=precision, preferred_element_type=F32
    )


NT = ((1,), (1,))
TN = ((0,), (0,))


def struct(shape, dtype):
    return jax.ShapeDtypeStruct(shape, dtype)


class Gate:
    waits, hands, handed = [], [], []


def wait_for(*arrays):
    Gate.waits += arrays


def hand_on(*arrays):
    Gate.hands += arrays


def whole_block():
    return pl.BlockSpec(memory_space=pltpu.VMEM)


def pallas(
    kernel,
    out_shape,
    grid=(),
    in_specs=None,
    out_specs=None,
    scratch_shapes=(),
    prefetch=0,
    input_output_aliases=None,
    us=1,
    mib=28,
    name=None,
):
    single = not isinstance(out_shape, (list, tuple))
    shapes = [out_shape] if single else list(out_shape)
    if out_specs is None:
        outs = [whole_block() for _ in shapes]
    else:
        outs = [out_specs] if single else list(out_specs)

    def call(*operands):
        waits, hands = Gate.waits, Gate.hands
        Gate.waits, Gate.hands = [], []
        given = len(operands)
        specs = list(in_specs) if in_specs is not None else [whole_block() for _ in operands]
        aliases = dict(input_output_aliases or {})
        aliases |= {given + len(waits) + i: len(shapes) + i for i in range(len(hands))}
        extra = len(waits) + len(hands)

        def body(*refs):
            kept = refs[:given] + refs[given + extra : given + extra + len(shapes)]
            kernel(*kept, *refs[given + extra + len(shapes) + len(hands) :])

        got = pl.pallas_call(
            body,
            grid_spec=pltpu.PrefetchScalarGridSpec(
                num_scalar_prefetch=prefetch,
                grid=grid,
                in_specs=specs + [anywhere() for _ in range(extra)],
                out_specs=outs + [anywhere() for _ in hands],
                scratch_shapes=scratch_shapes,
            ),
            out_shape=shapes + [struct(array.shape, array.dtype) for array in hands],
            input_output_aliases=aliases,
            compiler_params=pltpu.CompilerParams(vmem_limit_bytes=mib << 20),
            cost_estimate=pl.CostEstimate(
                flops=int(us * 1.15e9), bytes_accessed=0, transcendentals=0
            ),
            name=name,
        )(*operands, *waits, *hands)
        Gate.handed = list(got[len(shapes) :])
        return got[0] if single else list(got[: len(shapes)])

    return call


def fixed(shape, *start):
    start = start or (0,) * len(shape)
    return pl.BlockSpec(shape, lambda *_: start)


def per_block(shape, offset=0, *rest):
    rest = rest or (0,) * len(shape)
    return pl.BlockSpec((1,) + shape, lambda n: (n + offset,) + rest)


def anywhere():
    return pl.BlockSpec(memory_space=pl.ANY)


class Ring:
    def __init__(self, wide_size, narrow_size, in_order):
        self.wide, self.narrow, self.sorted = wide_size, narrow_size, in_order
        self.order = list(range(0, narrow_size, 2)) + list(range(1, narrow_size, 2))[::-1]
        place = {device: index for index, device in enumerate(self.order)}
        self.w = lax.axis_index("wide")
        self.n = lax.axis_index("narrow")
        self.core = self.w % 2
        self.pos = jnp.where(self.n % 2 == 0, self.n // 2, narrow_size - 1 - self.n // 2)

        def step(device, hops):
            return self.order[(place[device] + hops) % narrow_size]

        every = [(w, n) for w in range(wide_size) for n in range(narrow_size)]
        flat = lambda w, n: w * narrow_size + n
        bits = lambda size: [1 << i for i in range(size.bit_length() - 1)]
        self.forward = [(flat(w, n), flat(w, step(n, 1))) for w, n in every]
        self.backward = [(flat(w, n), flat(w, step(n, -1))) for w, n in every]
        self.by_core = [(flat(w, n), flat(w, step(n, 1 - 2 * (w % 2)))) for w, n in every]
        self.far_by_core = lambda hops: [
            (flat(w, n), flat(w, step(n, hops * (1 - 2 * (w % 2))))) for w, n in every
        ]
        self.by_core_back = [(dst, src) for src, dst in self.by_core]
        self.wide_swap = {
            bit: [(flat(w, n), flat(w ^ bit, n)) for w, n in every] for bit in bits(wide_size)
        }
        self.narrow_swap = {
            bit: [(flat(w, n), flat(w, n ^ bit)) for w, n in every] for bit in bits(narrow_size)
        }

    def move(self, tensor, pairs):
        return lax.ppermute(tensor, AXES, pairs)

    def swap(self, tensor, bit=1):
        return self.move(tensor, self.wide_swap[bit])

    def at(self, hops):
        index = (self.pos + hops + 2 * self.narrow) % self.narrow
        return jnp.where(2 * index < self.narrow, 2 * index, 2 * (self.narrow - 1 - index) + 1)

    def ordered(self, first, second):
        if not self.sorted:
            return first, second
        pick = lambda a, b: jnp.where(self.core == 0, a, b)
        return pick(first, second), pick(second, first)

    def places(self):
        size = self.narrow
        sign = 1 if self.sorted else jnp.where(self.core == 0, 1, -1)
        order = [self.n, self.at(size // 2)]
        for hops in range(1, size // 2):
            order += [self.at(-sign * hops), self.at(sign * hops)]
        return order

    def scatter_wide(self, parts):
        parts = list(parts)
        for bit in self.wide_swap:
            kept = [index for index in range(self.wide) if index % (2 * bit) == 0]
            moved = [self.swap(parts[index | bit], bit) for index in kept]
            if len(kept) == 1:
                return parts[0], moved[0]
            sums = add_groups([[parts[index], got] for index, got in zip(kept, moved)])
            for index, total in zip(kept, sums):
                parts[index] = total

    def gather_wide(self, block):
        pieces = {0: block}
        for bit in self.wide_swap:
            for shift in list(pieces):
                pieces[shift | bit] = self.swap(pieces[shift], bit)
        return [pieces[shift] for shift in range(self.wide)]


def blank(shape, dtype):
    return pallas(
        lambda o_ref: None,
        out_shape=struct(shape, dtype),
        out_specs=anywhere(),
        us=0.1,
        name="blank",
    )()


def put(out, piece, index):
    return lax.dynamic_update_index_in_dim(out, piece, index, 0)


def add_kernel(groups, *refs):
    refs, outs = refs[: -len(groups)], refs[-len(groups) :]
    for size, out_ref in zip(groups, outs):
        total = refs[0][...].astype(F32)
        for ref in refs[1:size]:
            total = total + ref[...].astype(F32)
        out_ref[...] = low(total)
        refs = refs[size:]


def add_groups(groups):
    first = groups[0][0]
    shape = first[0].shape[1:] if isinstance(first, tuple) else first.shape
    width, size = shape[-1], math.prod(shape)
    rows = size // width
    steps = max(1, size * 2 >> 20)
    specs, flat = [], []
    for item in [item for group in groups for item in group]:
        array, part = item if isinstance(item, tuple) else (item, 0)
        start = part * steps
        specs.append(pl.BlockSpec((rows // steps, width), lambda i, start=start: (start + i, 0)))
        flat.append(array.reshape(-1, width))
    sums = pallas(
        lambda *refs: add_kernel([len(group) for group in groups], *refs),
        grid=(steps,),
        in_specs=specs,
        out_specs=[pl.BlockSpec((rows // steps, width), lambda i: (i, 0))] * len(groups),
        out_shape=[struct((rows, width), BF16)] * len(groups),
        us=2,
        mib=20,
        name="add",
    )(*flat)
    return [total.reshape(shape) for total in sums]


def add_up(*arrays):
    return add_groups([arrays])[0]


def pass_kernel(o_ref):
    o_ref[...] = jnp.zeros_like(o_ref)


def pass_on(arrays, *earlier):
    wait_for(*earlier)
    hand_on(*arrays)
    pallas(pass_kernel, out_shape=struct((8, 128), F32), us=0.5, mib=4, name="pass")()
    return Gate.handed


class GatherShared:
    def __init__(self, ring, block):
        self.ring, self.current, self.own = ring, block, block
        self.pairs, self.far = [], None

    def send(self):
        self.moved = self.ring.move(self.current, self.ring.by_core)

    def take(self, moved):
        ring, self.current = self.ring, moved
        if 2 * (len(self.pairs) + 1) < ring.narrow:
            self.pairs.append(ring.ordered(self.current, ring.swap(self.current)))
            return self.pairs[-1]
        self.far = self.current
        return [self.far]

    def step(self, *earlier):
        self.send()
        return self.take(pass_on([self.moved], *earlier)[0] if earlier else self.moved)

    def finish(self):
        while self.far is None:
            self.step()
        return [self.own, self.far] + [piece for pair in self.pairs for piece in pair]


class ScatterOwn:
    def __init__(self, ring, blocks):
        self.ring, self.blocks, self.hops = ring, blocks, ring.narrow // 2
        self.ahead, self.behind = self.pick(self.hops), None

    def pick(self, hops):
        return lax.dynamic_index_in_dim(self.blocks, self.ring.at(hops), 0, keepdims=False)

    def step(self):
        ring, self.hops = self.ring, self.hops - 1
        ahead = ring.move(self.ahead, ring.backward)
        behind = [] if self.behind is None else [ring.move(self.behind, ring.forward)]
        if not self.hops:
            self.ahead = add_up(ahead, *behind, self.pick(0))
        elif behind:
            self.ahead, self.behind = add_groups(
                [[ahead, self.pick(-self.hops)], [behind[0], self.pick(self.hops)]]
            )
        else:
            self.ahead, self.behind = add_up(ahead, self.pick(-self.hops)), self.pick(self.hops)
        return self.ahead


def gather_direct(ring, block):
    half = ring.narrow // 2
    came = [ring.move(block, ring.far_by_core(hops)) for hops in range(1, half + 1)]
    pairs = [ring.ordered(piece, ring.swap(piece)) for piece in came[:-1]]
    return [block, came[-1]] + [piece for pair in pairs for piece in pair]


class GatherOwn:
    def __init__(self, ring, block, dtype):
        self.ring, self.hops, self.dtype = ring, 0, dtype
        self.moving = [block, block]
        self.out = blank((ring.narrow,) + block.shape, dtype)
        self.out = put(self.out, block.astype(dtype), ring.n)
        self.send()

    def send(self):
        ring, self.hops = self.ring, self.hops + 1
        if 2 * self.hops == ring.narrow:
            half = self.moving[0].shape[0] // 2
            self.moving = [self.moving[0][:half], self.moving[1][half:]]
        ways = (ring.forward, ring.backward)
        self.moving = [ring.move(block, way) for block, way in zip(self.moving, ways)]

    def place(self):
        self.done = 2 * self.hops >= self.ring.narrow
        for side, (block, sign) in enumerate(zip(self.moving, (-1, 1))):
            index = self.ring.at(sign * self.hops)
            start = side * block.shape[0] if self.done else 0
            block = block.astype(self.dtype)[None]
            self.out = lax.dynamic_update_slice(self.out, block, (index, start, 0))
        if not self.done:
            self.send()

    def beside(self, kernel):
        hand_on(*self.moving)
        got = kernel()
        self.moving = list(Gate.handed)
        self.place()
        return got

    def after(self, *earlier):
        self.moving = self.handed = list(pass_on(self.moving, *earlier))
        self.place()

    def finish(self):
        while not self.done:
            self.place()
        return self.out


class ScatterShared:
    def __init__(self, ring, own, far):
        self.ring, self.own, self.current, self.got = ring, own, far, far

    def step(self, pair=None):
        ring = self.ring
        moved = ring.move(self.current, ring.by_core_back)
        if pair:
            first, second = ring.ordered(*pair)
            self.current = add_up(moved, first, ring.swap(second))
        else:
            self.current = add_up(moved, self.own)
        return self.current


class FinishShared:
    def __init__(self, ring, partial):
        self.ring, half = ring, partial.shape[0] // 2
        cut = lambda side: lax.dynamic_slice_in_dim(partial, side * half, half, 0)
        self.current, self.theirs = cut(ring.core), cut(1 - ring.core)
        self.bits = list(ring.wide_swap)

    def step(self):
        ring, bit = self.ring, self.bits.pop(0)
        sent = self.theirs if bit == 1 else self.current
        self.current = add_up(self.current, ring.swap(sent, bit))
        return self.current

    def finish(self):
        while self.bits:
            self.step()
        self.other = other = self.ring.swap(self.current)
        first = jnp.where(self.ring.core == 0, self.current, other).astype(F32)
        second = jnp.where(self.ring.core == 0, other, self.current).astype(F32)
        return first, second


class AddEverywhere:
    def __init__(self, ring, tensor):
        self.ring, self.current = ring, tensor
        self.pairs = list(ring.wide_swap.values()) + list(ring.narrow_swap.values())

    def send(self):
        self.moved = self.ring.move(self.current, self.pairs.pop(0))

    def take(self, *earlier):
        moved = pass_on([self.moved], *earlier)[0] if earlier else self.moved
        self.current = self.current + moved

    def step(self):
        self.send()
        self.take()

    def finish(self):
        while self.pairs:
            self.step()
        return self.current


def split_three(tensor):
    top = low(tensor)
    rest = tensor - top.astype(F32)
    middle = low(rest)
    return top, middle, low(rest - middle.astype(F32))


def lanes_to_rows(vector, cols):
    length = vector.shape[1]
    count = -(-length // cols)
    if count * cols > length:
        vector = jnp.concatenate([vector, jnp.zeros((1, count * cols - length), F32)], 1)
    return jnp.concatenate([vector[:, i * cols : (i + 1) * cols] for i in range(count)], 0)


def rows_to_lanes(rows, start, length):
    count = -(-length // rows.shape[1])
    return jnp.concatenate([rows[start + i : start + i + 1] for i in range(count)], 1)[:, :length]


class Extra:
    def __init__(self, cols, depth):
        self.heads, self.full = cols // HEAD_DIM, VARS * PIX + VARS
        self.term_rows, self.fold_rows = -(-self.full // cols), depth // cols
        self.fold_start = 3 * self.heads * self.term_rows
        self.bias_start = self.fold_start + 2 * self.heads * self.fold_rows

    def term(self, rows, part, head):
        return rows_to_lanes(rows, (part * self.heads + head) * self.term_rows, self.full)

    def folded(self, rows, head):
        place = lambda part: self.fold_start + (part * self.heads + head) * self.fold_rows
        length = self.fold_rows * rows.shape[1]
        return rows_to_lanes(rows, place(0), length) + rows_to_lanes(rows, place(1), length)

    def bias(self, rows, index):
        parts = [rows[self.bias_start + 3 * i + index :][:1] for i in range(3)]
        return parts[0] + (parts[1] + parts[2])


def prepare_kernel(
    key_ref, query_ref, table_ref, value_ref, output_ref, triple_ref, bias_ref, o_ref
):
    depth, cols = key_ref.shape
    extra = Extra(cols, depth)
    heads, full = extra.heads, extra.full
    keys, table = key_ref[...], table_ref[...]
    lane = lax.broadcasted_iota(jnp.int32, (8, cols), 1)
    row = lax.broadcasted_iota(jnp.int32, (8, cols), 0)
    masked = jnp.where(lane // HEAD_DIM == row, query_ref[...], 0.0)
    folded = sum(dot(part, keys, NT) for part in split_three(masked)[::-1])
    folded_parts = split_three(folded)
    terms = sum(dot(part, table, NT) for part in folded_parts[::-1]) * SCALE
    rows = [
        lanes_to_rows(part[h : h + 1, :full].astype(F32), cols)
        for part in split_three(terms)
        for h in range(heads)
    ]
    rows += [
        lanes_to_rows(part[h : h + 1].astype(F32), cols)
        for part in folded_parts[:2]
        for h in range(heads)
    ]
    rows += [lanes_to_rows(part.astype(F32), cols) for part in split_three(bias_ref[...])]
    rows.append(jnp.zeros((depth - full - sum(part.shape[0] for part in rows), cols), F32))
    o_ref[:3] = triple_ref[...]
    o_ref[3] = output_ref[...].astype(F32).T.astype(BF16)
    o_ref[4, :full] = low(dot(table, value_ref[...])[:full])
    o_ref[4, full:] = low(jnp.concatenate(rows, 0))


def prepare_call(keys, query, table, values, output, triple, bias):
    depth, cols = keys.shape
    return pallas(
        prepare_kernel,
        out_shape=struct((5, depth, cols), BF16),
        us=5.7,
        mib=40,
        name="prepare",
    )(keys, query, table, values, output, triple, bias)


def stage_kernel(up_ref, down_ref, value_ref, bias_ref, o_ref):
    depth, hidden = up_ref.shape
    cols = value_ref.shape[1]
    flip = lambda ref: ref[...].astype(F32).T.astype(BF16)
    o_ref[:cols] = flip(value_ref)
    o_ref[cols : cols + hidden] = flip(up_ref)
    o_ref[cols + hidden : cols + 2 * hidden] = down_ref[...]
    parts = [part.astype(F32) for part in split_three(bias_ref[...])]
    block = jnp.concatenate(parts + [jnp.zeros((13, hidden), F32)], 0)
    if hidden < depth:
        block = jnp.concatenate([block, jnp.zeros((16, depth - hidden), F32)], 1)
    o_ref[cols + 2 * hidden :] = low(block)


def stage_call(up, down, value, bias):
    depth, hidden = up.shape
    return pallas(
        stage_kernel,
        out_shape=struct((value.shape[1] + 2 * hidden + 16, depth), BF16),
        us=2,
        mib=40,
        name="stage",
    )(up, down, value, bias)


def arrange_kernel(x_ref, x1_ref, xt_ref):
    pixels = x_ref[...]
    x1_ref[...] = jnp.concatenate([pixels, jnp.ones((pixels.shape[0], VARS), BF16)], 1)
    xt_ref[...] = pixels.astype(F32).T.astype(BF16)


def arrange_call(pixels):
    tokens, width = pixels.shape
    return pallas(
        arrange_kernel,
        out_shape=[
            struct((tokens, width + VARS), BF16),
            struct((width, tokens), BF16),
        ],
        us=3.3,
        mib=40,
        name="arrange",
    )(pixels)


def slot_mask():
    slot = lax.broadcasted_iota(jnp.int32, (VARS, VARS * PIX + VARS), 0)
    column = lax.broadcasted_iota(jnp.int32, (VARS, VARS * PIX + VARS), 1)
    return slot == jnp.where(column < VARS * PIX, column // PIX, column - VARS * PIX)


def mix(weights, pixels_wide):
    tokens = weights.shape[1]
    spread = weights[:, None, :] * pixels_wide
    return jnp.concatenate([low(spread.reshape(VARS * PIX, tokens)), low(weights)], 0)


def pool_kernel(count, x_ref, xt_ref, valid_ref, *refs):
    p_refs, w_refs, o_refs = refs[:count], refs[count : 2 * count], refs[2 * count :]
    tokens, width = x_ref.shape
    pixels = x_ref[...]
    pixels_wide = xt_ref[...].astype(F32).reshape(VARS, PIX, tokens)
    valid = valid_ref[...] > 0
    mask = slot_mask()
    for p_ref, w_ref, o_ref in zip(p_refs, w_refs, o_refs):
        _, depth, cols = p_ref.shape
        extra = Extra(cols, depth)
        rows = p_ref[0, width:].astype(F32)
        table_value = p_ref[0, :width].astype(F32).T.astype(BF16)
        parts = []
        for h in range(extra.heads):
            scores = jnp.zeros((VARS, tokens), F32)
            for part in (2, 1, 0):
                spread = low(jnp.where(mask, extra.term(rows, part, h), 0.0))
                scores = scores + dot(spread, pixels, NT)
            scores = jnp.where(valid, scores, -1e30)
            weights = jnp.exp(scores - jnp.max(scores, 0, keepdims=True))
            weights = weights / jnp.sum(weights, 0, keepdims=True)
            w_ref[h] = weights
            mixed = mix(weights, pixels_wide)
            parts.append(dot(table_value[h * HEAD_DIM : (h + 1) * HEAD_DIM], mixed))
        pooled = jnp.concatenate(parts, 0) if len(parts) > 1 else parts[0]
        o_ref[...] = low(pooled.T + extra.bias(rows, 0))


def slot_of(piece, first, count=1):
    return fixed((count,) + piece.shape[1:], first // count, 0, 0)


def pool_call(pixels, pixels_t, valid, pieces):
    tokens = pixels.shape[0]
    cols = pieces[0].shape[2]
    count = len(pieces)
    weights, pooled = (cols // HEAD_DIM, VARS, tokens), (tokens, cols)
    got = pallas(
        lambda *refs: pool_kernel(count, *refs),
        grid=(1,),
        in_specs=[fixed(pixels.shape), fixed(pixels_t.shape), fixed((VARS, 1))]
        + [slot_of(piece, 4) for piece in pieces],
        out_specs=[fixed(weights)] * count + [fixed(pooled)] * count,
        out_shape=[struct(weights, F32)] * count + [struct(pooled, BF16)] * count,
        us=7,
        mib=40,
        name="pool",
    )(pixels, pixels_t, valid, *pieces)
    return list(zip(got[:count], got[count:]))


def pool_back_kernel(count, first, last, x_ref, xt_ref, g_ref, gt_ref, *refs):
    groups = [refs[i * count : (i + 1) * count] for i in range(4)]
    rest = refs[4 * count :]
    if not first:
        before_ref, rest = rest[0], rest[1:]
    pack_refs, (gx_ref, terms_ref, shift_ref) = rest[:count], rest[count:]
    tokens, full = x_ref.shape
    width = VARS * PIX
    pixels = x_ref[...]
    pixels_wide = xt_ref[...].astype(F32).reshape(VARS, PIX, tokens)
    mask = slot_mask()
    total = jnp.zeros((width, tokens), F32) if first else before_ref[...]
    for index, (v_ref, out_ref, w_ref, p_ref) in enumerate(zip(*groups)):
        _, depth, cols = v_ref.shape
        extra = Extra(cols, depth)
        rows = v_ref[0, full:].astype(F32)
        grads = low(dot(g_ref[...], out_ref[0]))
        shift_ref[index] = jnp.sum(grads.astype(F32), 0, keepdims=True)
        lane = lax.broadcasted_iota(jnp.int32, grads.shape, 1)
        table_value = v_ref[0, :full]
        product = jnp.zeros((full, cols), F32)
        for h in range(extra.heads):
            weights = w_ref[h]
            own = jnp.where(lane // HEAD_DIM == h, grads, 0) if extra.heads > 1 else grads
            grad_mixed = dot(table_value, own, NT)
            grad_wide = grad_mixed[:width].reshape(VARS, PIX, tokens)
            grad_weights = jnp.sum(grad_wide * pixels_wide, 1) + grad_mixed[width:]
            inner = jnp.sum(weights * grad_weights, 0, keepdims=True)
            grad_scores = weights * (grad_weights - inner)
            product = product + dot(mix(weights, pixels_wide), own)
            total = total + (weights[:, None, :] * grad_wide).reshape(width, tokens)
            gs_top = low(grad_scores)
            gs_rest = low(grad_scores - gs_top.astype(F32))
            top, middle = [
                low(jnp.where(mask, extra.term(rows, part, h), 0.0))[:, :width] for part in (0, 1)
            ]
            stacked = jnp.concatenate([top, top, middle], 0)
            total = total + dot(stacked, jnp.concatenate([gs_top, gs_rest, gs_top], 0), TN)
            both = dot(jnp.concatenate([gs_top, gs_rest], 0), pixels)
            by_slot = jnp.where(mask, both[:VARS] + both[VARS:], 0.0)
            terms_ref[index, h : h + 1, :] = jnp.sum(by_slot, 0, keepdims=True)
        pack_ref = pack_refs[index]
        pack_ref[0] = low(dot(gt_ref[...], p_ref[...]))
        pack_ref[1, :full] = low(product)
        pack_ref[1, full:] = jnp.zeros((depth - full, cols), BF16)
    gx_ref[...] = low(total.T) if last else total


def pool_back_call(pixels, pixels_t, heads, pieces, grads, grads_t, before, last):
    count = len(pieces)
    tokens, full = pixels.shape
    width = pixels_t.shape[0]
    _, depth, cols = pieces[0].shape
    in_specs = [fixed(array.shape) for array in (pixels, pixels_t, grads, grads_t)]
    in_specs += [slot_of(piece, 4) for piece in pieces] + [slot_of(piece, 3) for piece in pieces]
    in_specs += [fixed(head[0].shape) for head in heads] + [fixed(head[1].shape) for head in heads]
    operands = [pixels, pixels_t, grads, grads_t, *pieces, *pieces]
    operands += [head[0] for head in heads] + [head[1] for head in heads]
    if before is not None:
        in_specs.append(fixed((width, tokens)))
        operands.append(before)
    shapes = [struct((2, depth, cols), BF16)] * count
    shapes.append(struct((tokens, width), BF16) if last else struct((width, tokens), F32))
    shapes.append(struct((count, cols // HEAD_DIM, full), F32))
    shapes.append(struct((count, 1, cols), F32))
    got = pallas(
        lambda *refs: pool_back_kernel(count, before is None, last, *refs),
        grid=(1,),
        in_specs=in_specs,
        out_specs=[fixed(shape.shape) for shape in shapes],
        out_shape=shapes,
        us=21,
        name="pool_back",
    )(*operands)
    return list(got[:count]), *got[count:]


def normalise(stream):
    centered = stream - jnp.mean(stream, -1, keepdims=True)
    scale = lax.rsqrt(jnp.mean(centered * centered, -1, keepdims=True) + 1e-05)
    return centered * scale, scale


def normalise_back(grad, stream, gain):
    hat, scale = normalise(stream)
    through = grad * gain
    inner = through - jnp.mean(through, -1, keepdims=True)
    inner = inner - hat * jnp.mean(through * hat, -1, keepdims=True)
    add = lambda tensor: jnp.sum(tensor, 0, keepdims=True)
    return scale * inner, add(grad * hat), add(grad)


def enter_kernel(count, *refs):
    p_refs, w_refs = refs[:count], refs[count : 2 * count]
    bias_ref, gain_ref, shift_ref, s_ref, x_ref, xt_ref = refs[2 * count :]
    stream = jnp.zeros(s_ref.shape, F32) + bias_ref[...]
    for p_ref, w_ref in zip(p_refs, w_refs):
        stream = stream + dot(p_ref[...], w_ref[0], NT)
    s_ref[...] = stream
    hat, _ = normalise(stream)
    rows = hat * gain_ref[...] + shift_ref[...]
    x_ref[...] = low(rows)
    xt_ref[...] = low(rows.T)


def enter_call(pooled, pieces, bias, gain, shift):
    tokens = pooled[0].shape[0]
    depth = pieces[0].shape[1]
    row = fixed((1, depth))
    return pallas(
        lambda *refs: enter_kernel(len(pieces), *refs),
        grid=(1,),
        in_specs=[fixed(part.shape) for part in pooled]
        + [slot_of(piece, 3) for piece in pieces]
        + [row, row, row],
        out_specs=[fixed((tokens, depth)), fixed((tokens, depth)), fixed((depth, tokens))],
        out_shape=[
            struct((tokens, depth), F32),
            struct((tokens, depth), BF16),
            struct((depth, tokens), BF16),
        ],
        us=7,
        mib=56,
        name="enter",
    )(*pooled, *pieces, bias, gain, shift)


def beside(ref):
    return jnp.concatenate([ref[i] for i in range(3)], 1)


def project_kernel(count, x_ref, *refs):
    w_refs, e_refs, q_refs = refs[:count], refs[count : 2 * count], refs[2 * count : -1]
    kv_ref = refs[-1]
    for index, (w_ref, e_ref) in enumerate(zip(w_refs, e_refs)):
        _, depth, cols = w_ref.shape
        extra = Extra(cols, depth)
        rows = e_ref[0, extra.full :].astype(F32)
        triple = dot(x_ref[...], beside(w_ref))
        q_refs[index // 2][index % 2] = low(triple[:, :cols] + extra.bias(rows, 1))
        kv_ref[index, 0] = low(triple[:, cols : 2 * cols])
        kv_ref[index, 1] = low(triple[:, 2 * cols :] + extra.bias(rows, 2))


def project_call(rows, pieces):
    count = len(pieces)
    cols = pieces[0].shape[2]
    tokens = rows.shape[0]
    shapes = [struct((2, tokens, cols), BF16)] * (count // 2)
    shapes.append(struct((count, 2, tokens, cols), BF16))
    got = pallas(
        lambda *refs: project_kernel(count, *refs),
        grid=(1,),
        in_specs=[fixed(rows.shape)]
        + [slot_of(piece, 0, 3) for piece in pieces]
        + [slot_of(piece, 4) for piece in pieces],
        out_specs=[fixed(shape.shape) for shape in shapes],
        out_shape=shapes,
        us=1.2 * count,
        mib=40,
        name="project",
    )(rows, *pieces, *pieces)
    return got[:-1], got[-1]


def project_back_kernel(count, first, xt_ref, gq_ref, gkv_ref, *refs):
    w_refs, rest = refs[:count], refs[2 * count :]
    if not first:
        before_ref, rest = rest[0], rest[1:]
    gw_refs, (gx_ref, sums_ref) = rest[:count], rest[count:]
    cols = gq_ref.shape[2]
    total = jnp.zeros(gx_ref.shape, F32) if first else before_ref[...]
    for index, (w_ref, gw_ref) in enumerate(zip(w_refs, gw_refs)):
        grads = jnp.concatenate([gq_ref[index], gkv_ref[index, 0], gkv_ref[index, 1]], 1)
        total = total + dot(grads, beside(w_ref), NT)
        products = low(dot(xt_ref[...], grads))
        for i in range(3):
            gw_ref[i] = products[:, i * cols : (i + 1) * cols]
        sums_ref[index] = jnp.sum(grads.astype(F32), 0, keepdims=True)
    gx_ref[...] = total


def project_back_call(rows_t, pieces, grad_query, grad_pair, grad_pieces, before):
    count = len(pieces)
    depth, tokens = rows_t.shape
    cols = pieces[0].shape[2]
    in_specs = [fixed(array.shape) for array in (rows_t, grad_query, grad_pair)]
    in_specs += [slot_of(piece, 0, 3) for piece in pieces] + [anywhere()] * count
    operands = [rows_t, grad_query, grad_pair, *pieces, *grad_pieces]
    if before is not None:
        in_specs.append(fixed((tokens, depth)))
        operands.append(before)
    shapes = [struct(piece.shape, BF16) for piece in grad_pieces]
    shapes += [struct((tokens, depth), F32), struct((count, 1, 3 * cols), F32)]
    got = pallas(
        lambda *refs: project_back_kernel(count, before is None, *refs),
        grid=(1,),
        in_specs=in_specs,
        out_specs=[slot_of(piece, 0, 3) for piece in grad_pieces]
        + [fixed(shape.shape) for shape in shapes[count:]],
        out_shape=shapes,
        input_output_aliases={3 + count + i: i for i in range(count)},
        us=13.6,
        name="project_back",
    )(*operands)
    return list(got[:count]), *got[count:]


def leave_kernel(g_ref, s_ref, before_ref, gain_ref, o_ref, ot_ref, sums_ref):
    through, gain, shift = normalise_back(g_ref[...], s_ref[...], gain_ref[...])
    total = before_ref[...] + through
    rounded = low(total)
    o_ref[...] = rounded
    ot_ref[...] = low(total.T)
    bias = jnp.sum(rounded.astype(F32), 0, keepdims=True)
    sums_ref[...] = jnp.concatenate([gain, shift, bias], 0)


def leave_call(grad_normed, stream, before, gain):
    tokens, depth = stream.shape
    return pallas(
        leave_kernel,
        out_shape=[
            struct((tokens, depth), BF16),
            struct((depth, tokens), BF16),
            struct((3, depth), F32),
        ],
        us=12,
        name="leave",
    )(grad_normed, stream, before, gain)


def attend_kernel(count, q_ref, *refs):
    sources, (o_ref, total_ref) = refs[:count], refs[count:]
    cols = q_ref.shape[2]
    heads = cols // HEAD_DIM
    scaled = q_ref[0] * SCALE
    lane = lax.broadcasted_iota(jnp.int32, scaled.shape, 1)
    values_t = [source[0, 1].T for source in sources]
    parts = []
    for h in range(heads):
        own = jnp.where(lane // HEAD_DIM == h, scaled, 0) if heads > 1 else scaled
        logits = [dot(source[0, 0], own, NT) for source in sources]
        peak = jnp.max(logits[0], 0, keepdims=True)
        for piece in logits[1:]:
            peak = jnp.maximum(peak, jnp.max(piece, 0, keepdims=True))
        norm = jnp.zeros_like(peak)
        out = jnp.zeros((HEAD_DIM, peak.shape[1]), F32)
        for piece, value in zip(logits, values_t):
            weight = jnp.exp(piece - peak)
            norm = norm + jnp.sum(weight, 0, keepdims=True)
            out = out + dot(value[h * HEAD_DIM : (h + 1) * HEAD_DIM], low(weight))
        parts.append(out / norm)
        total_ref[0, h] = peak + jnp.log(norm)
    full = jnp.concatenate(parts, 0) if heads > 1 else parts[0]
    o_ref[0] = full.T


def pair_spec(shape, flip, start=0):
    place = lambda n: (start + (1 - n if flip else n),) + (0,) * len(shape)
    return pl.BlockSpec((1,) + shape, place)


def attend_call(queries, sources, flips, start):
    count, tokens, cols = queries.shape
    heads = cols // HEAD_DIM
    keys = sum(array.shape[2] for array in sources)
    work = count * tokens * keys * cols
    return pallas(
        lambda *refs: attend_kernel(len(sources), *refs),
        grid=(count,),
        in_specs=[per_block((tokens, cols))]
        + [pair_spec(array.shape[1:], flip, start) for array, flip in zip(sources, flips)],
        out_specs=[per_block((tokens, cols)), per_block((heads, 1, tokens))],
        out_shape=[
            struct((count, tokens, cols), F32),
            struct((count, heads, 1, tokens), F32),
        ],
        us=8.7,
        name="attend",
    )(queries, *sources)


def middle_kernel(count, s_ref, *refs):
    o_refs, w_refs = refs[:count], refs[count : 3 * count]
    bias_ref, gain_ref, shift_ref, s1_ref, x_ref, xt_ref = refs[3 * count :]
    stream = s_ref[...] + bias_ref[...]
    for index, w_ref in enumerate(w_refs):
        stream = stream + dot(low(o_refs[index // 2][index % 2]), w_ref[...])
    s1_ref[...] = stream
    hat, _ = normalise(stream)
    rows = hat * gain_ref[...] + shift_ref[...]
    x_ref[...] = low(rows)
    xt_ref[...] = low(rows.T)


def middle_call(stream, attended, weights, bias, gain, shift):
    tokens, depth = stream.shape
    operands = [stream, *attended, *weights, bias, gain, shift]
    shapes = [
        struct((tokens, depth), F32),
        struct((tokens, depth), BF16),
        struct((depth, tokens), BF16),
    ]
    return pallas(
        lambda *refs: middle_kernel(len(attended), *refs),
        grid=(1,),
        in_specs=[fixed(array.shape) for array in operands],
        out_specs=[fixed(shape.shape) for shape in shapes],
        out_shape=shapes,
        us=5,
        mib=40,
        name="middle",
    )(*operands)


def middle_back_kernel(g_ref, gt_ref, o_ref, wa_ref, wb_ref, go_ref, delta_ref, ga_ref, gb_ref):
    _, tokens, cols = o_ref.shape
    heads = cols // HEAD_DIM
    lane = lax.broadcasted_iota(jnp.int32, (8, cols), 1)
    row = lax.broadcasted_iota(jnp.int32, (8, cols), 0)
    mask = jnp.where(lane // HEAD_DIM == row, 1.0, 0.0)
    for index, (w_ref, gw_ref) in enumerate(((wa_ref, ga_ref), (wb_ref, gb_ref))):
        grads = low(dot(g_ref[...], w_ref[...], NT))
        go_ref[index] = grads
        attended = o_ref[index]
        gw_ref[0] = low(dot(gt_ref[...], low(attended)))
        sums = dot(mask, grads.astype(F32) * attended, NT, precision=highest)
        for h in range(heads):
            delta_ref[index, h] = sums[h : h + 1]


def middle_back_call(grads, grads_t, attended, weights):
    count, tokens, cols = attended.shape
    depth = grads.shape[1]
    heads = cols // HEAD_DIM
    piece = struct((4, depth, cols), BF16)
    operands = [grads, grads_t, attended, *weights]
    return pallas(
        middle_back_kernel,
        grid=(1,),
        in_specs=[fixed(array.shape) for array in operands],
        out_specs=[fixed(attended.shape), fixed((count, heads, 1, tokens))]
        + [slot_of(piece, 3)] * 2,
        out_shape=[
            struct(attended.shape, BF16),
            struct((count, heads, 1, tokens), F32),
            piece,
            piece,
        ],
        us=4,
        name="middle_back",
    )(*operands)


def attend_back_kernel(count, first, last, together, q_ref, g_ref, total_ref, delta_ref, *refs):
    sources, rest = refs[:count], refs[count:]
    before_ref, gq_ref, targets = (
        (None, rest[0], rest[1:]) if first else (rest[0], rest[1], rest[2:])
    )
    if together:
        targets = [targets[0].at[i] for i in range(count)]
    cols = q_ref.shape[2]
    heads = cols // HEAD_DIM
    scaled = q_ref[0] * SCALE
    grads = g_ref[0]
    lane = lax.broadcasted_iota(jnp.int32, scaled.shape, 1)
    pick = lambda tensor, h: jnp.where(lane // HEAD_DIM == h, tensor, 0) if heads > 1 else tensor
    own_q = [pick(scaled, h) for h in range(heads)]
    own_g = [pick(grads, h) for h in range(heads)]
    queries_t = [jnp.zeros((HEAD_DIM, scaled.shape[0]), F32) for h in range(heads)]
    for source, target in zip(sources, targets):
        keys, values = source[0, 0], source[0, 1]
        keys_t = keys.T
        grad_keys = jnp.zeros(keys.shape, F32)
        grad_values = jnp.zeros(keys.shape, F32)
        for h in range(heads):
            weight = jnp.exp(dot(keys, own_q[h], NT) - total_ref[0, h])
            grad_weight = dot(values, own_g[h], NT)
            grad_logit = low(weight * (grad_weight - delta_ref[0, h]))
            grad_values = grad_values + dot(low(weight), own_g[h])
            grad_keys = grad_keys + dot(grad_logit, own_q[h])
            queries_t[h] = queries_t[h] + dot(
                keys_t[h * HEAD_DIM : (h + 1) * HEAD_DIM], grad_logit
            )
        target[0, 0] = low(grad_keys)
        target[0, 1] = low(grad_values)
    full = jnp.concatenate(queries_t, 0) if heads > 1 else queries_t[0]
    if before_ref is not None:
        full = full + before_ref[0]
    gq_ref[0] = low(full * SCALE).T if last else full


def attend_back_call(queries, grads, totals, deltas, sources, flips, start, before, last, together):
    count, tokens, cols = queries.shape
    heads = cols // HEAD_DIM
    keys = sum(array.shape[2] for array in sources)
    work = count * tokens * keys * cols
    block = sources[0].shape[1:]
    first = before is None
    outs = [pair_spec(block, flip) for flip in flips]
    shapes = [struct((count,) + block, BF16) for _ in sources]
    if together:
        flip = flips[0]
        place = lambda n: (0, 1 - n if flip else n) + (0,) * len(block)
        outs = [pl.BlockSpec((len(sources), 1) + block, place)]
        shapes = [struct((len(sources), count) + block, BF16)]
    result = struct((count, tokens, cols), BF16) if last else struct((count, cols, tokens), F32)
    return pallas(
        lambda *refs: attend_back_kernel(len(sources), first, last, together, *refs),
        grid=(count,),
        in_specs=[
            per_block((tokens, cols)),
            per_block((tokens, cols)),
            per_block((heads, 1, tokens)),
            per_block((heads, 1, tokens)),
        ]
        + [pair_spec(block, flip, start) for flip in flips]
        + ([] if first else [per_block((cols, tokens))]),
        out_specs=[per_block(result.shape[1:])] + outs,
        out_shape=[result] + shapes,
        us=15.2,
        name="attend_back",
    )(queries, grads, totals, deltas, *sources, *([] if first else [before]))


def feed_parts(w_ref, cols):
    hidden = (w_ref.shape[1] - 16 - cols) // 2
    rows_of = lambda start: jnp.concatenate([w_ref[i, start : start + hidden] for i in range(2)], 0)
    bias = []
    for i in range(2):
        rows = w_ref[i, cols + 2 * hidden :, :hidden].astype(F32)
        bias.append(rows[0:1] + (rows[1:2] + rows[2:3]))
    return rows_of(cols), rows_of(cols + hidden), jnp.concatenate(bias, 1)


def gate_of(before):
    return 0.5 * (1.0 + lax.erf(before * 0.7071067811865476))


def feed_kernel(cols, x_ref, w_ref, y_ref, y_sum):
    step = pl.program_id(0)
    up, down, bias = feed_parts(w_ref, cols)
    before = dot(x_ref[...], up, NT) + bias
    part = dot(low(before * gate_of(before)), down)

    @pl.when(step == 0)
    def _():
        y_sum[...] = part

    @pl.when(step > 0)
    def _():
        y_sum[...] += part

    @pl.when(step == pl.num_programs(0) - 1)
    def _():
        y_ref[...] = low(y_sum[...])


def feed_call(cols, rows, staged):
    whole = fixed(rows.shape)
    return pallas(
        lambda *refs: feed_kernel(cols, *refs),
        grid=(staged.shape[0] // 2,),
        in_specs=[whole, pl.BlockSpec((2,) + staged.shape[1:], lambda n: (n, 0, 0))],
        out_specs=whole,
        out_shape=struct(rows.shape, BF16),
        scratch_shapes=[pltpu.VMEM(rows.shape, F32)],
        us=4,
        mib=40,
        name="feed",
    )(rows, staged)


def feed_back_kernel(first, cols, x_ref, g_ref, w_ref, *refs):
    if not first:
        before_ref, refs = refs[0], refs[1:]
    gx_ref, gb_ref, gw_ref, gx_sum = refs
    step = pl.program_id(0)
    up, down, bias = feed_parts(w_ref, cols)
    hidden = up.shape[0] // 2
    rows, grads = x_ref[...], g_ref[...]
    before = dot(rows, up, NT) + bias
    bell = gate_of(before)
    active = low(before * bell)
    slope = bell + before * (0.3989422804014327 * jnp.exp(-0.5 * before * before))
    grad_hidden = low(slope * dot(grads, down, NT))
    part_sum = dot(grad_hidden, up)
    grad_up = dot(grad_hidden, rows, TN)
    grad_down = dot(active, grads, TN)
    gb_ref[0] = jnp.sum(grad_hidden.astype(F32), 0, keepdims=True)
    for i in range(2):
        part = slice(i * hidden, (i + 1) * hidden)
        made = jnp.concatenate([grad_up[part], grad_down[part]], 0)
        made = made if first else made + before_ref[i].astype(F32)
        gw_ref[i] = low(made)

    @pl.when(step == 0)
    def _():
        gx_sum[...] = part_sum

    @pl.when(step > 0)
    def _():
        gx_sum[...] += part_sum

    @pl.when(step == pl.num_programs(0) - 1)
    def _():
        gx_ref[...] = low(gx_sum[...])


def feed_back_call(cols, rows, grads, staged, before):
    count, lines, depth = staged.shape
    lines = lines - 16 - cols
    whole = fixed(rows.shape)
    pair = pl.BlockSpec((2, lines, depth), lambda n: (n, 0, 0))
    first = before is None
    return pallas(
        lambda *refs: feed_back_kernel(first, cols, *refs),
        grid=(count // 2,),
        in_specs=[whole, whole, pl.BlockSpec((2,) + staged.shape[1:], lambda n: (n, 0, 0))]
        + ([] if first else [pair]),
        out_specs=[whole, pl.BlockSpec((1, 1, lines), lambda n: (n, 0, 0)), pair],
        out_shape=[
            struct(rows.shape, BF16),
            struct((count // 2, 1, lines), F32),
            struct((count, lines, depth), BF16),
        ],
        scratch_shapes=[pltpu.VMEM(rows.shape, F32)],
        us=9,
        mib=40,
        name="feed_back",
    )(rows, grads, staged, *([] if first else [before]))


def turn_kernel(count, *refs):
    g_ref, s_ref, gain_ref, gs_ref, g1_ref, g1t_ref, sums_ref = refs[count:]
    grad = refs[0][...].astype(F32)
    for ref in refs[1:count]:
        grad = grad + ref[...].astype(F32)
    through, gain, shift = normalise_back(grad, s_ref[...], gain_ref[...])
    grads = g_ref[...].astype(F32)
    total = grads + through
    gs_ref[...] = total
    rounded = low(total)
    g1_ref[...] = rounded
    g1t_ref[...] = low(total.T)
    add = lambda tensor: jnp.sum(tensor, 0, keepdims=True)
    sums_ref[...] = jnp.concatenate([gain, shift, add(grads), add(rounded.astype(F32))], 0)


def turn_call(parts, grads, stream, gain):
    tokens, depth = stream.shape
    return pallas(
        lambda *refs: turn_kernel(len(parts), *refs),
        out_shape=[
            struct((tokens, depth), F32),
            struct((tokens, depth), BF16),
            struct((depth, tokens), BF16),
            struct((4, depth), F32),
        ],
        us=8,
        name="turn",
    )(*parts, grads, stream, gain)


def assemble_kernel(w_ref, *refs):
    pieces, (up_ref, down_ref) = refs[:-2], refs[-2:]
    hidden = pieces[0].shape[0] // 2
    for index, piece in enumerate(pieces):

        @pl.when(pl.program_id(0) == index)
        def _():
            up_ref[...] = piece[:hidden].astype(F32).T
            down_ref[...] = piece[hidden:].astype(F32)


def assemble_call(w, pieces):
    count = len(pieces)
    lines, depth = pieces[0].shape
    hidden = lines // 2
    direct = hidden % 128 == 0
    up_place = (
        (lambda i, w_ref: (0, w_ref[0] ^ i)) if direct else (lambda i, w_ref: (w_ref[0] ^ i, 0))
    )
    up, down = pallas(
        assemble_kernel,
        prefetch=1,
        grid=(count,),
        in_specs=[pl.BlockSpec((lines, depth), lambda i, w_ref: (0, 0)) for _ in pieces],
        out_specs=[
            pl.BlockSpec((depth, hidden), up_place),
            pl.BlockSpec((hidden, depth), lambda i, w_ref: (w_ref[0] ^ i, 0)),
        ],
        out_shape=[
            struct((depth, count * hidden) if direct else (count * depth, hidden), F32),
            struct((count * hidden, depth), F32),
        ],
        us=3.3,
        name="assemble",
    )(w.reshape(1), *pieces)
    if not direct:
        up = up.reshape(count, depth, hidden).transpose(1, 0, 2).reshape(depth, count * hidden)
    return up, down


def table_kernel(count, order_ref, terms_ref, v_ref, *refs):
    p_refs, e_refs = refs[:count], refs[count : 2 * count]
    patch_ref, slot_ref = refs[2 * count :]
    depth = patch_ref.shape[1]
    cols = p_refs[0].shape[1]
    extra = Extra(cols, depth)
    folded = []
    total = jnp.zeros((extra.full, depth), F32)
    for index, (p_ref, e_ref) in enumerate(zip(p_refs, e_refs)):
        rows = e_ref[0, extra.full :].astype(F32)
        folded += [extra.folded(rows, h) for h in range(extra.heads)]
        total = total + dot(p_ref[...], v_ref[order_ref[index]])
    total = total + dot(terms_ref[...], jnp.concatenate(folded, 0), TN, precision=highest)
    width = patch_ref.shape[0]
    patch_ref[...] = total[:width]
    slot_ref[...] = total[width:]


def table_call(order, terms, values, products, pieces):
    _, depth, cols = pieces[0].shape
    width = VARS * PIX
    return pallas(
        lambda *refs: table_kernel(len(pieces), *refs),
        prefetch=1,
        grid=(1,),
        in_specs=[fixed(terms.shape), fixed((values.shape[0], cols, depth))]
        + [fixed(part.shape) for part in products]
        + [slot_of(piece, 4) for piece in pieces],
        out_specs=[fixed((width, depth)), fixed((VARS, depth))],
        out_shape=[struct((width, depth), F32), struct((VARS, depth), F32)],
        us=9,
        mib=56,
        name="table_back",
    )(order, terms, values, *products, *pieces)


def on_device(
    wide_size,
    narrow_size,
    variables,
    valid_slots,
    out_grad,
    patch_embed,
    variable_embed,
    pool_query,
    pool_key,
    pool_value,
    value_shift,
    pool_output,
    pool_bias,
    first_gain,
    first_shift,
    self_weights,
    query_bias,
    value_bias,
    self_output,
    output_bias,
    second_gain,
    second_shift,
    feed_up,
    up_bias,
    feed_down,
    down_bias,
):
    samples, token_count, input_width = variables.shape
    model_width = patch_embed.shape[1]
    local_dim = pool_query.shape[0]
    heads = local_dim // HEAD_DIM
    hidden = up_bias.shape[0]
    shares = narrow_size // samples
    permuted = wide_size == 4 and shares == 1
    ring = Ring(wide_size, narrow_size, not permuted)
    tokens = token_count // shares
    groups = narrow_size // 2
    row = lambda vector: vector.reshape(1, -1)
    pair_of = lambda pieces, g: pieces[2 * g : 2 * g + 2]
    place = (ring.n // shares, (ring.n % shares) * tokens, 0)
    pixels = lax.dynamic_slice(variables, place, (1, tokens, input_width))[0]
    grads = lax.dynamic_slice(out_grad, place, (1, tokens, model_width))[0]
    valid = lax.dynamic_index_in_dim(valid_slots, ring.n // shares, 0, keepdims=False)
    valid = valid.reshape(VARS, 1)

    filler = jnp.zeros((model_width - input_width - VARS, model_width), BF16)
    table_full = jnp.concatenate([patch_embed, variable_embed, filler], 0)
    gather = GatherShared(
        ring,
        prepare_call(
            pool_key,
            row(pool_query),
            table_full,
            pool_value,
            pool_output,
            self_weights.transpose(1, 0, 2),
            row(jnp.concatenate([value_shift, query_bias, value_bias])),
        ),
    )
    pixels_one, pixels_t = arrange_call(pixels)
    all_grads = ring.gather_wide(grads)
    quarter = hidden // wide_size
    cut_out = lambda tensor, axis: lax.dynamic_slice_in_dim(tensor, ring.w * quarter, quarter, axis)
    feed_own = stage_call(
        cut_out(feed_up, 1), cut_out(feed_down, 0), pool_value, row(cut_out(up_bias, 0))
    )
    pool = lambda pieces: pool_call(pixels_one, pixels_t, valid, pieces)
    wait_for(feed_own)
    pooled = pool([gather.own])
    for g in range(1, groups):
        got = list(gather.step())
        wait_for(pooled[-1][1])
        if g == 2:
            wait_for(*all_grads)
        pooled += pool(got)
    gather.step()
    wait_for(pooled[-1][1])
    hand_on(feed_own, self_output)
    far = pool([gather.far])
    feed_all = lax.all_gather(Gate.handed[0], "narrow")
    gather_mixer = GatherShared(ring, Gate.handed[1])
    pooled = [pooled[0], far[0]] + pooled[1:]
    pieces = gather.finish()
    stream_zero, normed_one, normed_one_t = enter_call(
        [head[1] for head in pooled], pieces, row(pool_bias), row(first_gain), row(first_shift)
    )

    subsets = [[s * shares + i for i in range(shares)] for s in range(samples)]
    chunks = [[g] for g in range(groups)]
    gather_mixer.step(stream_zero)
    queries, sources, flips, starts = [], [], [], []
    for chunk in chunks:
        if queries:
            wait_for(queries[-1])
        mine, pair = project_call(normed_one, pieces[2 * chunk[0] : 2 * chunk[-1] + 2])
        queries += mine
        if permuted:
            across = ring.swap(pair, 2)
            got = [pair, ring.swap(pair, 1), across, ring.swap(across, 1)]
        else:
            full = lax.all_gather(pair, "wide", axis=2, tiled=True)
            if shares > 1:
                full = lax.all_gather(
                    full, "narrow", axis=2, tiled=True, axis_index_groups=subsets
                )
            got = [full]
        for g in chunk:
            sources.append(got)
            flips.append([False, g > 0, False, g > 0] if permuted else [False])
            starts.append(2 * (g - chunk[0]))
    gather_mixer.step(queries[-1])
    attended, totals = [], []
    for g in range(groups):
        if attended:
            wait_for(attended[-1])
        got = attend_call(queries[g], sources[g], flips[g], starts[g])
        attended.append(got[0])
        totals.append(got[1])
        if g < 2:
            gather_mixer.step(got[0])
    self_pieces = gather_mixer.finish()
    order = jnp.stack(ring.places()).astype(jnp.int32)
    stream_one, normed_two, _ = middle_call(
        stream_zero, attended, self_pieces, row(output_bias), row(second_gain), row(second_shift)
    )

    all_rows = ring.gather_wide(normed_two)
    y_all, gx_all, gb_all, grad_feed = [], [], [], None
    near = max(1, wide_size // 2)
    plan = [(False, i) for i in range(near)] + [(True, 0)]
    plan += [(False, i) for i in range(near, wide_size)]
    plan += [(True, i) for i in range(1, wide_size)]
    latest = None
    for way_back, index in plan:
        if latest is not None:
            wait_for(latest)
        if not way_back:
            y_all.append(feed_call(local_dim, all_rows[index], feed_all))
            latest = y_all[-1]
            if index == wide_size - 1:
                y_parts = ring.scatter_wide(y_all)
                block_own = y_parts[0].astype(F32) + y_parts[1].astype(F32)
                block_own = low(stream_one + down_bias + block_own)
            continue
        if index == wide_size - 1:
            wait_for(block_own)
        got = feed_back_call(
            local_dim, all_rows[index], all_grads[index], feed_all, grad_feed
        )
        gx_all.append(got[0])
        gb_all.append(got[1])
        grad_feed = got[2]
        latest = got[0]
    gather_out = GatherOwn(ring, block_own, BF16)
    scatter_feed = ScatterOwn(ring, grad_feed)
    grad_parts = ring.scatter_wide(gx_all)
    grad_up_bias = sum(gb_all).reshape(narrow_size, quarter)
    grad_stream_one, grad_one, grad_one_t, sums_two = turn_call(
        grad_parts, grads, stream_one, row(second_gain)
    )

    waiting = {}
    backward = [0] + list(range(groups - 1, 0, -1))
    for turn, g in enumerate(backward):
        grad_attended, deltas, *grad_pair_mixers = middle_back_call(
            grad_one, grad_one_t, attended[g], pair_of(self_pieces, g)
        )
        back = lambda chosen, before, last, together: attend_back_call(
            queries[g],
            grad_attended,
            totals[g],
            deltas,
            [sources[g][i] for i in chosen],
            [flips[g][i] for i in chosen],
            starts[g],
            before,
            last,
            together,
        )
        if permuted:
            some, crossing = back([1, 3], None, False, True)
            crossed = ring.swap(crossing)
            grad_query, grad_own, grad_across = back([0, 2], some, True, False)
            far = add_up(grad_across, (crossed, 1))
            grad_pair = [grad_own, (crossed, 0), ring.swap(far, 2)]
        else:
            grad_query, full = back([0], None, True, False)
            if shares > 1:
                full = lax.psum_scatter(
                    full, "narrow", scatter_dimension=2, tiled=True, axis_index_groups=subsets
                )
            far = lax.psum_scatter(full, "wide", scatter_dimension=2, tiled=True)
            grad_pair = [far]
        waiting[g] = (grad_query, grad_pair, grad_pair_mixers)
        wait_for(far)
        if turn in (0, 2):
            wait_for(gather_out.beside(scatter_feed.step))
    grad_normed_one, grad_pieces, sums_triple = None, {}, [None] * groups
    for turn, g in enumerate(backward):
        grad_query, grad_pair, grad_pair_mixers = waiting[g]
        if grad_normed_one is not None:
            wait_for(grad_normed_one)
        grad_pair = add_up(*grad_pair)
        back = lambda: project_back_call(
            normed_one_t,
            pair_of(pieces, g),
            grad_query,
            grad_pair,
            grad_pair_mixers,
            grad_normed_one,
        )
        if turn == 3:
            wait_for(gather_out.beside(scatter_feed.step))
        made, grad_normed_one, sums = back()
        grad_pieces[g], sums_triple[g] = made, sums
    scatter = ScatterShared(ring, *grad_pieces[0])
    grad_zero, grad_zero_t, sums_one = leave_call(
        grad_normed_one, stream_zero, grad_stream_one, row(first_gain)
    )

    grad_pixels, grad_terms, grad_shifts = None, [None] * groups, [None] * groups
    for turn, g in enumerate(backward):
        if turn > 1:
            wait_for(grad_pixels)
            added = scatter.step(grad_pieces[backward[turn - 1]])
            wait_for(added)
            wait_for(scatter_last.step(made))
        back = lambda: pool_back_call(
            pixels_one,
            pixels_t,
            pair_of(pooled, g),
            pair_of(pieces, g),
            grad_zero,
            grad_zero_t,
            grad_pixels,
            turn == groups - 1,
        )
        if turn == 1:
            wait_for(grad_pixels)
            wait_for(gather_out.beside(scatter_feed.step))
        made, grad_pixels, terms, shifts = back()
        if turn == 0:
            scatter_last = ScatterShared(ring, *made)
        grad_terms[g], grad_shifts[g] = terms, shifts

    def sort_into(places, tensor, back=False):
        same = jnp.stack([jnp.stack([p == i for p in places]) for i in range(narrow_size)])
        same = same.T if back else same
        return jnp.sum(jnp.where(same[:, :, None], tensor[None], 0.0), 1)

    places = ring.places()
    sums_triple = jnp.concatenate(sums_triple, 0).reshape(narrow_size, -1)
    up_bias_row = lax.dynamic_update_slice(
        jnp.zeros((narrow_size, hidden), F32),
        grad_up_bias,
        (0, ring.w * quarter),
    )
    own_sums = jnp.concatenate(
        [
            jnp.concatenate(grad_shifts, 0).reshape(narrow_size, -1),
            sums_triple[:, :local_dim],
            sums_triple[:, 2 * local_dim :],
            jnp.concatenate(grad_terms, 0).reshape(narrow_size, -1),
        ],
        1,
    )
    own_sums = jnp.concatenate([up_bias_row, sort_into(places, own_sums)], 1)
    own_length = own_sums.shape[1]
    shared_sums = jnp.concatenate([sums_one, sums_two], 0)
    all_sums = jnp.concatenate([own_sums.reshape(-1), shared_sums.reshape(-1)]).reshape(-1, 128)
    adder = AddEverywhere(ring, all_sums)
    adder.step()
    adder.step()
    scatter_last.step(made)
    hand_on(grad_pixels, scatter.current)
    scatter_last.step()
    grad_pixels, scatter.current = Gate.handed
    gather_pixels = GatherOwn(ring, grad_pixels, F32)
    finish_last = FinishShared(ring, scatter_last.current)
    finish_last.step()
    finish_last.step()
    grad_pool_output, product = finish_last.finish()
    product = low(product[0, : input_width + VARS])
    products = gather_direct(ring, product)
    scatter.step(grad_pieces[backward[-1]])
    passes = narrow_size // 2 - 1
    for hop in range(passes):
        gather_pixels.after()
        if hop:
            adder.take(gather_pixels.handed[0])
        if adder.pairs:
            adder.send()
        wait_for(gather_pixels.handed[0])
        if hop == 0:
            scatter.step()
            finish = FinishShared(ring, scatter.current)
            (grad_feed_own,) = pass_on([scatter_feed.ahead], gather_pixels.handed[0])
            grad_feed_pieces = ring.gather_wide(grad_feed_own)
        elif finish.bits:
            finish.step()
        else:
            Gate.waits = []
        if hop == passes - 1:
            grad_pool_output, late_product, block_out = pass_on(
                [grad_pool_output, product, gather_out.finish()], gather_pixels.handed[0]
            )
    adder.take()
    while adder.pairs:
        adder.step()
    block_out = block_out.reshape(samples, token_count, model_width)
    grad_first, grad_second = finish.finish()
    grad_feed_up, grad_feed_down = assemble_call(ring.w, grad_feed_pieces)
    grad_variables = gather_pixels.finish().reshape(samples, token_count, input_width)
    grad_triple = jnp.concatenate([grad_first, grad_second[:1]], 0).transpose(1, 0, 2)
    grad_self_output = grad_second[1].T
    grad_pool_output = grad_pool_output[0].T
    grad_pool_value = dot(patch_embed, late_product[:input_width], TN)
    grad_pool_value = grad_pool_value + dot(variable_embed, late_product[input_width:], TN)

    summed = adder.current.reshape(-1)
    own_all = summed[: narrow_size * own_length].reshape(narrow_size, own_length)
    shared_all = summed[narrow_size * own_length :].reshape(-1, model_width)
    grad_first_gain, grad_first_shift, grad_pool_bias = shared_all[:3]
    grad_second_gain, grad_second_shift, grad_down_bias, grad_output_bias = shared_all[3:]
    own = lax.dynamic_index_in_dim(own_all, ring.n, 0, keepdims=False)
    grad_up_bias = own[:hidden]
    grad_value_shift, grad_query_bias, grad_value_bias = own[hidden : hidden + 3 * local_dim].reshape(
        3, local_dim
    )
    terms_start = 3 * local_dim + hidden
    grad_proj = SCALE * own[terms_start:].reshape(heads, -1)
    grad_folded = dot(grad_proj[:, :input_width], patch_embed.astype(F32), precision=highest)
    grad_folded = grad_folded + dot(
        grad_proj[:, input_width:], variable_embed.astype(F32), precision=highest
    )
    query_heads = pool_query.reshape(heads, HEAD_DIM)
    key_heads = pool_key.astype(F32).reshape(model_width, heads, HEAD_DIM)
    grad_pool_key = (grad_folded.T[:, :, None] * query_heads).reshape(model_width, local_dim)
    grad_pool_query = jnp.einsum("dhe,hd->he", key_heads, grad_folded, precision=highest).reshape(
        local_dim
    )
    grad_terms = SCALE * sort_into(places, own_all[:, terms_start:], True)
    wait_for(finish.other, grad_pool_value, grad_feed_up)
    grad_patch, grad_slot = table_call(
        order,
        grad_terms.reshape(narrow_size * heads, -1),
        feed_all,
        products,
        pieces,
    )
    return (
        block_out,
        grad_variables,
        grad_patch,
        grad_slot,
        grad_pool_query,
        grad_pool_key,
        grad_pool_value,
        grad_value_shift,
        grad_pool_output,
        grad_pool_bias,
        grad_first_gain,
        grad_first_shift,
        grad_triple,
        grad_query_bias,
        grad_value_bias,
        grad_self_output,
        grad_output_bias,
        grad_second_gain,
        grad_second_shift,
        grad_feed_up,
        grad_up_bias,
        grad_feed_down,
        grad_down_bias,
    )


def solution(mesh):
    wide_size, narrow_size = mesh.shape["wide"], mesh.shape["narrow"]

    def body(*arrays):
        return on_device(wide_size, narrow_size, *arrays)

    return jax.shard_map(
        body,
        mesh=mesh,
        in_specs=(
            P(None, "wide", None),
            P(),
            P(None, "wide", None),
            P(),
            P(),
            P("narrow"),
            P(None, "narrow"),
            P(None, "narrow"),
            P("narrow"),
            P("narrow", None),
            P(),
            P(),
            P(),
            P(None, None, "narrow"),
            P("narrow"),
            P("narrow"),
            P("narrow", None),
            P(),
            P(),
            P(),
            P(None, "narrow"),
            P("narrow"),
            P("narrow", None),
            P(),
        ),
        out_specs=(
            P(None, "wide", None),
            P(None, "wide", None),
            P(),
            P(),
            P("narrow"),
            P(None, "narrow"),
            P(None, "narrow"),
            P("narrow"),
            P("narrow", None),
            P(),
            P(),
            P(),
            P(None, None, "narrow"),
            P("narrow"),
            P("narrow"),
            P("narrow", None),
            P(),
            P(),
            P(),
            P(None, "narrow"),
            P("narrow"),
            P("narrow", None),
            P(),
        ),
        check_vma=False,
    )
```
